128 devices in a mesh: rows: 16 (over x_hi, z, core), chan: 8 (over y, x_lo).
Axes of the slice: x: 4 (x_hi: 2, x_lo: 2; x = x_hi * 2 + x_lo), y: 4, z: 4, core: 2. Of those that a mesh axis runs over, the one named last changes fastest.
Arguments:
- coarse_input: bfloat16 [2, 256, 256, 256], P(None, 'rows', None, 'chan'), may hold values from -6 to 6
- coarse_pre: bfloat16 [2, 256, 256, 256], P(None, 'rows', None, 'chan'), may hold values from -8 to 8
- skip_feats: bfloat16 [2, 512, 512, 128], P(None, ('rows', 'chan')), may hold values from -6 to 6
- fine_pre: bfloat16 [2, 512, 512, 128], P(None, ('rows', 'chan')), may hold values from -8 to 8
- fine_cotangent: bfloat16 [2, 512, 512, 128], P(None, ('rows', 'chan')), may hold values from -6 to 6
- fine_weight: bfloat16 [3, 3, 384, 128], replicated, may hold values from -0.109375 to 0.109375
- coarse_weight: bfloat16 [3, 3, 256, 256], replicated, may hold values from -0.125 to 0.125
Outputs:
- grad_skip: bfloat16 [2, 512, 512, 128], P(None, ('rows', 'chan'))
- grad_input: bfloat16 [2, 256, 256, 256], P(None, 'rows', None, 'chan')
- grad_fine_weight: float32 [3, 3, 384, 128], replicated
- grad_coarse_weight: float32 [3, 3, 256, 256], replicated
The draws below stay inside these ranges and needn't reach their ends.
All inputs are finite; a program needn't handle non-finite values.
Results may differ from the reference program's by a relative error of at most 0.0058.
Values may be sent and summed in bfloat16 or wider, within the bound.
No kernel may reach another device: no remote copies, remote signals or barrier semaphores. Data moves between devices by JAX's collectives and lax.ppermute only.
A program may use at most 192 MiB of HBM per device.

```python
import math
import jax
import jax.numpy as jnp

C4 = 256
CS = 128
C3 = 128
W4 = 256
B = 2
H4 = 256
H3 = 512
W3 = 512


def level_of(stream_key, extent, pieces, low, largest):
    gain, own = 1.0, jax.random.fold_in(stream_key, 6)
    for axis_at, parts in pieces:
        draws = jnp.exp(jax.random.uniform(jax.random.fold_in(own, axis_at), (parts,), jnp.float32, low / len(pieces), largest / len(pieces)))
        gain = gain * jnp.repeat(draws, extent[axis_at] // parts).reshape([-1 if axis == axis_at else 1 for axis in range(len(extent))])
    return gain


def normal_values(own_key, extent, spread, most, shards=(), dtype=jnp.bfloat16):
    result = spread * jax.random.normal(own_key, extent, jnp.float32)
    if shards:
        result = result * level_of(own_key, extent, shards, -0.22, 0.18)
    return jnp.clip(result, -most, most).astype(dtype)


def setup_inputs(seed: int = 0) -> dict:
    arg_keys = jax.random.split(jax.random.key(seed), 8)
    coarse_input = normal_values(arg_keys[0], (B, H4, W4, C4), 1.0, 6.0, ((1, 16), (3, 8)))
    coarse_pre = normal_values(arg_keys[1], (B, H4, W4, C4), 1.5, 8.0, ((1, 16), (3, 8)))
    skip_feats = normal_values(arg_keys[2], (B, H3, W3, CS), 1.0, 6.0, ((1, 128),))
    fine_pre = normal_values(arg_keys[3], (B, H3, W3, C3), 1.5, 8.0, ((1, 128),))
    fine_cotangent = normal_values(arg_keys[4], (B, H3, W3, C3), 1.0, 6.0, ((1, 128),))
    fine_weight = normal_values(arg_keys[5], (3, 3, C4 + CS, C3), (9 * (C4 + CS)) ** -0.5, 0.109375)
    coarse_weight = normal_values(arg_keys[6], (3, 3, C4, C4), (9 * C4) ** -0.5, 0.125)
    return {"coarse_input": coarse_input, "coarse_pre": coarse_pre, "skip_feats": skip_feats, "fine_pre": fine_pre, "fine_cotangent": fine_cotangent, "fine_weight": fine_weight, "coarse_weight": coarse_weight}


def silu_grad(value):
    sigma = jax.nn.sigmoid(value)
    return sigma * (1.0 + value * (1.0 - sigma))

def upsample(field):
    return jnp.repeat(jnp.repeat(field, 2, axis=-3), 2, axis=-2)

def pooling(field):
    shape = field.shape
    return field.reshape(shape[:-3] + (shape[-3] // 2, 2, shape[-2] // 2, 2, shape[-1])).sum(axis=(-4, -2))

def tap_grads(inputs, padded):
    height, breadth = (inputs.shape[-3], inputs.shape[-2])
    wide_inputs = inputs.astype(jnp.float32)
    kernel_rows = []
    for vertical in range(3):
        row_taps = []
        for lateral in range(3):
            window = padded[..., 2 - vertical:2 - vertical + height, 2 - lateral:2 - lateral + breadth, :]
            row_taps.append(jnp.einsum('...hwi,...hwo->io', wide_inputs, window.astype(jnp.float32)))
        kernel_rows.append(jnp.stack(row_taps))
    return jnp.stack(kernel_rows)

def tap_back(padded, kernel):
    height, breadth = (padded.shape[-3] - 2, padded.shape[-2] - 2)
    total = None
    for vertical in range(3):
        for lateral in range(3):
            window = padded[..., 2 - vertical:2 - vertical + height, 2 - lateral:2 - lateral + breadth, :]
            term = jnp.einsum('...hwo,io->...hwi', window.astype(jnp.float32), kernel[vertical, lateral].astype(jnp.float32))
            total = term if total is None else total + term
    return total

def reference(coarse_input, coarse_pre, skip_feats, fine_pre, fine_cotangent, fine_weight, coarse_weight):
    channels = coarse_weight.shape[2]
    samples = fine_pre.shape[0]
    grad_fine = jnp.zeros(fine_weight.shape, jnp.float32)
    grad_coarse = jnp.zeros(coarse_weight.shape, jnp.float32)
    skip_list = []
    input_list = []
    for sample in range(samples):
        pre_value = coarse_pre[sample].astype(jnp.float32)
        upsampled = upsample(jax.nn.silu(pre_value)).astype(jnp.bfloat16)
        stacked = jnp.concatenate([upsampled, skip_feats[sample]], axis=-1)
        fine_grad = (fine_cotangent[sample].astype(jnp.float32) * silu_grad(fine_pre[sample].astype(jnp.float32))).astype(jnp.bfloat16)
        fine_pad = jnp.pad(fine_grad, ((1, 1), (1, 1), (0, 0)))
        grad_fine = grad_fine + tap_grads(stacked, fine_pad)
        back = tap_back(fine_pad, fine_weight)
        skip_list.append(back[..., channels:].astype(jnp.bfloat16))
        coarse_grad = (pooling(back[..., :channels]) * silu_grad(pre_value)).astype(jnp.bfloat16)
        coarse_pad = jnp.pad(coarse_grad, ((1, 1), (1, 1), (0, 0)))
        grad_coarse = grad_coarse + tap_grads(coarse_input[sample], coarse_pad)
        input_list.append(tap_back(coarse_pad, coarse_weight).astype(jnp.bfloat16))
    fine_cells = samples * fine_pre.shape[1] * fine_pre.shape[2]
    coarse_cells = samples * coarse_pre.shape[1] * coarse_pre.shape[2]
    return (jnp.stack(skip_list), jnp.stack(input_list), grad_fine * (1.0 / math.sqrt(fine_cells)), grad_coarse * (1.0 / math.sqrt(coarse_cells)))
```

```python
import functools
import math

import jax
import jax.numpy as jnp
from jax import lax
from jax.experimental import pallas as pl
from jax.experimental.pallas import tpu as pltpu
from jax.sharding import Mesh
from jax.sharding import PartitionSpec as P

F32 = jnp.float32
BF16 = jnp.bfloat16
MIB = 1 << 20
VMEM = 28

SPLIT = (("xh", 2), ("z", 4), ("core", 2), ("y", 4), ("xl", 2))
ROWS = ("xh", "z", "core")
CHAN = ("y", "xl")
ALL = ROWS + CHAN
CHIPS = ("xh", "xl", "z", "y")


def params(limit):
    return pltpu.CompilerParams(vmem_limit_bytes=limit * MIB)


def cost(flops, nbytes):
    return pl.CostEstimate(flops=int(flops), bytes_accessed=int(nbytes), transcendentals=0)


def silu_grad(value):
    sigma = jax.nn.sigmoid(value)
    return sigma * (1.0 + value * (1.0 - sigma))


def shifted(field):
    extent = field.shape[0]
    index = lax.broadcasted_iota(jnp.int32, field.shape, 0)
    before = jnp.where(index == 0, 0.0, pltpu.roll(field, 1, 0))
    after = jnp.where(index == extent - 1, 0.0, pltpu.roll(field, extent - 1, 0))
    return before, after


def tdot(left, right):
    return lax.dot_general(left, right, (((0,), (0,)), ((), ())), preferred_element_type=F32)


def dott(left, right):
    return lax.dot_general(left, right, (((1,), (1,)), ((), ())), preferred_element_type=F32)


def tiles(block):
    return block.astype(BF16).reshape(block.shape[0] // 16, 16, block.shape[1])


def box_kernel(
    cot_ref, pre_ref, low_ref, high_ref, weight_ref, grad_ref, pooled_ref, box_ref, rows32, up_weight
):
    sample = pl.program_id(0)
    c3 = cot_ref.shape[-1]
    c4 = pooled_ref.shape[-1]
    half = pooled_ref.shape[-2]

    @pl.when(sample == 0)
    def _():
        for dy in range(3):
            for d in range(3):
                at = (dy * 3 + d) * c3
                up_weight[at : at + c3, :] = weight_ref[2 - dy, 2 - d, :c4, :].astype(F32).T.astype(BF16)

    for v in range(6):
        if v == 0:
            grad = low_ref[0]
        elif v == 5:
            grad = high_ref[0]
        else:
            grad = cot_ref[0, v - 1].astype(F32) * silu_grad(pre_ref[0, v - 1].astype(F32))
            grad = grad.astype(BF16)
        grad_ref[0, v] = grad
        rows32[v] = grad.astype(F32)

    for v in range(5):
        even = rows32[v, pl.ds(0, half, 2), :] + rows32[v + 1, pl.ds(0, half, 2), :]
        odd = rows32[v, pl.ds(1, half, 2), :] + rows32[v + 1, pl.ds(1, half, 2), :]
        before, _ = shifted(odd)
        _, after = shifted(even)
        sums = ((before + even).astype(BF16), (even + odd).astype(BF16), (odd + after).astype(BF16))
        for i in range(2):
            dy = v - 2 * i
            if 0 <= dy <= 2:
                for d in range(3):
                    at = (dy * 3 + d) * c3
                    box_ref[0, i * half : (i + 1) * half, at : at + c3] = sums[d]

    pooled = jnp.dot(box_ref[0], up_weight[...], preferred_element_type=F32)
    pooled_ref[0] = pooled.reshape(pooled_ref.shape[1:])


def box_level(cot, pre, low, high, weight, cs):
    samples, height, wide, c3 = cot.shape
    c4 = weight.shape[2] - cs
    half = wide // 2
    block = pl.BlockSpec((1, height, wide, c3), lambda s: (s, 0, 0, 0))
    edge = pl.BlockSpec((1, wide, c3), lambda s: (s, 0, 0))
    return pl.pallas_call(
        box_kernel,
        grid=(samples,),
        in_specs=[block, block, edge, edge, pl.BlockSpec(weight.shape, lambda s: (0, 0, 0, 0))],
        out_specs=[
            pl.BlockSpec((1, height + 2, wide, c3), lambda s: (s, 0, 0, 0)),
            pl.BlockSpec((1, 2, half, c4), lambda s: (s, 0, 0, 0)),
            pl.BlockSpec((1, 2 * half, 9 * c3), lambda s: (s, 0, 0)),
        ],
        out_shape=[
            jax.ShapeDtypeStruct((samples, height + 2, wide, c3), BF16),
            jax.ShapeDtypeStruct((samples, 2, half, c4), F32),
            jax.ShapeDtypeStruct((samples, 2 * half, 9 * c3), BF16),
        ],
        scratch_shapes=[pltpu.VMEM((6, wide, c3), F32), pltpu.VMEM((9 * c3, c4), BF16)],
        compiler_params=params(VMEM),
        cost_estimate=cost(1.5e9, 8e6),
        name="box_level",
    )(cot, pre, low, high, weight)


def fine_kernel(
    core_ref, grad_ref, skip_ref, weight_ref, pre_ref, box_ref,
    grad_skip_ref, keep_ref, send_ref,
    taps, skip_weight, total, up_total, *, scale,
):
    sample = pl.program_id(0)
    c3 = grad_ref.shape[-1]
    cs = skip_ref.shape[-1]
    c4 = weight_ref.shape[2] - cs
    half = pre_ref.shape[-1]

    @pl.when(sample == 0)
    def _():
        total[...] = jnp.zeros_like(total)
        up_total[...] = jnp.zeros_like(up_total)
        for u in range(4):
            for d in range(3):
                at = (u * 3 + d) * c3
                for t in range(2):
                    dy = u - t
                    if 0 <= dy <= 2:
                        block = weight_ref[2 - dy, 2 - d, c4:, :].astype(F32).T.astype(BF16)
                    else:
                        block = jnp.zeros((c3, cs), BF16)
                    skip_weight[at : at + c3, t * cs : (t + 1) * cs] = block

    for i in range(2):
        value = pre_ref[:, 0, 0, i].reshape(c4, half).astype(F32)
        value = (value * jax.nn.sigmoid(value)).astype(BF16)
        up_total[...] += jnp.dot(value, box_ref[0, i * half : (i + 1) * half, :], preferred_element_type=F32)

    for v in range(6):
        grad = grad_ref[0, v]
        before, after = shifted(grad.astype(F32))
        at = v * 3 * c3
        taps[:, at : at + c3] = before.astype(BF16)
        taps[:, at + c3 : at + 2 * c3] = grad
        taps[:, at + 2 * c3 : at + 3 * c3] = after.astype(BF16)

    for pair in range(2):
        window = taps[:, 2 * pair * 3 * c3 : (2 * pair + 4) * 3 * c3]
        back = jnp.dot(window, skip_weight[...], preferred_element_type=F32)
        grad_skip_ref[0, 2 * pair] = back[:, :cs].astype(BF16)
        grad_skip_ref[0, 2 * pair + 1] = back[:, cs:].astype(BF16)
        feats = jnp.concatenate([skip_ref[0, 2 * pair], skip_ref[0, 2 * pair + 1]], axis=1)
        total[...] += tdot(feats, window)

    @pl.when(sample == pl.num_programs(0) - 1)
    def _():
        core = core_ref[0]

        def put(tap, at, value):
            part = value.shape[0] // 2
            low, high = value[:part], value[part:]
            keep_ref[tap, at : at + part // 16] = tiles(jnp.where(core == 0, low, high))
            send_ref[tap, at : at + part // 16] = tiles(jnp.where(core == 0, high, low))

        for dy in range(3):
            for d in range(3):
                first = (dy * 3 + d) * c3
                second = ((dy + 1) * 3 + d) * c3
                tap = (2 - dy) * 3 + 2 - d
                put(tap, 0, up_total[:, first : first + c3] * scale)
                value = total[:cs, first : first + c3] + total[cs:, second : second + c3]
                put(tap, c4 // 32, value * scale)


def fine_level(core, grad, skip, weight, received, box, fine_cells):
    samples, height, wide, cs = skip.shape
    c3 = grad.shape[-1]
    c4 = weight.shape[2] - cs
    half = wide // 2
    peers, own = received.shape[0], received.shape[-2]
    part = jax.ShapeDtypeStruct((9, (c4 + cs) // 32, 16, c3), BF16)
    whole = pl.BlockSpec(part.shape, lambda s: (0, 0, 0, 0))
    return pl.pallas_call(
        functools.partial(fine_kernel, scale=1.0 / math.sqrt(fine_cells)),
        grid=(samples,),
        in_specs=[
            pl.BlockSpec(memory_space=pltpu.SMEM),
            pl.BlockSpec((1, height + 2, wide, c3), lambda s: (s, 0, 0, 0)),
            pl.BlockSpec((1, height, wide, cs), lambda s: (s, 0, 0, 0)),
            pl.BlockSpec(weight.shape, lambda s: (0, 0, 0, 0)),
            pl.BlockSpec((peers, 1, 1, 2, own, half), lambda s: (0, 0, s, 0, 0, 0)),
            pl.BlockSpec((1, 2 * half, 9 * c3), lambda s: (s, 0, 0)),
        ],
        out_specs=[pl.BlockSpec((1, height, wide, cs), lambda s: (s, 0, 0, 0)), whole, whole],
        out_shape=[jax.ShapeDtypeStruct((samples, height, wide, cs), BF16), part, part],
        scratch_shapes=[
            pltpu.VMEM((wide, 18 * c3), BF16),
            pltpu.VMEM((12 * c3, 2 * cs), BF16),
            pltpu.VMEM((2 * cs, 12 * c3), F32),
            pltpu.VMEM((c4, 9 * c3), F32),
        ],
        compiler_params=params(VMEM),
        cost_estimate=cost(6e9, 12e6),
        name="fine_level",
    )(core, grad, skip, weight, received, box)


def coarse_grad_kernel(pooled_ref, pre_ref, first_ref, second_ref):
    channels, wide = pooled_ref.shape[-1], pooled_ref.shape[-2]
    for i, out_ref in enumerate((first_ref, second_ref)):
        value = pre_ref[:, 0, 0, i].reshape(channels, wide).astype(F32).T
        out_ref[0] = (pooled_ref[0, i] * silu_grad(value)).astype(BF16)


def coarse_grad(pooled, received):
    samples, _, wide, c4 = pooled.shape
    peers, _, _, _, own, _ = received.shape
    out = jax.ShapeDtypeStruct((samples, wide, c4), BF16)
    spec = pl.BlockSpec((1, wide, c4), lambda s: (s, 0, 0))
    return pl.pallas_call(
        coarse_grad_kernel,
        grid=(samples,),
        in_specs=[
            pl.BlockSpec((1, 2, wide, c4), lambda s: (s, 0, 0, 0)),
            pl.BlockSpec((peers, 1, 1, 2, own, wide), lambda s: (0, 0, s, 0, 0, 0)),
        ],
        out_specs=[spec, spec],
        out_shape=[out, out],
        compiler_params=params(VMEM),
        cost_estimate=cost(2e7, 2e6),
        name="coarse_grad",
    )(pooled, received)


def fill_coarse_taps(rows, taps):
    wide, c4 = rows[0].shape
    for v, row in enumerate(rows):
        value = row.astype(F32)
        before, after = shifted(value)
        taps[v * wide : (v + 1) * wide, :c4] = before.astype(BF16)
        taps[v * wide : (v + 1) * wide, c4 : 2 * c4] = row
        taps[v * wide : (v + 1) * wide, 2 * c4 :] = after.astype(BF16)


def coarse_weight_kernel(
    core_ref, input_ref, low_ref, first_ref, second_ref, high_ref, keep_ref, send_ref, taps, total, *, scale
):
    sample = pl.program_id(0)
    wide = input_ref.shape[-1]
    c4 = input_ref.shape[0] * input_ref.shape[-2]

    @pl.when(sample == 0)
    def _():
        total[...] = jnp.zeros_like(total)

    fill_coarse_taps((low_ref[0], first_ref[0], second_ref[0], high_ref[0]), taps)
    values = jnp.concatenate([input_ref[:, 0, 0, i].reshape(c4, wide) for i in range(2)], axis=1)
    for dy in range(3):
        total[dy] += jnp.dot(values, taps[dy * wide : (dy + 2) * wide, :], preferred_element_type=F32)

    @pl.when(sample == pl.num_programs(0) - 1)
    def _():
        core = core_ref[0]
        part = c4 // 2
        count = part // 16
        for dy in range(3):
            for d in range(3):
                for side in range(c4 // 128):
                    at = d * c4 + side * 128
                    value = total[dy, :, at : at + 128] * scale
                    low, high = value[:part], value[part:]
                    tap = ((2 - dy) * 3 + 2 - d) * (c4 // 128) + side
                    keep_ref[tap * count : (tap + 1) * count] = tiles(jnp.where(core == 0, low, high))
                    send_ref[tap * count : (tap + 1) * count] = tiles(jnp.where(core == 0, high, low))


def coarse_specs(samples, wide, c4):
    return [pl.BlockSpec((1, wide, c4), lambda s: (s, 0, 0))] * 4


def coarse_weight_level(core, received, rows, coarse_cells):
    peers, _, samples, _, own, wide = received.shape
    c4 = peers * own
    part = jax.ShapeDtypeStruct((9 * (c4 // 128) * (c4 // 32), 16, 128), BF16)
    whole = pl.BlockSpec(part.shape, lambda s: (0, 0, 0))
    return pl.pallas_call(
        functools.partial(coarse_weight_kernel, scale=1.0 / math.sqrt(coarse_cells)),
        grid=(samples,),
        in_specs=[
            pl.BlockSpec(memory_space=pltpu.SMEM),
            pl.BlockSpec((peers, 1, 1, 2, own, wide), lambda s: (0, 1, s, 0, 0, 0)),
        ] + coarse_specs(samples, wide, c4),
        out_specs=[whole, whole],
        out_shape=[part, part],
        scratch_shapes=[pltpu.VMEM((4 * wide, 3 * c4), BF16), pltpu.VMEM((3, c4, 3 * c4), F32)],
        compiler_params=params(VMEM),
        cost_estimate=cost(1.3e9, 3e6),
        name="coarse_weight_level",
    )(core, received, *rows)


def coarse_input_kernel(weight_ref, low_ref, first_ref, second_ref, high_ref, out_ref, taps):
    wide, c4 = low_ref.shape[1:]
    peers, own = out_ref.shape[0], out_ref.shape[-2]
    fill_coarse_taps((low_ref[0], first_ref[0], second_ref[0], high_ref[0]), taps)
    total = None
    for dy in range(3):
        for d in range(3):
            window = taps[dy * wide : (dy + 2) * wide, d * c4 : (d + 1) * c4]
            term = dott(weight_ref[2 - dy, 2 - d], window)
            total = term if total is None else total + term
    total = total.astype(BF16)
    for i in range(2):
        out_ref[:, 0, i] = total[:, i * wide : (i + 1) * wide].reshape(peers, own, wide)


def coarse_input_level(weight, rows, peers):
    samples, wide, c4 = rows[0].shape
    own = c4 // peers
    return pl.pallas_call(
        coarse_input_kernel,
        grid=(samples,),
        in_specs=[pl.BlockSpec(weight.shape, lambda s: (0, 0, 0, 0))] + coarse_specs(samples, wide, c4),
        out_specs=pl.BlockSpec((peers, 1, 2, own, wide), lambda s: (0, s, 0, 0, 0)),
        out_shape=jax.ShapeDtypeStruct((peers, samples, 2, own, wide), BF16),
        scratch_shapes=[pltpu.VMEM((4 * wide, 3 * c4), BF16)],
        compiler_params=params(VMEM),
        cost_estimate=cost(1.3e9, 3e6),
        name="coarse_input_level",
    )(weight, *rows)


def join_kernel(coarse_ref, coarse_more_ref, fine_ref, fine_more_ref, out_ref):
    count = coarse_ref.shape[0]
    out_ref[:count] = (coarse_ref[...].astype(F32) + coarse_more_ref[...].astype(F32)).astype(BF16)
    fines = fine_ref.shape[0]
    out_ref[count : count + fines] = (fine_ref[...].astype(F32) + fine_more_ref[...].astype(F32)).astype(BF16)
    rest = out_ref.shape[0] - count - fines
    if rest:
        out_ref[count + fines :] = jnp.zeros((rest,) + out_ref.shape[1:], BF16)


def sum_kernel(parts_ref, out_ref):
    total = parts_ref[0].astype(F32)
    for k in range(1, parts_ref.shape[0]):
        total = total + parts_ref[k].astype(F32)
    total = total.astype(BF16)
    for k in range(out_ref.shape[0]):
        out_ref[k] = total


def unpack_kernel(core_ref, mine_ref, other_ref, fine_ref, coarse_ref):
    c4 = coarse_ref.shape[-1]
    cs = fine_ref.shape[-2] - c4
    sides = c4 // 128
    lines = c4 // 32
    skips = cs // 32
    mine = core_ref[0]
    for core in range(2):

        def take(at, count):
            block = jnp.where(mine == core, mine_ref[at : at + count].astype(F32), other_ref[at : at + count].astype(F32))
            return block.reshape(count * 16, 128)

        for tap in range(9):
            for side in range(sides):
                block = take((tap * sides + side) * lines, lines)
                coarse_ref[tap, core * lines * 16 : (core + 1) * lines * 16, side * 128 : (side + 1) * 128] = block
            at = 9 * sides * lines + tap * (lines + skips)
            fine_ref[tap, core * lines * 16 : (core + 1) * lines * 16, :] = take(at, lines)
            fine_ref[tap, c4 + core * skips * 16 : c4 + (core + 1) * skips * 16, :] = take(at + lines, skips)


SWAP = ((0, 1), (1, 0))


def grad_sums(fine_keep, fine_more, coarse_keep, coarse_more):
    chips = 1
    for axis in CHIPS:
        chips *= lax.axis_size(axis)
    fine_keep, fine_more = (a.reshape((-1, 16, 128)) for a in (fine_keep, fine_more))
    count = coarse_keep.shape[0] + fine_keep.shape[0]
    each = -(-count // chips)
    joined = pl.pallas_call(
        join_kernel,
        out_shape=jax.ShapeDtypeStruct((chips * each, 16, 128), BF16),
        compiler_params=params(VMEM),
        cost_estimate=cost(1e6, 3e6),
        name="join",
    )(coarse_keep, coarse_more, fine_keep, fine_more)
    parts = lax.all_to_all(joined.reshape(chips, each, 16, 128), CHIPS, 0, 0, tiled=True)
    summed = pl.pallas_call(
        sum_kernel,
        out_shape=jax.ShapeDtypeStruct((chips, each, 16, 128), BF16),
        compiler_params=params(VMEM),
        cost_estimate=cost(1e6, 1.3e6),
        name="sum_parts",
    )(parts)
    return lax.all_to_all(summed, CHIPS, 0, 0, tiled=True).reshape(chips * each, 16, 128)


def unpacked(core, mine, other, fine_shape, coarse_shape):
    fine_flat = (9,) + fine_shape[2:]
    coarse_flat = (9,) + coarse_shape[2:]
    vmem = pl.BlockSpec(memory_space=pltpu.VMEM)
    fine, coarse = pl.pallas_call(
        unpack_kernel,
        in_specs=[pl.BlockSpec(memory_space=pltpu.SMEM), vmem, vmem],
        out_shape=[jax.ShapeDtypeStruct(fine_flat, F32), jax.ShapeDtypeStruct(coarse_flat, F32)],
        compiler_params=params(VMEM),
        cost_estimate=cost(1e6, 6e6),
        name="unpack",
    )(core, mine, other)
    return fine.reshape(fine_shape), coarse.reshape(coarse_shape)


def edges(low, high):
    count = 1
    for axis in ALL:
        count *= lax.axis_size(axis)
    forward = [(i, i + 1) for i in range(count - 1)]
    backward = [(target, source) for source, target in forward]
    return lax.ppermute(high, ALL, forward), lax.ppermute(low, ALL, backward)


def shards(coarse_input, coarse_pre, skip_feats, fine_pre, fine_cotangent, fine_weight, coarse_weight):
    peers = 1
    for axis in CHAN:
        peers *= lax.axis_size(axis)
    devices = peers
    for axis in ROWS:
        devices *= lax.axis_size(axis)
    samples, lines, wide, own = coarse_input.shape
    core = lax.axis_index("core").astype(jnp.int32).reshape(1)

    def grad_row(line):
        return (
            fine_cotangent[:, line].astype(F32) * silu_grad(fine_pre[:, line].astype(F32))
        ).astype(BF16)

    top, bottom = grad_row(0), grad_row(-1)
    low, high = edges(top, bottom)
    both = jnp.stack([coarse_pre, coarse_input]).reshape(2, samples, peers, lines // peers, wide, own)
    both = both.transpose(2, 0, 1, 3, 5, 4)
    both, top, bottom = lax.optimization_barrier((both, top, bottom))
    received = lax.all_to_all(both, CHAN, 0, 0, tiled=True)

    cs = skip_feats.shape[-1]
    fine_cells = fine_pre.shape[0] * fine_pre.shape[1] * fine_pre.shape[2] * devices
    fine_grad, pooled, box = box_level(fine_cotangent, fine_pre, low, high, fine_weight, cs)
    first, second = coarse_grad(pooled, received)
    coarse_low, coarse_high = edges(first, second)
    grad_skip, fine_keep, fine_send = fine_level(
        core, fine_grad, skip_feats, fine_weight, received, box, fine_cells
    )
    fine_more = lax.ppermute(fine_send, "core", SWAP)
    rows = (coarse_low, first, second, coarse_high)
    coarse_cells = samples * (lines // peers) * wide * devices
    coarse_keep, coarse_send = coarse_weight_level(core, received, rows, coarse_cells)
    coarse_more = lax.ppermute(coarse_send, "core", SWAP)
    back = coarse_input_level(coarse_weight, rows, peers)
    mine = grad_sums(fine_keep, fine_more, coarse_keep, coarse_more)
    back, mine = lax.optimization_barrier((back, mine))
    other = lax.ppermute(mine, "core", SWAP)
    back = lax.all_to_all(back, CHAN, 0, 0, tiled=True)
    grad_input = back.transpose(1, 0, 2, 4, 3).reshape(coarse_input.shape)
    grad_fine, grad_coarse = unpacked(core, mine, other, fine_weight.shape, coarse_weight.shape)
    return grad_skip, grad_input, grad_fine, grad_coarse


def solution(mesh):
    split = Mesh(mesh.devices.reshape([size for _, size in SPLIT]), tuple(name for name, _ in SPLIT))
    coarse = P(None, ROWS, None, CHAN)
    fine = P(None, ALL, None, None)
    return jax.shard_map(
        shards,
        mesh=split,
        in_specs=(coarse, coarse, fine, fine, fine, P(), P()),
        out_specs=(fine, coarse, P(), P()),
        check_vma=False,
    )
```

```python
import functools
import math

import jax
import jax.numpy as jnp
from jax import lax
from jax.experimental import pallas as pl
from jax.experimental.pallas import tpu as pltpu
from jax.sharding import Mesh
from jax.sharding import PartitionSpec as P

F32 = jnp.float32
BF16 = jnp.bfloat16
MIB = 1 << 20
VMEM = 18

SPLIT = (("xh", 2), ("z", 4), ("core", 2), ("y", 4), ("xl", 2))
ROWS = ("xh", "z", "core")
CHAN = ("y", "xl")
ALL = ROWS + CHAN
CHIPS = ("xh", "xl", "z", "y")


def params(limit):
    return pltpu.CompilerParams(vmem_limit_bytes=limit * MIB)


def cost(flops, nbytes):
    return pl.CostEstimate(flops=int(flops), bytes_accessed=int(nbytes), transcendentals=0)


def silu_grad(value):
    sigma = jax.nn.sigmoid(value)
    return sigma * (1.0 + value * (1.0 - sigma))


def shifted(field):
    extent = field.shape[0]
    index = lax.broadcasted_iota(jnp.int32, field.shape, 0)
    before = jnp.where(index == 0, 0.0, pltpu.roll(field, 1, 0))
    after = jnp.where(index == extent - 1, 0.0, pltpu.roll(field, extent - 1, 0))
    return before, after


def tdot(left, right):
    return lax.dot_general(left, right, (((0,), (0,)), ((), ())), preferred_element_type=F32)


def dott(left, right):
    return lax.dot_general(left, right, (((1,), (1,)), ((), ())), preferred_element_type=F32)


def tiles(block):
    return block.astype(BF16).reshape(block.shape[0] // 16, 16, block.shape[1])


def box_sums(upper, lower, half):
    even = upper[pl.ds(0, half, 2), :] + lower[pl.ds(0, half, 2), :]
    odd = upper[pl.ds(1, half, 2), :] + lower[pl.ds(1, half, 2), :]
    before, _ = shifted(odd)
    _, after = shifted(even)
    return (before + even).astype(BF16), (even + odd).astype(BF16), (odd + after).astype(BF16)


def box_kernel(cot_ref, pre_ref, weight_ref, grad_ref, pooled_ref, box_ref, up_weight, rows32):
    c3 = cot_ref.shape[-1]
    c4 = pooled_ref.shape[-1]
    half = pooled_ref.shape[-2]
    reach = 3 * c3

    @pl.when(pl.program_id(0) == 0)
    def _():
        for dy in range(3):
            for d in range(3):
                at = (dy * 3 + d) * c3
                up_weight[at : at + c3, :] = weight_ref[2 - dy, 2 - d, :c4, :].astype(F32).T.astype(BF16)

    for v in range(4):
        grad = (cot_ref[0, v].astype(F32) * silu_grad(pre_ref[0, v].astype(F32))).astype(BF16)
        grad_ref[0, v] = grad
        rows32[v] = grad.astype(F32)
    for v in range(3):
        for d, value in enumerate(box_sums(rows32.at[v], rows32.at[v + 1], half)):
            at = v * reach + d * c3
            box_ref[0, :, at : at + c3] = value
    pooled_ref[0, 0] = jnp.dot(box_ref[0, :, : 2 * reach], up_weight[reach:, :], preferred_element_type=F32)
    pooled_ref[0, 1] = jnp.dot(box_ref[0, :, reach:], up_weight[: 2 * reach, :], preferred_element_type=F32)


def box_level(cot, pre, weight, cs):
    samples, height, wide, c3 = cot.shape
    c4 = weight.shape[2] - cs
    half = wide // 2
    block = pl.BlockSpec((1, height, wide, c3), lambda s: (s, 0, 0, 0))
    return pl.pallas_call(
        box_kernel,
        grid=(samples,),
        in_specs=[block, block, pl.BlockSpec(weight.shape, lambda s: (0, 0, 0, 0))],
        out_specs=[
            block,
            pl.BlockSpec((1, 2, half, c4), lambda s: (s, 0, 0, 0)),
            pl.BlockSpec((1, half, 9 * c3), lambda s: (s, 0, 0)),
            pl.BlockSpec((9 * c3, c4), lambda s: (0, 0)),
        ],
        out_shape=[
            jax.ShapeDtypeStruct((samples, height, wide, c3), BF16),
            jax.ShapeDtypeStruct((samples, 2, half, c4), F32),
            jax.ShapeDtypeStruct((samples, half, 9 * c3), BF16),
            jax.ShapeDtypeStruct((9 * c3, c4), BF16),
        ],
        scratch_shapes=[pltpu.VMEM((height, wide, c3), F32)],
        compiler_params=params(VMEM),
        cost_estimate=cost(1.2e9, 8e6),
        name="box_level",
    )(cot, pre, weight)


def fine_kernel(
    core_ref, grad_ref, low_ref, high_ref, skip_ref, weight_ref, grad_skip_ref, keep_ref, send_ref, taps, skip_weight, total, *, scale
):
    sample = pl.program_id(0)
    c3 = grad_ref.shape[-1]
    cs = skip_ref.shape[-1]
    c4 = weight_ref.shape[2] - cs

    @pl.when(sample == 0)
    def _():
        total[...] = jnp.zeros_like(total)
        for u in range(4):
            for d in range(3):
                at = (u * 3 + d) * c3
                for t in range(2):
                    dy = u - t
                    if 0 <= dy <= 2:
                        block = weight_ref[2 - dy, 2 - d, c4:, :].astype(F32).T.astype(BF16)
                    else:
                        block = jnp.zeros((c3, cs), BF16)
                    skip_weight[at : at + c3, t * cs : (t + 1) * cs] = block

    for v in range(6):
        grad = low_ref[0] if v == 0 else high_ref[0] if v == 5 else grad_ref[0, v - 1]
        before, after = shifted(grad.astype(F32))
        at = v * 3 * c3
        taps[:, at : at + c3] = before.astype(BF16)
        taps[:, at + c3 : at + 2 * c3] = grad
        taps[:, at + 2 * c3 : at + 3 * c3] = after.astype(BF16)

    for pair in range(2):
        window = taps[:, 2 * pair * 3 * c3 : (2 * pair + 4) * 3 * c3]
        back = jnp.dot(window, skip_weight[...], preferred_element_type=F32)
        grad_skip_ref[0, 2 * pair] = back[:, :cs].astype(BF16)
        grad_skip_ref[0, 2 * pair + 1] = back[:, cs:].astype(BF16)
        feats = jnp.concatenate([skip_ref[0, 2 * pair], skip_ref[0, 2 * pair + 1]], axis=1)
        total[...] += tdot(feats, window)

    @pl.when(sample == pl.num_programs(0) - 1)
    def _():
        core = core_ref[0]

        part = cs // 2
        for dy in range(3):
            for d in range(3):
                first = (dy * 3 + d) * c3
                second = ((dy + 1) * 3 + d) * c3
                value = (total[:cs, first : first + c3] + total[cs:, second : second + c3]) * scale
                low, high = value[:part], value[part:]
                tap = (2 - dy) * 3 + 2 - d
                keep_ref[tap] = tiles(jnp.where(core == 0, low, high))
                send_ref[tap] = tiles(jnp.where(core == 0, high, low))


def fine_level(core, grad, low, high, skip, weight, fine_cells):
    samples, height, wide, cs = skip.shape
    c3 = grad.shape[-1]
    part = jax.ShapeDtypeStruct((9, cs // 32, 16, c3), BF16)
    whole = pl.BlockSpec(part.shape, lambda s: (0, 0, 0, 0))
    return pl.pallas_call(
        functools.partial(fine_kernel, scale=1.0 / math.sqrt(fine_cells)),
        grid=(samples,),
        in_specs=[
            pl.BlockSpec(memory_space=pltpu.SMEM),
            pl.BlockSpec((1, height, wide, c3), lambda s: (s, 0, 0, 0)),
            pl.BlockSpec((1, wide, c3), lambda s: (s, 0, 0)),
            pl.BlockSpec((1, wide, c3), lambda s: (s, 0, 0)),
            pl.BlockSpec((1, height, wide, cs), lambda s: (s, 0, 0, 0)),
            pl.BlockSpec(weight.shape, lambda s: (0, 0, 0, 0)),
        ],
        out_specs=[pl.BlockSpec((1, height, wide, cs), lambda s: (s, 0, 0, 0)), whole, whole],
        out_shape=[jax.ShapeDtypeStruct((samples, height, wide, cs), BF16), part, part],
        scratch_shapes=[
            pltpu.VMEM((wide, 18 * c3), BF16),
            pltpu.VMEM((12 * c3, 2 * cs), BF16),
            pltpu.VMEM((2 * cs, 12 * c3), F32),
        ],
        compiler_params=params(VMEM),
        cost_estimate=cost(5e9, 8e6),
        name="fine_level",
    )(core, grad, low, high, skip, weight)


def coarse_grad_kernel(
    low_ref, high_ref, top_ref, bottom_ref, pooled_ref, low_weight_ref, high_weight_ref, pre_ref,
    first_ref, second_ref, box_low_ref, box_high_ref, edge32,
):
    channels, half = pooled_ref.shape[-1], pooled_ref.shape[-2]
    c3 = low_ref.shape[-1]
    sides = (
        (low_ref, top_ref, low_weight_ref, first_ref, box_low_ref),
        (bottom_ref, high_ref, high_weight_ref, second_ref, box_high_ref),
    )
    for i, (upper, lower, weight_ref, out_ref, box_ref) in enumerate(sides):
        edge32[0] = upper[...].reshape(edge32.shape[1:]).astype(F32)
        edge32[1] = lower[...].reshape(edge32.shape[1:]).astype(F32)
        for d, value in enumerate(box_sums(edge32.at[0], edge32.at[1], half)):
            box_ref[0, :, d * c3 : (d + 1) * c3] = value
        pooled = pooled_ref[0, i] + jnp.dot(box_ref[0], weight_ref[...], preferred_element_type=F32)
        value = pre_ref[:, 0, 0, i].reshape(channels, half).astype(F32).T
        out_ref[0] = (pooled * silu_grad(value)).astype(BF16)


def coarse_grad(low, high, grad, pooled, up_weight, received):
    samples, _, half, c4 = pooled.shape
    peers, _, _, _, own, _ = received.shape
    _, height, wide, c3 = grad.shape
    out = jax.ShapeDtypeStruct((samples, half, c4), BF16)
    box = jax.ShapeDtypeStruct((samples, half, 3 * c3), BF16)
    edge = pl.BlockSpec((1, wide, c3), lambda s: (s, 0, 0))
    spec = pl.BlockSpec((1, half, c4), lambda s: (s, 0, 0))
    box_spec = pl.BlockSpec((1, half, 3 * c3), lambda s: (s, 0, 0))
    return pl.pallas_call(
        coarse_grad_kernel,
        grid=(samples,),
        in_specs=[
            edge, edge,
            pl.BlockSpec((1, 1, wide, c3), lambda s: (s, 0, 0, 0)),
            pl.BlockSpec((1, 1, wide, c3), lambda s: (s, height - 1, 0, 0)),
            pl.BlockSpec((1, 2, half, c4), lambda s: (s, 0, 0, 0)),
            pl.BlockSpec((3 * c3, c4), lambda s: (0, 0)),
            pl.BlockSpec((3 * c3, c4), lambda s: (2, 0)),
            pl.BlockSpec((peers, 1, 1, 2, own, half), lambda s: (0, 0, s, 0, 0, 0)),
        ],
        out_specs=[spec, spec, box_spec, box_spec],
        out_shape=[out, out, box, box],
        scratch_shapes=[pltpu.VMEM((2, wide, c3), F32)],
        compiler_params=params(VMEM),
        cost_estimate=cost(4e8, 4e6),
        name="coarse_grad",
    )(low, high, grad, grad, pooled, up_weight, up_weight, received)


def up_kernel(
    core_ref, pre_ref, box_ref, box_low_ref, box_high_ref, skip_keep_ref, skip_send_ref, keep_ref, send_ref, total,
    *, scale
):
    sample = pl.program_id(0)
    wide = pre_ref.shape[-1]
    c4 = pre_ref.shape[0] * pre_ref.shape[-2]
    c3 = keep_ref.shape[-1]

    @pl.when(sample == 0)
    def _():
        total[...] = jnp.zeros_like(total)

    reach = 3 * c3
    windows = (
        ((0, box_low_ref[0]), (reach, box_ref[0, :, : 2 * reach])),
        ((0, box_ref[0, :, reach:]), (2 * reach, box_high_ref[0])),
    )
    for i in range(2):
        value = pre_ref[:, 0, 0, i].reshape(c4, wide).astype(F32)
        value = (value * jax.nn.sigmoid(value)).astype(BF16)
        for at, window in windows[i]:
            total[:, at : at + window.shape[1]] += jnp.dot(value, window, preferred_element_type=F32)

    @pl.when(sample == pl.num_programs(0) - 1)
    def _():
        core = core_ref[0]
        part = c4 // 2
        mine = part // 16
        for dy in range(3):
            for d in range(3):
                at = (dy * 3 + d) * c3
                value = total[:, at : at + c3] * scale
                low, high = value[:part], value[part:]
                tap = (2 - dy) * 3 + 2 - d
                keep_ref[tap, :mine] = tiles(jnp.where(core == 0, low, high))
                send_ref[tap, :mine] = tiles(jnp.where(core == 0, high, low))
                keep_ref[tap, mine:] = skip_keep_ref[tap]
                send_ref[tap, mine:] = skip_send_ref[tap]


def up_level(core, received, box, box_low, box_high, skip_keep, skip_send, fine_cells):
    peers, _, samples, _, own, wide = received.shape
    c4 = peers * own
    c3 = box.shape[-1] // 9
    part = jax.ShapeDtypeStruct((9, c4 // 32 + skip_keep.shape[1], 16, c3), BF16)
    whole = pl.BlockSpec(part.shape, lambda s: (0, 0, 0, 0))
    skips = pl.BlockSpec(skip_keep.shape, lambda s: (0, 0, 0, 0))
    return pl.pallas_call(
        functools.partial(up_kernel, scale=1.0 / math.sqrt(fine_cells)),
        grid=(samples,),
        in_specs=[
            pl.BlockSpec(memory_space=pltpu.SMEM),
            pl.BlockSpec((peers, 1, 1, 2, own, wide), lambda s: (0, 0, s, 0, 0, 0)),
            pl.BlockSpec((1, wide, 9 * c3), lambda s: (s, 0, 0)),
            pl.BlockSpec((1, wide, 3 * c3), lambda s: (s, 0, 0)),
            pl.BlockSpec((1, wide, 3 * c3), lambda s: (s, 0, 0)),
            skips, skips,
        ],
        out_specs=[whole, whole],
        out_shape=[part, part],
        scratch_shapes=[pltpu.VMEM((c4, 9 * c3), F32)],
        compiler_params=params(VMEM),
        cost_estimate=cost(1e9, 5e6),
        name="up_level",
    )(core, received, box, box_low, box_high, skip_keep, skip_send)


def fill_coarse_taps(rows, taps):
    wide, c4 = rows[0].shape
    for v, row in enumerate(rows):
        value = row.astype(F32)
        before, after = shifted(value)
        taps[v * wide : (v + 1) * wide, :c4] = before.astype(BF16)
        taps[v * wide : (v + 1) * wide, c4 : 2 * c4] = row
        taps[v * wide : (v + 1) * wide, 2 * c4 :] = after.astype(BF16)


def coarse_weight_kernel(
    core_ref, input_ref, low_ref, first_ref, second_ref, high_ref, keep_ref, send_ref, taps, total, *, scale
):
    sample = pl.program_id(0)
    wide = input_ref.shape[-1]
    c4 = input_ref.shape[0] * input_ref.shape[-2]

    @pl.when(sample == 0)
    def _():
        total[...] = jnp.zeros_like(total)

    fill_coarse_taps((low_ref[0], first_ref[0], second_ref[0], high_ref[0]), taps)
    values = jnp.concatenate([input_ref[:, 0, 0, i].reshape(c4, wide) for i in range(2)], axis=1)
    for dy in range(3):
        total[dy] += jnp.dot(values, taps[dy * wide : (dy + 2) * wide, :], preferred_element_type=F32)

    @pl.when(sample == pl.num_programs(0) - 1)
    def _():
        core = core_ref[0]
        part = c4 // 2
        count = part // 16
        for dy in range(3):
            for d in range(3):
                for side in range(c4 // 128):
                    at = d * c4 + side * 128
                    value = total[dy, :, at : at + 128] * scale
                    low, high = value[:part], value[part:]
                    tap = ((2 - dy) * 3 + 2 - d) * (c4 // 128) + side
                    keep_ref[tap * count : (tap + 1) * count] = tiles(jnp.where(core == 0, low, high))
                    send_ref[tap * count : (tap + 1) * count] = tiles(jnp.where(core == 0, high, low))


def coarse_specs(wide, c4, count):
    return [pl.BlockSpec((1, wide, c4), lambda s: (s, 0, 0))] * count


def coarse_weight_level(core, received, rows, coarse_cells):
    peers, _, samples, _, own, wide = received.shape
    c4 = peers * own
    part = jax.ShapeDtypeStruct((9 * (c4 // 128) * (c4 // 32), 16, 128), BF16)
    whole = pl.BlockSpec(part.shape, lambda s: (0, 0, 0))
    return pl.pallas_call(
        functools.partial(coarse_weight_kernel, scale=1.0 / math.sqrt(coarse_cells)),
        grid=(samples,),
        in_specs=[
            pl.BlockSpec(memory_space=pltpu.SMEM),
            pl.BlockSpec((peers, 1, 1, 2, own, wide), lambda s: (0, 1, s, 0, 0, 0)),
        ] + coarse_specs(wide, c4, 4),
        out_specs=[whole, whole],
        out_shape=[part, part],
        scratch_shapes=[pltpu.VMEM((4 * wide, 3 * c4), BF16), pltpu.VMEM((3, c4, 3 * c4), F32)],
        compiler_params=params(VMEM),
        cost_estimate=cost(1.3e9, 3e6),
        name="coarse_weight_level",
    )(core, received, *rows)


def coarse_input_kernel(chan_ref, weight_ref, low_ref, first_ref, second_ref, high_ref, *rest):
    *piece_refs, taps, stage = rest
    wide, c4 = low_ref.shape[1:]
    own = c4 // len(piece_refs)
    fill_coarse_taps((low_ref[0], first_ref[0], second_ref[0], high_ref[0]), taps)
    total = None
    for dy in range(3):
        for d in range(3):
            window = taps[dy * wide : (dy + 2) * wide, d * c4 : (d + 1) * c4]
            term = dott(weight_ref[2 - dy, 2 - d], window)
            total = term if total is None else total + term
    stage[...] = total.astype(BF16)
    for k, ref in enumerate(piece_refs):
        at = pl.multiple_of(jnp.bitwise_xor(chan_ref[0], k) * own, own)
        for i in range(2):
            ref[0, i] = stage[pl.ds(at, own), i * wide : (i + 1) * wide]


def coarse_input_level(chan, weight, rows, peers):
    samples, wide, c4 = rows[0].shape
    own = c4 // peers
    return pl.pallas_call(
        coarse_input_kernel,
        grid=(samples,),
        in_specs=[
            pl.BlockSpec(memory_space=pltpu.SMEM),
            pl.BlockSpec(weight.shape, lambda s: (0, 0, 0, 0)),
        ] + coarse_specs(wide, c4, 4),
        out_specs=[pl.BlockSpec((1, 2, own, wide), lambda s: (s, 0, 0, 0))] * peers,
        out_shape=[jax.ShapeDtypeStruct((samples, 2, own, wide), BF16)] * peers,
        scratch_shapes=[pltpu.VMEM((4 * wide, 3 * c4), BF16), pltpu.VMEM((c4, 2 * wide), BF16)],
        compiler_params=params(VMEM),
        cost_estimate=cost(1.3e9, 3e6),
        name="coarse_input_level",
    )(chan, weight, *rows)


def place_kernel(chan_ref, *refs):
    *piece_refs, out_ref = refs
    for k, ref in enumerate(piece_refs):
        at = jnp.bitwise_xor(chan_ref[0], k) * 2
        out_ref[:, pl.ds(at, 2)] = ref[...]


def placed(chan, pieces):
    samples, rows, own, wide = pieces[0].shape
    return pl.pallas_call(
        place_kernel,
        in_specs=[pl.BlockSpec(memory_space=pltpu.SMEM)] + [pl.BlockSpec(memory_space=pltpu.VMEM)] * len(pieces),
        out_shape=jax.ShapeDtypeStruct((samples, rows * len(pieces), own, wide), BF16),
        compiler_params=params(VMEM),
        cost_estimate=cost(1e6, 1e6),
        name="place",
    )(chan, *pieces)


def join_kernel(coarse_ref, coarse_more_ref, fine_ref, fine_more_ref, out_ref):
    count = coarse_ref.shape[0]
    out_ref[:count] = (coarse_ref[...].astype(F32) + coarse_more_ref[...].astype(F32)).astype(BF16)
    fines = fine_ref.shape[0]
    out_ref[count : count + fines] = (fine_ref[...].astype(F32) + fine_more_ref[...].astype(F32)).astype(BF16)
    rest = out_ref.shape[0] - count - fines
    if rest:
        out_ref[count + fines :] = jnp.zeros((rest,) + out_ref.shape[1:], BF16)


def sum_kernel(parts_ref, out_ref):
    total = parts_ref[0].astype(F32)
    for k in range(1, parts_ref.shape[0]):
        total = total + parts_ref[k].astype(F32)
    total = total.astype(BF16)
    for k in range(out_ref.shape[0]):
        out_ref[k] = total


def unpack_kernel(core_ref, mine_ref, other_ref, fine_ref, coarse_ref):
    c4 = coarse_ref.shape[-1]
    cs = fine_ref.shape[-2] - c4
    sides = c4 // 128
    lines = c4 // 32
    skips = cs // 32
    mine = core_ref[0]
    for core in range(2):

        def take(at, count):
            block = jnp.where(mine == core, mine_ref[at : at + count].astype(F32), other_ref[at : at + count].astype(F32))
            return block.reshape(count * 16, 128)

        for tap in range(9):
            for side in range(sides):
                block = take((tap * sides + side) * lines, lines)
                coarse_ref[tap, core * lines * 16 : (core + 1) * lines * 16, side * 128 : (side + 1) * 128] = block
            at = 9 * sides * lines + tap * (lines + skips)
            fine_ref[tap, core * lines * 16 : (core + 1) * lines * 16, :] = take(at, lines)
            fine_ref[tap, c4 + core * skips * 16 : c4 + (core + 1) * skips * 16, :] = take(at + lines, skips)


SWAP = ((0, 1), (1, 0))


def grad_sums(fine_keep, fine_more, coarse_keep, coarse_more, back):
    chips = 1
    for axis in CHIPS:
        chips *= lax.axis_size(axis)
    fine_keep, fine_more = (a.reshape((-1, 16, 128)) for a in (fine_keep, fine_more))
    count = coarse_keep.shape[0] + fine_keep.shape[0]
    each = -(-count // chips)
    joined = pl.pallas_call(
        join_kernel,
        out_shape=jax.ShapeDtypeStruct((chips * each, 16, 128), BF16),
        compiler_params=params(VMEM),
        cost_estimate=cost(1e6, 3e6),
        name="join",
    )(coarse_keep, coarse_more, fine_keep, fine_more)
    parts = lax.all_to_all(joined.reshape(chips, each, 16, 128), CHIPS, 0, 0, tiled=True)
    summed = pl.pallas_call(
        sum_kernel,
        out_shape=jax.ShapeDtypeStruct((chips, each, 16, 128), BF16),
        compiler_params=params(VMEM),
        cost_estimate=cost(1e6, 1.3e6),
        name="sum_parts",
    )(parts)
    summed, *back = lax.optimization_barrier((summed, *back))
    return lax.all_to_all(summed, CHIPS, 0, 0, tiled=True).reshape(chips * each, 16, 128), back


def unpacked(core, mine, other, fine_shape, coarse_shape):
    fine_flat = (9,) + fine_shape[2:]
    coarse_flat = (9,) + coarse_shape[2:]
    vmem = pl.BlockSpec(memory_space=pltpu.VMEM)
    fine, coarse = pl.pallas_call(
        unpack_kernel,
        in_specs=[pl.BlockSpec(memory_space=pltpu.SMEM), vmem, vmem],
        out_shape=[jax.ShapeDtypeStruct(fine_flat, F32), jax.ShapeDtypeStruct(coarse_flat, F32)],
        compiler_params=params(VMEM),
        cost_estimate=cost(1e6, 6e6),
        name="unpack",
    )(core, mine, other)
    return fine.reshape(fine_shape), coarse.reshape(coarse_shape)


def edges(low, high, axes):
    count = 1
    for axis in axes:
        count *= lax.axis_size(axis)
    forward = [(i, i + 1) for i in range(count - 1)]
    backward = [(target, source) for source, target in forward]
    return lax.ppermute(high, axes, forward), lax.ppermute(low, axes, backward)


def shards(coarse_input, coarse_pre, skip_feats, fine_pre, fine_cotangent, fine_weight, coarse_weight):
    peers = 1
    for axis in CHAN:
        peers *= lax.axis_size(axis)
    devices = peers
    for axis in ROWS:
        devices *= lax.axis_size(axis)
    samples, lines, wide, own = coarse_input.shape
    core = lax.axis_index("core").astype(jnp.int32).reshape(1)
    chan = lax.axis_index(CHAN).astype(jnp.int32).reshape(1)

    def grad_row(line):
        return (
            fine_cotangent[:, line].astype(F32) * silu_grad(fine_pre[:, line].astype(F32))
        ).astype(BF16)

    pieces = jnp.stack([coarse_pre, coarse_input]).reshape(2, samples, peers, lines // peers, wide, own)
    pieces = pieces.transpose(2, 0, 1, 3, 5, 4)
    received = lax.all_to_all(pieces, CHAN, 0, 0, tiled=True)
    low, high = edges(grad_row(0), grad_row(-1), ALL)

    cs = skip_feats.shape[-1]
    fine_cells = fine_pre.shape[0] * fine_pre.shape[1] * fine_pre.shape[2] * devices
    fine_grad, pooled, box, up_weight = box_level(fine_cotangent, fine_pre, fine_weight, cs)
    pooled = pltpu.with_memory_space_constraint(pooled, pltpu.HBM)
    first, second, box_low, box_high = coarse_grad(low, high, fine_grad, pooled, up_weight, received)
    coarse_low, coarse_high = edges(first, second, ALL)
    low, first = lax.optimization_barrier((low, first))
    grad_skip, skip_keep, skip_send = fine_level(core, fine_grad, low, high, skip_feats, fine_weight, fine_cells)
    fine_keep, fine_send = up_level(core, received, box, box_low, box_high, skip_keep, skip_send, fine_cells)
    fine_more = lax.ppermute(fine_send, "core", SWAP)
    coarse_low, coarse_high, fine_keep = lax.optimization_barrier((coarse_low, coarse_high, fine_keep))
    rows = (coarse_low, first, second, coarse_high)
    coarse_cells = samples * (lines // peers) * wide * devices
    coarse_keep, coarse_send = coarse_weight_level(core, received, rows, coarse_cells)
    coarse_more = lax.ppermute(coarse_send, "core", SWAP)
    back = coarse_input_level(chan, coarse_weight, rows, peers)
    back = [back[0]] + [
        lax.ppermute(back[k], CHAN, [(i, i ^ k) for i in range(peers)]) for k in range(1, peers)
    ]
    mine, back = grad_sums(fine_keep, fine_more, coarse_keep, coarse_more, back)
    other = lax.ppermute(mine, "core", SWAP)
    grad_input = placed(chan, back).transpose(0, 1, 3, 2)
    grad_fine, grad_coarse = unpacked(core, mine, other, fine_weight.shape, coarse_weight.shape)
    return grad_skip, grad_input, grad_fine, grad_coarse


def solution(mesh):
    split = Mesh(mesh.devices.reshape([size for _, size in SPLIT]), tuple(name for name, _ in SPLIT))
    coarse = P(None, ROWS, None, CHAN)
    fine = P(None, ALL, None, None)
    return jax.shard_map(
        shards,
        mesh=split,
        in_specs=(coarse, coarse, fine, fine, fine, P(), P()),
        out_specs=(fine, coarse, P(), P()),
        check_vma=False,
    )
```

```python
import functools
import math

import jax
import jax.numpy as jnp
from jax import lax
from jax.experimental import pallas as pl
from jax.experimental.pallas import tpu as pltpu
from jax.sharding import Mesh
from jax.sharding import PartitionSpec as P

F32 = jnp.float32
BF16 = jnp.bfloat16
MIB = 1 << 20
VMEM = 18
EARLY = 6
LONG = 1e11

SPLIT = (("xh", 2), ("z", 4), ("core", 2), ("y", 4), ("xl", 2))
ROWS = ("xh", "z", "core")
CHAN = ("y", "xl")
ALL = ROWS + CHAN
CHIPS = ("xh", "xl", "z", "y")


def params(limit):
    return pltpu.CompilerParams(vmem_limit_bytes=limit * MIB)


def cost(flops, nbytes):
    return pl.CostEstimate(flops=int(flops), bytes_accessed=int(nbytes), transcendentals=0)


def in_hbm(array):
    return pltpu.with_memory_space_constraint(array, pltpu.HBM)


def silu_grad(value):
    sigma = jax.nn.sigmoid(value)
    return sigma * (1.0 + value * (1.0 - sigma))


def shifted(field):
    extent = field.shape[0]
    index = lax.broadcasted_iota(jnp.int32, field.shape, 0)
    before = jnp.where(index == 0, 0.0, pltpu.roll(field, 1, 0))
    after = jnp.where(index == extent - 1, 0.0, pltpu.roll(field, extent - 1, 0))
    return before, after


def tdot(left, right):
    return lax.dot_general(left, right, (((0,), (0,)), ((), ())), preferred_element_type=F32)


def dott(left, right):
    return lax.dot_general(left, right, (((1,), (1,)), ((), ())), preferred_element_type=F32)


def tiles(block):
    return block.astype(BF16).reshape(block.shape[0] // 16, 16, block.shape[1])


def box_sums(upper, lower, half):
    even = upper[pl.ds(0, half, 2), :] + lower[pl.ds(0, half, 2), :]
    odd = upper[pl.ds(1, half, 2), :] + lower[pl.ds(1, half, 2), :]
    before, _ = shifted(odd)
    _, after = shifted(even)
    return (before + even).astype(BF16), (even + odd).astype(BF16), (odd + after).astype(BF16)


def box_kernel(
    place_ref, cot_ref, pre_ref, near_ref, far_ref, weight_ref, grad_ref, pooled_ref, box_ref, rows32, up_weight
):
    c3 = cot_ref.shape[-1]
    c4 = pooled_ref.shape[-1]
    half = pooled_ref.shape[-2]
    odd = place_ref[0] >= 2

    @pl.when(pl.program_id(0) == 0)
    def _():
        for dy in range(3):
            for d in range(3):
                at = (dy * 3 + d) * c3
                up_weight[at : at + c3, :] = weight_ref[2 - dy, 2 - d, :c4, :].astype(F32).T.astype(BF16)

    for v in range(6):
        if v == 0:
            grad = jnp.where(odd, near_ref[0], far_ref[0])
        elif v == 5:
            grad = jnp.where(odd, far_ref[0], near_ref[0])
        else:
            grad = (cot_ref[0, v - 1].astype(F32) * silu_grad(pre_ref[0, v - 1].astype(F32))).astype(BF16)
        grad_ref[0, v] = grad
        rows32[v] = grad.astype(F32)
    for v in range(5):
        sums = box_sums(rows32.at[v], rows32.at[v + 1], half)
        for i in range(2):
            dy = v - 2 * i
            if 0 <= dy <= 2:
                for d in range(3):
                    at = (dy * 3 + d) * c3
                    box_ref[0, i * half : (i + 1) * half, at : at + c3] = sums[d]
    pooled = jnp.dot(box_ref[0], up_weight[...], preferred_element_type=F32)
    pooled_ref[0] = pooled.reshape(pooled_ref.shape[1:])


def box_level(place, cot, pre, near, far, weight, cs):
    samples, height, wide, c3 = cot.shape
    c4 = weight.shape[2] - cs
    half = wide // 2
    block = pl.BlockSpec((1, height, wide, c3), lambda s: (s, 0, 0, 0))
    edge = pl.BlockSpec((1, wide, c3), lambda s: (s, 0, 0))
    return pl.pallas_call(
        box_kernel,
        grid=(samples,),
        in_specs=[
            pl.BlockSpec(memory_space=pltpu.SMEM), block, block, edge, edge,
            pl.BlockSpec(weight.shape, lambda s: (0, 0, 0, 0)),
        ],
        out_specs=[
            pl.BlockSpec((1, height + 2, wide, c3), lambda s: (s, 0, 0, 0)),
            pl.BlockSpec((1, 2, half, c4), lambda s: (s, 0, 0, 0)),
            pl.BlockSpec((1, 2 * half, 9 * c3), lambda s: (s, 0, 0)),
        ],
        out_shape=[
            jax.ShapeDtypeStruct((samples, height + 2, wide, c3), BF16),
            jax.ShapeDtypeStruct((samples, 2, half, c4), F32),
            jax.ShapeDtypeStruct((samples, 2 * half, 9 * c3), BF16),
        ],
        scratch_shapes=[pltpu.VMEM((6, wide, c3), F32), pltpu.VMEM((9 * c3, c4), BF16)],
        compiler_params=params(VMEM),
        cost_estimate=cost(LONG, 8e6),
        name="box_level",
    )(place, cot, pre, near, far, weight)


def fine_kernel(
    place_ref, grad_ref, skip_ref, weight_ref, grad_skip_ref, keep_ref, send_ref, taps, skip_weight, total, *, scale
):
    sample = pl.program_id(0)
    c3 = grad_ref.shape[-1]
    cs = skip_ref.shape[-1]
    c4 = weight_ref.shape[2] - cs

    @pl.when(sample == 0)
    def _():
        total[...] = jnp.zeros_like(total)
        for u in range(4):
            for d in range(3):
                at = (u * 3 + d) * c3
                for t in range(2):
                    dy = u - t
                    if 0 <= dy <= 2:
                        block = weight_ref[2 - dy, 2 - d, c4:, :].astype(F32).T.astype(BF16)
                    else:
                        block = jnp.zeros((c3, cs), BF16)
                    skip_weight[at : at + c3, t * cs : (t + 1) * cs] = block

    for v in range(6):
        grad = grad_ref[0, v]
        before, after = shifted(grad.astype(F32))
        at = v * 3 * c3
        taps[:, at : at + c3] = before.astype(BF16)
        taps[:, at + c3 : at + 2 * c3] = grad
        taps[:, at + 2 * c3 : at + 3 * c3] = after.astype(BF16)

    for pair in range(2):
        window = taps[:, 2 * pair * 3 * c3 : (2 * pair + 4) * 3 * c3]
        back = jnp.dot(window, skip_weight[...], preferred_element_type=F32)
        grad_skip_ref[0, 2 * pair] = back[:, :cs].astype(BF16)
        grad_skip_ref[0, 2 * pair + 1] = back[:, cs:].astype(BF16)
        feats = jnp.concatenate([skip_ref[0, 2 * pair], skip_ref[0, 2 * pair + 1]], axis=1)
        total[...] += tdot(feats, window)

    @pl.when(sample == pl.num_programs(0) - 1)
    def _():
        core = place_ref[0] % 2

        part = cs // 2
        for dy in range(3):
            for d in range(3):
                first = (dy * 3 + d) * c3
                second = ((dy + 1) * 3 + d) * c3
                value = (total[:cs, first : first + c3] + total[cs:, second : second + c3]) * scale
                low, high = value[:part], value[part:]
                tap = (2 - dy) * 3 + 2 - d
                keep_ref[tap] = tiles(jnp.where(core == 0, low, high))
                send_ref[tap] = tiles(jnp.where(core == 0, high, low))


def fine_level(place, grad, skip, weight, fine_cells):
    samples, height, wide, cs = skip.shape
    c3 = grad.shape[-1]
    part = jax.ShapeDtypeStruct((9, cs // 32, 16, c3), BF16)
    whole = pl.BlockSpec(part.shape, lambda s: (0, 0, 0, 0))
    return pl.pallas_call(
        functools.partial(fine_kernel, scale=1.0 / math.sqrt(fine_cells)),
        grid=(samples,),
        in_specs=[
            pl.BlockSpec(memory_space=pltpu.SMEM),
            pl.BlockSpec((1, height + 2, wide, c3), lambda s: (s, 0, 0, 0)),
            pl.BlockSpec((1, height, wide, cs), lambda s: (s, 0, 0, 0)),
            pl.BlockSpec(weight.shape, lambda s: (0, 0, 0, 0)),
        ],
        out_specs=[pl.BlockSpec((1, height, wide, cs), lambda s: (s, 0, 0, 0)), whole, whole],
        out_shape=[jax.ShapeDtypeStruct((samples, height, wide, cs), BF16), part, part],
        scratch_shapes=[
            pltpu.VMEM((wide, 18 * c3), BF16),
            pltpu.VMEM((12 * c3, 2 * cs), BF16),
            pltpu.VMEM((2 * cs, 12 * c3), F32),
        ],
        compiler_params=params(VMEM),
        cost_estimate=cost(5e9, 8e6),
        name="fine_level",
    )(place, grad, skip, weight)


def coarse_grad_kernel(place_ref, pooled_ref, pre_ref, near_ref, far_ref):
    channels, half = pooled_ref.shape[-1], pooled_ref.shape[-2]
    odd = place_ref[0] >= 2
    rows = []
    for i in range(2):
        value = pre_ref[:, 0, 0, i].reshape(channels, half).astype(F32).T
        rows.append((pooled_ref[0, i] * silu_grad(value)).astype(BF16))
    near_ref[0] = jnp.where(odd, rows[0], rows[1])
    far_ref[0] = jnp.where(odd, rows[1], rows[0])


def coarse_grad(place, pooled, received):
    samples, _, half, c4 = pooled.shape
    peers, _, _, _, own, _ = received.shape
    out = jax.ShapeDtypeStruct((samples, half, c4), BF16)
    spec = pl.BlockSpec((1, half, c4), lambda s: (s, 0, 0))
    return pl.pallas_call(
        coarse_grad_kernel,
        grid=(samples,),
        in_specs=[
            pl.BlockSpec(memory_space=pltpu.SMEM),
            pl.BlockSpec((1, 2, half, c4), lambda s: (s, 0, 0, 0)),
            pl.BlockSpec((peers, 1, 1, 2, own, half), lambda s: (0, 0, s, 0, 0, 0)),
        ],
        out_specs=[spec, spec],
        out_shape=[out, out],
        compiler_params=params(VMEM),
        cost_estimate=cost(2e7, 2e6),
        name="coarse_grad",
    )(place, in_hbm(pooled), received)


def up_kernel(
    place_ref, pre_ref, box_ref, skip_keep_ref, skip_send_ref, keep_ref, send_ref, total, *, scale
):
    sample = pl.program_id(0)
    wide = pre_ref.shape[-1]
    c4 = pre_ref.shape[0] * pre_ref.shape[-2]
    c3 = keep_ref.shape[-1]

    @pl.when(sample == 0)
    def _():
        total[...] = jnp.zeros_like(total)

    value = jnp.concatenate([pre_ref[:, 0, 0, i].reshape(c4, wide) for i in range(2)], axis=1).astype(F32)
    value = (value * jax.nn.sigmoid(value)).astype(BF16)
    total[...] += jnp.dot(value, box_ref[0], preferred_element_type=F32)

    @pl.when(sample == pl.num_programs(0) - 1)
    def _():
        core = place_ref[0] % 2
        part = c4 // 2
        mine = part // 16
        for dy in range(3):
            for d in range(3):
                at = (dy * 3 + d) * c3
                value = total[:, at : at + c3] * scale
                low, high = value[:part], value[part:]
                tap = (2 - dy) * 3 + 2 - d
                keep_ref[tap, :mine] = tiles(jnp.where(core == 0, low, high))
                send_ref[tap, :mine] = tiles(jnp.where(core == 0, high, low))
                keep_ref[tap, mine:] = skip_keep_ref[tap]
                send_ref[tap, mine:] = skip_send_ref[tap]


def up_level(place, received, box, skip_keep, skip_send, fine_cells):
    peers, _, samples, _, own, wide = received.shape
    c4 = peers * own
    c3 = box.shape[-1] // 9
    part = jax.ShapeDtypeStruct((9, c4 // 32 + skip_keep.shape[1], 16, c3), BF16)
    whole = pl.BlockSpec(part.shape, lambda s: (0, 0, 0, 0))
    skips = pl.BlockSpec(skip_keep.shape, lambda s: (0, 0, 0, 0))
    return pl.pallas_call(
        functools.partial(up_kernel, scale=1.0 / math.sqrt(fine_cells)),
        grid=(samples,),
        in_specs=[
            pl.BlockSpec(memory_space=pltpu.SMEM),
            pl.BlockSpec((peers, 1, 1, 2, own, wide), lambda s: (0, 0, s, 0, 0, 0)),
            pl.BlockSpec((1, 2 * wide, 9 * c3), lambda s: (s, 0, 0)),
            skips, skips,
        ],
        out_specs=[whole, whole],
        out_shape=[part, part],
        scratch_shapes=[pltpu.VMEM((c4, 9 * c3), F32)],
        compiler_params=params(VMEM),
        cost_estimate=cost(1e9, 5e6),
        name="up_level",
    )(place, received, box, skip_keep, skip_send)


def fill_coarse_taps(odd, rows, taps):
    wide, c4 = rows[0].shape

    def fill(order):
        for v, row in zip(order, rows):
            before, after = shifted(row.astype(F32))
            lines = slice(v * wide, (v + 1) * wide)
            taps[lines, :c4] = before.astype(BF16)
            taps[lines, c4 : 2 * c4] = row
            taps[lines, 2 * c4 :] = after.astype(BF16)

    pl.when(odd)(lambda: fill((3, 2, 1, 0)))
    pl.when(jnp.logical_not(odd))(lambda: fill((0, 1, 2, 3)))


def coarse_weight_kernel(
    place_ref, input_ref, first_ref, second_ref, third_ref, fourth_ref, out_ref, taps, total, *, scale
):
    sample = pl.program_id(0)
    wide = input_ref.shape[-1]
    part = input_ref.shape[0] * input_ref.shape[-2]
    c4 = first_ref.shape[-1]

    @pl.when(sample == 0)
    def _():
        total[...] = jnp.zeros_like(total)

    rows = (first_ref[0], second_ref[0], third_ref[0], fourth_ref[0])
    fill_coarse_taps(place_ref[0] >= 2, rows, taps)
    values = jnp.concatenate([input_ref[:, 0, 0, i].reshape(part, wide) for i in range(2)], axis=1)
    for dy in range(3):
        total[dy] += jnp.dot(values, taps[dy * wide : (dy + 2) * wide, :], preferred_element_type=F32)

    @pl.when(sample == pl.num_programs(0) - 1)
    def _():
        count = part // 16
        for dy in range(3):
            for d in range(3):
                for side in range(c4 // 128):
                    at = d * c4 + side * 128
                    tap = ((2 - dy) * 3 + 2 - d) * (c4 // 128) + side
                    out_ref[tap * count : (tap + 1) * count] = tiles(total[dy, :, at : at + 128] * scale)


def coarse_specs(wide, c4, count):
    return [pl.BlockSpec((1, wide, c4), lambda s: (s, 0, 0))] * count


def coarse_weight_level(place, received, rows, coarse_cells):
    peers, _, samples, _, own, wide = received.shape
    c4 = peers * own
    shape = (9 * (c4 // 128) * (c4 // 32), 16, 128)
    return pl.pallas_call(
        functools.partial(coarse_weight_kernel, scale=1.0 / math.sqrt(coarse_cells)),
        grid_spec=pltpu.PrefetchScalarGridSpec(
            num_scalar_prefetch=1,
            grid=(samples,),
            in_specs=[pl.BlockSpec((peers // 2, 1, 1, 2, own, wide), lambda s, place: (place[0] % 2, 1, s, 0, 0, 0))]
            + [pl.BlockSpec((1, wide, c4), lambda s, place: (s, 0, 0))] * 4,
            out_specs=pl.BlockSpec(shape, lambda s, place: (0, 0, 0)),
            scratch_shapes=[pltpu.VMEM((4 * wide, 3 * c4), BF16), pltpu.VMEM((3, c4 // 2, 3 * c4), F32)],
        ),
        out_shape=jax.ShapeDtypeStruct(shape, BF16),
        compiler_params=params(VMEM),
        cost_estimate=cost(0.7e9, 2e6),
        name="coarse_weight_level",
    )(place, received, *rows)


def coarse_input_kernel(chan_ref, weight_ref, first_ref, second_ref, third_ref, fourth_ref, *rest):
    *piece_refs, taps, stage = rest
    wide, c4 = first_ref.shape[1:]
    own = c4 // len(piece_refs)
    rows = (first_ref[0], second_ref[0], third_ref[0], fourth_ref[0])
    fill_coarse_taps(chan_ref[0] % 2 == 1, rows, taps)
    total = None
    for dy in range(3):
        for d in range(3):
            window = taps[dy * wide : (dy + 2) * wide, d * c4 : (d + 1) * c4]
            term = dott(weight_ref[2 - dy, 2 - d], window)
            total = term if total is None else total + term
    stage[...] = total.astype(BF16)
    for k, ref in enumerate(piece_refs):
        at = pl.multiple_of(jnp.bitwise_xor(chan_ref[0], k) * own, own)
        for i in range(2):
            ref[0, i] = stage[pl.ds(at, own), i * wide : (i + 1) * wide]


def coarse_input_level(chan, weight, rows, peers):
    samples, wide, c4 = rows[0].shape
    own = c4 // peers
    return pl.pallas_call(
        coarse_input_kernel,
        grid=(samples,),
        in_specs=[
            pl.BlockSpec(memory_space=pltpu.SMEM),
            pl.BlockSpec(weight.shape, lambda s: (0, 0, 0, 0)),
        ] + coarse_specs(wide, c4, 4),
        out_specs=[pl.BlockSpec((1, 2, own, wide), lambda s: (s, 0, 0, 0))] * peers,
        out_shape=[jax.ShapeDtypeStruct((samples, 2, own, wide), BF16)] * peers,
        scratch_shapes=[pltpu.VMEM((4 * wide, 3 * c4), BF16), pltpu.VMEM((c4, 2 * wide), BF16)],
        compiler_params=params(VMEM),
        cost_estimate=cost(1.3e9, 3e6),
        name="coarse_input_level",
    )(chan, weight, *rows)


def place_kernel(first, count, chan_ref, *refs):
    out_ref = refs[-1]
    if len(refs) > count + 1:
        out_ref[...] = refs[count][...]
    for k in range(count):
        at = jnp.bitwise_xor(chan_ref[0], first + k) * 2
        out_ref[:, pl.ds(at, 2)] = refs[k][...]


def placed(chan, pieces, first, peers, earlier=(), flops=1e6):
    samples, rows, own, wide = pieces[0].shape
    vmem = pl.BlockSpec(memory_space=pltpu.VMEM)
    return pl.pallas_call(
        functools.partial(place_kernel, first, len(pieces)),
        in_specs=[pl.BlockSpec(memory_space=pltpu.SMEM)] + [vmem] * (len(pieces) + len(earlier)),
        out_shape=jax.ShapeDtypeStruct((samples, rows * peers, own, wide), BF16),
        compiler_params=params(VMEM),
        cost_estimate=cost(flops, 1e6),
        name="place",
    )(chan, *pieces, *earlier)


def join_kernel(coarse_ref, coarse_more_ref, fine_ref, fine_more_ref, out_ref):
    count = coarse_ref.shape[0]
    out_ref[:count] = (coarse_ref[...].astype(F32) + coarse_more_ref[...].astype(F32)).astype(BF16)
    fines = fine_ref.shape[0]
    out_ref[count : count + fines] = (fine_ref[...].astype(F32) + fine_more_ref[...].astype(F32)).astype(BF16)
    rest = out_ref.shape[0] - count - fines
    if rest:
        out_ref[count + fines :] = jnp.zeros((rest,) + out_ref.shape[1:], BF16)


def sum_kernel(parts_ref, out_ref):
    total = parts_ref[0].astype(F32)
    for k in range(1, parts_ref.shape[0]):
        total = total + parts_ref[k].astype(F32)
    total = total.astype(BF16)
    for k in range(out_ref.shape[0]):
        out_ref[k] = total


def unpack_kernel(place_ref, parts_ref, *rest):
    fine_ref, coarse_ref, fine_stage, coarse_stage, sems = rest[-5:]
    c4 = coarse_ref.shape[-1]
    sides = c4 // 128
    lines, skips = c4 // 2, (fine_ref.shape[-2] - c4) // 2
    line_tiles, skip_tiles = lines // 16, skips // 16
    core = place_ref[0] % 2
    rows = pl.ds(pl.multiple_of(core * lines, lines), lines)
    skip_rows = pl.ds(pl.multiple_of(c4 + core * skips, skips), skips)

    def take(at, count):
        return parts_ref[at : at + count].astype(F32).reshape(count * 16, 128)

    copies = []

    def send(source, target):
        copies.append(pltpu.make_async_copy(source, target, sems.at[len(copies)]))
        copies[-1].start()

    for tap in range(9):
        for side in range(sides):
            at = (tap * sides + side) * line_tiles
            coarse_stage[tap, :, side * 128 : (side + 1) * 128] = take(at, line_tiles)
        send(coarse_stage.at[tap], coarse_ref.at[tap, rows])
        at = 9 * sides * line_tiles + tap * (line_tiles + skip_tiles)
        fine_stage[tap, :lines] = take(at, line_tiles)
        fine_stage[tap, lines:] = take(at + line_tiles, skip_tiles)
        send(fine_stage.at[tap, pl.ds(0, lines)], fine_ref.at[tap, rows])
        send(fine_stage.at[tap, pl.ds(lines, skips)], fine_ref.at[tap, skip_rows])
    for copy in copies:
        copy.wait()


SWAP = ((0, 1), (1, 0))


def grad_sums(fine_keep, fine_more, coarse_keep, coarse_more):
    chips = 1
    for axis in CHIPS:
        chips *= lax.axis_size(axis)
    fine_keep, fine_more = (a.reshape((-1, 16, 128)) for a in (fine_keep, fine_more))
    count = coarse_keep.shape[0] + fine_keep.shape[0]
    each = -(-count // chips)
    joined = pl.pallas_call(
        join_kernel,
        out_shape=jax.ShapeDtypeStruct((chips * each, 16, 128), BF16),
        compiler_params=params(VMEM),
        cost_estimate=cost(1e6, 3e6),
        name="join",
    )(coarse_keep, coarse_more, fine_keep, fine_more)
    parts = lax.all_to_all(joined.reshape(chips, each, 16, 128), CHIPS, 0, 0, tiled=True)
    summed = pl.pallas_call(
        sum_kernel,
        out_shape=jax.ShapeDtypeStruct((chips, each, 16, 128), BF16),
        compiler_params=params(VMEM),
        cost_estimate=cost(1e6, 1.3e6),
        name="sum_parts",
    )(parts)
    return lax.all_to_all(summed, CHIPS, 0, 0, tiled=True).reshape(chips * each, 16, 128)


def unpacked(place, half, fine_shape, coarse_shape, earlier=()):
    shapes = [jax.ShapeDtypeStruct((9,) + shape[2:], F32) for shape in (fine_shape, coarse_shape)]
    hbm = pl.BlockSpec(memory_space=pltpu.HBM)
    return pl.pallas_call(
        unpack_kernel,
        in_specs=[pl.BlockSpec(memory_space=pltpu.SMEM), pl.BlockSpec(memory_space=pltpu.VMEM)]
        + [hbm] * len(earlier),
        out_specs=[hbm, hbm],
        out_shape=shapes,
        input_output_aliases={2 + i: i for i in range(len(earlier))},
        scratch_shapes=[
            pltpu.VMEM((9, fine_shape[2] // 2, fine_shape[3]), F32),
            pltpu.VMEM((9, coarse_shape[2] // 2, coarse_shape[3]), F32),
            pltpu.SemaphoreType.DMA((27,)),
        ],
        compiler_params=params(VMEM),
        cost_estimate=cost(1, 1),
        name="unpack",
    )(place, half, *earlier)


def start_kernel(
    place_ref, pre_ref, input_ref, cot_ref, fine_pre_ref, pieces_ref, near_ref, far_ref, rows, row_sems, sems
):
    peers, _, samples, lines, _, _ = pieces_ref.shape
    odd = place_ref[0] >= 2
    last = cot_ref.shape[1] - 1
    row_copies = []
    for a, ref in enumerate((cot_ref, fine_pre_ref)):
        for e, line in enumerate((jnp.where(odd, 0, last), jnp.where(odd, last, 0))):
            for s in range(samples):
                row_copies.append(
                    pltpu.make_async_copy(ref.at[s, line], rows.at[a, e, s], row_sems.at[len(row_copies)])
                )
    copies = []
    for c in range(peers):
        for a, ref in enumerate((pre_ref, input_ref)):
            for s in range(samples):
                copies.append(
                    pltpu.make_async_copy(
                        ref.at[s, pl.ds(c * lines, lines)], pieces_ref.at[c, a, s], sems.at[len(copies)]
                    )
                )
    for copy in row_copies + copies:
        copy.start()
    for copy in row_copies:
        copy.wait()
    for e, out_ref in enumerate((near_ref, far_ref)):
        for s in range(samples):
            grad = rows[0, e, s].astype(F32) * silu_grad(rows[1, e, s].astype(F32))
            out_ref[s] = grad.astype(BF16)
    for copy in copies:
        copy.wait()


def start_level(place, pre, values, cot, fine_pre, peers):
    samples, lines, own, wide = pre.shape
    fine_wide, c3 = cot.shape[2:]
    hbm = pl.BlockSpec(memory_space=pltpu.HBM)
    vmem = pl.BlockSpec(memory_space=pltpu.VMEM)
    edge = jax.ShapeDtypeStruct((samples, fine_wide, c3), BF16)
    return pl.pallas_call(
        start_kernel,
        in_specs=[pl.BlockSpec(memory_space=pltpu.SMEM), hbm, hbm, hbm, hbm],
        out_specs=[vmem, vmem, vmem],
        out_shape=[jax.ShapeDtypeStruct((peers, 2, samples, lines // peers, own, wide), BF16), edge, edge],
        scratch_shapes=[
            pltpu.VMEM((2, 2, samples, fine_wide, c3), BF16),
            pltpu.SemaphoreType.DMA((4 * samples,)),
            pltpu.SemaphoreType.DMA((peers * 2 * samples,)),
        ],
        compiler_params=params(VMEM),
        cost_estimate=cost(1e7, 3e6),
        name="start",
    )(place, *(in_hbm(a) for a in (pre, values, cot, fine_pre)))


def swapped(near, far):
    count = 1
    for axis in ALL:
        count *= lax.axis_size(axis)
    inside = [(i, i ^ 1) for i in range(count)]
    outside = [(i, i + 1) for i in range(1, count - 1, 2)]
    outside += [(target, source) for source, target in outside]
    return lax.ppermute(near, ALL, inside), lax.ppermute(far, ALL, outside)


def shards(coarse_input, coarse_pre, skip_feats, fine_pre, fine_cotangent, fine_weight, coarse_weight):
    peers = 1
    for axis in CHAN:
        peers *= lax.axis_size(axis)
    devices = peers
    for axis in ROWS:
        devices *= lax.axis_size(axis)
    samples, lines, wide, own = coarse_input.shape
    core = lax.axis_index("core").astype(jnp.int32)
    chan = lax.axis_index(CHAN).astype(jnp.int32).reshape(1)
    place = (core + 2 * (lax.axis_index("xl").astype(jnp.int32))).reshape(1)
    other_place = (1 - core + 2 * (lax.axis_index("xl").astype(jnp.int32))).reshape(1)

    pieces, edge_near, edge_far = start_level(
        place, coarse_pre.transpose(0, 1, 3, 2), coarse_input.transpose(0, 1, 3, 2), fine_cotangent, fine_pre, peers
    )
    edge_near, edge_far = swapped(edge_near, edge_far)
    received = lax.all_to_all(pieces, CHAN, 0, 0, tiled=True)

    cs = skip_feats.shape[-1]
    fine_cells = fine_pre.shape[0] * fine_pre.shape[1] * fine_pre.shape[2] * devices
    edge_near, edge_far, cotangent = lax.optimization_barrier((edge_near, edge_far, fine_cotangent))
    fine_grad, pooled, box = box_level(place, cotangent, fine_pre, edge_near, edge_far, fine_weight, cs)
    near, far = coarse_grad(place, pooled, received)
    from_near, from_far = swapped(near, far)
    fine_grad, near = lax.optimization_barrier((fine_grad, near))
    grad_skip, skip_keep, skip_send = fine_level(place, fine_grad, skip_feats, fine_weight, fine_cells)
    fine_keep, fine_send = up_level(place, received, box, skip_keep, skip_send, fine_cells)
    fine_more = lax.ppermute(fine_send, "core", SWAP)
    from_near, from_far, fine_keep = lax.optimization_barrier((from_near, from_far, fine_keep))
    rows = (from_far, far, near, from_near)
    coarse_cells = samples * (lines // peers) * wide * devices
    coarse_send = coarse_weight_level(other_place, received, rows, coarse_cells)
    coarse_more = lax.ppermute(coarse_send, "core", SWAP)
    coarse_keep = coarse_weight_level(place, received, rows, coarse_cells)
    back = coarse_input_level(chan, coarse_weight, rows, peers)

    def home(k, piece):
        return lax.ppermute(piece, CHAN, [(i, i ^ k) for i in range(peers)])

    mine = grad_sums(fine_keep, fine_more, coarse_keep, coarse_more)
    early = [back[0]] + [home(k, back[k]) for k in range(1, EARLY)]
    grad_input = placed(chan, early, 0, peers, flops=LONG)
    grad_input, *late = lax.optimization_barrier((grad_input, *back[EARLY:]))
    late = [home(EARLY + k, piece) for k, piece in enumerate(late)]
    mine, grad_input = lax.optimization_barrier((mine, grad_input))
    grad_input = placed(chan, late, EARLY, peers, (grad_input,), flops=LONG)
    other = lax.ppermute(mine, "core", SWAP)
    sums = unpacked(place, mine, fine_weight.shape, coarse_weight.shape)
    grad_fine, grad_coarse = unpacked(other_place, other, fine_weight.shape, coarse_weight.shape, sums)
    return (
        grad_skip,
        grad_input.transpose(0, 1, 3, 2),
        grad_fine.reshape(fine_weight.shape),
        grad_coarse.reshape(coarse_weight.shape),
    )


def solution(mesh):
    split = Mesh(mesh.devices.reshape([size for _, size in SPLIT]), tuple(name for name, _ in SPLIT))
    coarse = P(None, ROWS, None, CHAN)
    fine = P(None, ALL, None, None)
    return jax.shard_map(
        shards,
        mesh=split,
        in_specs=(coarse, coarse, fine, fine, fine, P(), P()),
        out_specs=(fine, coarse, P(), P()),
        check_vma=False,
    )
```

```python
import functools
import math

import jax
import jax.numpy as jnp
from jax import lax
from jax.experimental import pallas as pl
from jax.experimental.pallas import tpu as pltpu
from jax.sharding import Mesh
from jax.sharding import PartitionSpec as P

F32 = jnp.float32
BF16 = jnp.bfloat16
MIB = 1 << 20
VMEM = 18
EARLY = 6
LONG = 1e11

SPLIT = (("xh", 2), ("z", 4), ("core", 2), ("y", 4), ("xl", 2))
ROWS = ("xh", "z", "core")
CHAN = ("y", "xl")
ALL = ROWS + CHAN
CHIPS = ("xh", "z", "y", "xl")


def params(limit):
    return pltpu.CompilerParams(vmem_limit_bytes=limit * MIB)


def cost(flops, nbytes):
    return pl.CostEstimate(flops=int(flops), bytes_accessed=int(nbytes), transcendentals=0)


def in_hbm(array):
    return pltpu.with_memory_space_constraint(array, pltpu.HBM)


def silu_grad(value):
    sigma = jax.nn.sigmoid(value)
    return sigma * (1.0 + value * (1.0 - sigma))


def shifted(field):
    extent = field.shape[0]
    index = lax.broadcasted_iota(jnp.int32, field.shape, 0)
    before = jnp.where(index == 0, 0.0, pltpu.roll(field, 1, 0))
    after = jnp.where(index == extent - 1, 0.0, pltpu.roll(field, extent - 1, 0))
    return before, after


def tdot(left, right):
    return lax.dot_general(left, right, (((0,), (0,)), ((), ())), preferred_element_type=F32)


def dott(left, right):
    return lax.dot_general(left, right, (((1,), (1,)), ((), ())), preferred_element_type=F32)


def tiles(block):
    return block.astype(BF16).reshape(block.shape[0] // 16, 16, block.shape[1])


def box_sums(upper, lower, half):
    even = upper[pl.ds(0, half, 2), :] + lower[pl.ds(0, half, 2), :]
    odd = upper[pl.ds(1, half, 2), :] + lower[pl.ds(1, half, 2), :]
    before, _ = shifted(odd)
    _, after = shifted(even)
    return (before + even).astype(BF16), (even + odd).astype(BF16), (odd + after).astype(BF16)


def box_kernel(cot_ref, pre_ref, weight_ref, grad_ref, box_ref, edge_ref, pooled_ref, up_weight, rows32):
    c3 = cot_ref.shape[-1]
    half = pooled_ref.shape[-2]
    reach = 3 * c3

    @pl.when(pl.program_id(0) == 0)
    def _():
        for dy in range(3):
            for d in range(3):
                at = (dy * 3 + d) * c3
                up_weight[at : at + c3, :] = weight_ref[2 - dy, 2 - d].astype(F32).T.astype(BF16)

    for v in range(4):
        grad = (cot_ref[0, v].astype(F32) * silu_grad(pre_ref[0, v].astype(F32))).astype(BF16)
        grad_ref[0, v] = grad
        rows32[v] = grad.astype(F32)
        if v % 3 == 0:
            edge_ref[0, v // 3] = grad
    for v in range(3):
        for d, value in enumerate(box_sums(rows32.at[v], rows32.at[v + 1], half)):
            at = v * reach + d * c3
            box_ref[0, :, at : at + c3] = value
    pooled_ref[0, 0] = jnp.dot(box_ref[0, :, : 2 * reach], up_weight[reach:, :], preferred_element_type=F32)
    pooled_ref[0, 1] = jnp.dot(box_ref[0, :, reach:], up_weight[: 2 * reach, :], preferred_element_type=F32)


def box_level(cot, pre, weight, cs):
    samples, height, wide, c3 = cot.shape
    c4 = weight.shape[2] - cs
    half = wide // 2
    block = pl.BlockSpec((1, height, wide, c3), lambda s: (s, 0, 0, 0))
    return pl.pallas_call(
        box_kernel,
        grid=(samples,),
        in_specs=[block, block, pl.BlockSpec((3, 3, c4, c3), lambda s: (0, 0, 0, 0))],
        out_specs=[
            block,
            pl.BlockSpec((1, half, 9 * c3), lambda s: (s, 0, 0)),
            pl.BlockSpec((1, 2, wide, c3), lambda s: (s, 0, 0, 0)),
            pl.BlockSpec((1, 2, half, c4), lambda s: (s, 0, 0, 0)),
            pl.BlockSpec((9 * c3, c4), lambda s: (0, 0)),
        ],
        out_shape=[
            pltpu.HBM((samples, height, wide, c3), BF16),
            pltpu.HBM((samples, half, 9 * c3), BF16),
            jax.ShapeDtypeStruct((samples, 2, wide, c3), BF16),
            jax.ShapeDtypeStruct((samples, 2, half, c4), F32),
            jax.ShapeDtypeStruct((9 * c3, c4), BF16),
        ],
        scratch_shapes=[pltpu.VMEM((height, wide, c3), F32)],
        compiler_params=params(VMEM),
        cost_estimate=cost(1.2e9, 8e6),
        name="box_level",
    )(in_hbm(cot), in_hbm(pre), in_hbm(weight))


def edge_kernel(
    place_ref, near_ref, far_ref, edge_ref, pooled_ref, low_weight_ref, high_weight_ref,
    out_ref, box_low_ref, box_high_ref, rows32,
):
    half = pooled_ref.shape[-2]
    c3 = edge_ref.shape[-1]
    odd = place_ref[0] >= 2
    near, far = near_ref[0].astype(F32), far_ref[0].astype(F32)
    sides = (
        (jnp.where(odd, near, far), edge_ref[0, 0].astype(F32), low_weight_ref, box_low_ref),
        (edge_ref[0, 1].astype(F32), jnp.where(odd, far, near), high_weight_ref, box_high_ref),
    )
    for i, (upper, lower, weight_ref, box_ref) in enumerate(sides):
        rows32[0] = upper
        rows32[1] = lower
        for d, value in enumerate(box_sums(rows32.at[0], rows32.at[1], half)):
            box_ref[0, :, d * c3 : (d + 1) * c3] = value
        out_ref[0, i] = pooled_ref[0, i] + jnp.dot(box_ref[0], weight_ref[...], preferred_element_type=F32)


def edge_level(place, near, far, edge, pooled, up_weight):
    samples, _, half, c4 = pooled.shape
    _, _, wide, c3 = edge.shape
    row = pl.BlockSpec((1, wide, c3), lambda s: (s, 0, 0))
    whole = pl.BlockSpec((1, 2, half, c4), lambda s: (s, 0, 0, 0))
    box_spec = pl.BlockSpec((1, half, 3 * c3), lambda s: (s, 0, 0))
    box = pltpu.HBM((samples, half, 3 * c3), BF16)
    return pl.pallas_call(
        edge_kernel,
        grid=(samples,),
        in_specs=[
            pl.BlockSpec(memory_space=pltpu.SMEM), row, row,
            pl.BlockSpec((1, 2, wide, c3), lambda s: (s, 0, 0, 0)), whole,
            pl.BlockSpec((3 * c3, c4), lambda s: (0, 0)),
            pl.BlockSpec((3 * c3, c4), lambda s: (2, 0)),
        ],
        out_specs=[whole, box_spec, box_spec],
        out_shape=[pltpu.HBM((samples, 2, half, c4), F32), box, box],
        scratch_shapes=[pltpu.VMEM((2, wide, c3), F32)],
        compiler_params=params(VMEM),
        cost_estimate=cost(LONG, 4e6),
        name="edge_level",
    )(place, in_hbm(near), in_hbm(far), edge, pooled, up_weight, up_weight)


def fine_kernel(
    place_ref, grad_ref, near_ref, far_ref, skip_ref, weight_ref, grad_skip_ref, keep_ref, send_ref, taps, skip_weight, total, *, scale
):
    sample = pl.program_id(0)
    odd = place_ref[0] >= 2
    c3 = grad_ref.shape[-1]
    cs = skip_ref.shape[-1]
    c4 = weight_ref.shape[2] - cs

    @pl.when(sample == 0)
    def _():
        total[...] = jnp.zeros_like(total)
        for u in range(4):
            for d in range(3):
                at = (u * 3 + d) * c3
                for t in range(2):
                    dy = u - t
                    if 0 <= dy <= 2:
                        block = weight_ref[2 - dy, 2 - d, c4:, :].astype(F32).T.astype(BF16)
                    else:
                        block = jnp.zeros((c3, cs), BF16)
                    skip_weight[at : at + c3, t * cs : (t + 1) * cs] = block

    for v in range(6):
        if v == 0:
            grad = jnp.where(odd, near_ref[0], far_ref[0])
        elif v == 5:
            grad = jnp.where(odd, far_ref[0], near_ref[0])
        else:
            grad = grad_ref[0, v - 1]
        before, after = shifted(grad.astype(F32))
        at = v * 3 * c3
        taps[:, at : at + c3] = before.astype(BF16)
        taps[:, at + c3 : at + 2 * c3] = grad
        taps[:, at + 2 * c3 : at + 3 * c3] = after.astype(BF16)

    for pair in range(2):
        window = taps[:, 2 * pair * 3 * c3 : (2 * pair + 4) * 3 * c3]
        back = jnp.dot(window, skip_weight[...], preferred_element_type=F32)
        grad_skip_ref[0, 2 * pair] = back[:, :cs].astype(BF16)
        grad_skip_ref[0, 2 * pair + 1] = back[:, cs:].astype(BF16)
        feats = jnp.concatenate([skip_ref[0, 2 * pair], skip_ref[0, 2 * pair + 1]], axis=1)
        total[...] += tdot(feats, window)

    @pl.when(sample == pl.num_programs(0) - 1)
    def _():
        core = place_ref[0] % 2

        part = cs // 2
        for dy in range(3):
            for d in range(3):
                first = (dy * 3 + d) * c3
                second = ((dy + 1) * 3 + d) * c3
                value = (total[:cs, first : first + c3] + total[cs:, second : second + c3]) * scale
                low, high = value[:part], value[part:]
                tap = (2 - dy) * 3 + 2 - d
                keep_ref[tap] = tiles(jnp.where(core == 0, low, high))
                send_ref[tap] = tiles(jnp.where(core == 0, high, low))


def fine_level(place, grad, near, far, skip, weight, fine_cells):
    samples, height, wide, cs = skip.shape
    c3 = grad.shape[-1]
    part = jax.ShapeDtypeStruct((9, cs // 32, 16, c3), BF16)
    whole = pl.BlockSpec(part.shape, lambda s: (0, 0, 0, 0))
    return pl.pallas_call(
        functools.partial(fine_kernel, scale=1.0 / math.sqrt(fine_cells)),
        grid=(samples,),
        in_specs=[
            pl.BlockSpec(memory_space=pltpu.SMEM),
            pl.BlockSpec((1, height, wide, c3), lambda s: (s, 0, 0, 0)),
            pl.BlockSpec((1, wide, c3), lambda s: (s, 0, 0)),
            pl.BlockSpec((1, wide, c3), lambda s: (s, 0, 0)),
            pl.BlockSpec((1, height, wide, cs), lambda s: (s, 0, 0, 0)),
            pl.BlockSpec(weight.shape, lambda s: (0, 0, 0, 0)),
        ],
        out_specs=[pl.BlockSpec((1, height, wide, cs), lambda s: (s, 0, 0, 0)), whole, whole],
        out_shape=[jax.ShapeDtypeStruct((samples, height, wide, cs), BF16), part, part],
        scratch_shapes=[
            pltpu.VMEM((wide, 18 * c3), BF16),
            pltpu.VMEM((12 * c3, 2 * cs), BF16),
            pltpu.VMEM((2 * cs, 12 * c3), F32),
        ],
        compiler_params=params(VMEM),
        cost_estimate=cost(5e9, 8e6),
        name="fine_level",
    )(place, *(in_hbm(a) for a in (grad, near, far, skip, weight)))


def coarse_grad_kernel(place_ref, pooled_ref, pre_ref, near_ref, far_ref):
    channels, half = pooled_ref.shape[-1], pooled_ref.shape[-2]
    odd = place_ref[0] >= 2
    rows = []
    for i in range(2):
        value = pre_ref[:, 0, 0, i].reshape(channels, half).astype(F32).T
        rows.append((pooled_ref[0, i] * silu_grad(value)).astype(BF16))
    near_ref[0] = jnp.where(odd, rows[0], rows[1])
    far_ref[0] = jnp.where(odd, rows[1], rows[0])


def coarse_grad(place, pooled, received):
    samples, _, half, c4 = pooled.shape
    peers, _, _, _, own, _ = received.shape
    out = jax.ShapeDtypeStruct((samples, half, c4), BF16)
    spec = pl.BlockSpec((1, half, c4), lambda s: (s, 0, 0))
    return pl.pallas_call(
        coarse_grad_kernel,
        grid=(samples,),
        in_specs=[
            pl.BlockSpec(memory_space=pltpu.SMEM),
            pl.BlockSpec((1, 2, half, c4), lambda s: (s, 0, 0, 0)),
            pl.BlockSpec((peers, 1, 1, 2, own, half), lambda s: (0, 0, s, 0, 0, 0)),
        ],
        out_specs=[spec, spec],
        out_shape=[out, out],
        compiler_params=params(VMEM),
        cost_estimate=cost(2e7, 2e6),
        name="coarse_grad",
    )(place, in_hbm(pooled), received)


def up_kernel(
    place_ref, pre_ref, box_ref, box_low_ref, box_high_ref, skip_keep_ref, skip_send_ref, keep_ref, send_ref, total,
    *, scale
):
    sample = pl.program_id(0)
    wide = pre_ref.shape[-1]
    c4 = pre_ref.shape[0] * pre_ref.shape[-2]
    c3 = keep_ref.shape[-1]

    @pl.when(sample == 0)
    def _():
        total[...] = jnp.zeros_like(total)

    reach = 3 * c3
    windows = (
        ((0, box_low_ref[0]), (reach, box_ref[0, :, : 2 * reach])),
        ((0, box_ref[0, :, reach:]), (2 * reach, box_high_ref[0])),
    )
    for i in range(2):
        value = pre_ref[:, 0, 0, i].reshape(c4, wide).astype(F32)
        value = (value * jax.nn.sigmoid(value)).astype(BF16)
        for at, window in windows[i]:
            total[:, at : at + window.shape[1]] += jnp.dot(value, window, preferred_element_type=F32)

    @pl.when(sample == pl.num_programs(0) - 1)
    def _():
        core = place_ref[0] % 2
        part = c4 // 2
        mine = part // 16
        for dy in range(3):
            for d in range(3):
                at = (dy * 3 + d) * c3
                value = total[:, at : at + c3] * scale
                low, high = value[:part], value[part:]
                tap = (2 - dy) * 3 + 2 - d
                keep_ref[tap, :mine] = tiles(jnp.where(core == 0, low, high))
                send_ref[tap, :mine] = tiles(jnp.where(core == 0, high, low))
                keep_ref[tap, mine:] = skip_keep_ref[tap]
                send_ref[tap, mine:] = skip_send_ref[tap]


def up_level(place, received, box, box_low, box_high, skip_keep, skip_send, fine_cells):
    peers, _, samples, _, own, wide = received.shape
    c4 = peers * own
    c3 = box.shape[-1] // 9
    part = jax.ShapeDtypeStruct((9, c4 // 32 + skip_keep.shape[1], 16, c3), BF16)
    whole = pl.BlockSpec(part.shape, lambda s: (0, 0, 0, 0))
    skips = pl.BlockSpec(skip_keep.shape, lambda s: (0, 0, 0, 0))
    return pl.pallas_call(
        functools.partial(up_kernel, scale=1.0 / math.sqrt(fine_cells)),
        grid=(samples,),
        in_specs=[
            pl.BlockSpec(memory_space=pltpu.SMEM),
            pl.BlockSpec((peers, 1, 1, 2, own, wide), lambda s: (0, 0, s, 0, 0, 0)),
            pl.BlockSpec((1, wide, 9 * c3), lambda s: (s, 0, 0)),
            pl.BlockSpec((1, wide, 3 * c3), lambda s: (s, 0, 0)),
            pl.BlockSpec((1, wide, 3 * c3), lambda s: (s, 0, 0)),
            skips, skips,
        ],
        out_specs=[whole, whole],
        out_shape=[part, part],
        scratch_shapes=[pltpu.VMEM((c4, 9 * c3), F32)],
        compiler_params=params(VMEM),
        cost_estimate=cost(1e9, 5e6),
        name="up_level",
    )(place, received, box, box_low, box_high, skip_keep, skip_send)


def fill_coarse_taps(odd, rows, taps):
    wide, c4 = rows[0].shape

    def fill(order):
        for v, row in zip(order, rows):
            before, after = shifted(row.astype(F32))
            lines = slice(v * wide, (v + 1) * wide)
            taps[lines, :c4] = before.astype(BF16)
            taps[lines, c4 : 2 * c4] = row
            taps[lines, 2 * c4 :] = after.astype(BF16)

    count = len(rows)
    pl.when(odd)(lambda: fill(range(count - 1, -1, -1)))
    pl.when(jnp.logical_not(odd))(lambda: fill(range(count)))


def dot32(left, right):
    return jnp.dot(left, right, preferred_element_type=F32)


def own_weight_kernel(place_ref, input_ref, far_ref, near_ref, out_ref, taps):
    wide = input_ref.shape[-1]
    c4 = far_ref.shape[-1]

    @pl.when(pl.program_id(0) == 0)
    def _():
        out_ref[...] = jnp.zeros_like(out_ref)

    fill_coarse_taps(place_ref[0] >= 2, (far_ref[0], near_ref[0]), taps)
    first, second = (input_ref[:, 0, 0, i].reshape(c4, wide) for i in range(2))
    out_ref[0] += dot32(second, taps[:wide, :])
    out_ref[1] += dot32(jnp.concatenate([first, second], axis=1), taps[...])
    out_ref[2] += dot32(first, taps[wide:, :])


def own_weight_level(place, received, far, near):
    peers, _, samples, _, own, wide = received.shape
    c4 = peers * own
    row = pl.BlockSpec((1, wide, c4), lambda s: (s, 0, 0))
    return pl.pallas_call(
        own_weight_kernel,
        grid=(samples,),
        in_specs=[
            pl.BlockSpec(memory_space=pltpu.SMEM),
            pl.BlockSpec((peers, 1, 1, 2, own, wide), lambda s: (0, 1, s, 0, 0, 0)),
            row, row,
        ],
        out_specs=pl.BlockSpec((3, c4, 3 * c4), lambda s: (0, 0, 0)),
        out_shape=jax.ShapeDtypeStruct((3, c4, 3 * c4), F32),
        scratch_shapes=[pltpu.VMEM((2 * wide, 3 * c4), BF16)],
        compiler_params=params(VMEM),
        cost_estimate=cost(9e8, 4e6),
        name="own_weight_level",
    )(place, received, far, near)


def coarse_weight_kernel(place_ref, input_ref, from_far_ref, from_near_ref, own_ref, out_ref, taps, total, *, scale):
    sample = pl.program_id(0)
    wide = input_ref.shape[-1]
    part = input_ref.shape[0] * input_ref.shape[-2]
    c4 = from_far_ref.shape[-1]

    fill_coarse_taps(place_ref[0] >= 2, (from_far_ref[0], from_near_ref[0]), taps)
    terms = [dot32(input_ref[:, 0, 0, i].reshape(part, wide), taps[i * wide : (i + 1) * wide, :]) for i in range(2)]

    @pl.when(sample == 0)
    def _():
        for i, term in enumerate(terms):
            total[i] = term

    @pl.when(sample > 0)
    def _():
        for i, term in enumerate(terms):
            total[i] += term

    @pl.when(sample == pl.num_programs(0) - 1)
    def _():
        count = part // 16
        for dy in range(3):
            for d in range(3):
                for side in range(c4 // 128):
                    at = d * c4 + side * 128
                    value = own_ref[dy, :, at : at + 128]
                    if dy != 1:
                        value = value + total[dy // 2, :, at : at + 128]
                    tap = ((2 - dy) * 3 + 2 - d) * (c4 // 128) + side
                    out_ref[tap * count : (tap + 1) * count] = tiles(value * scale)


def coarse_weight_level(place, received, from_far, from_near, own_terms, coarse_cells):
    peers, _, samples, _, own, wide = received.shape
    c4 = peers * own
    shape = (9 * (c4 // 128) * (c4 // 32), 16, 128)
    row = pl.BlockSpec((1, wide, c4), lambda s, place: (s, 0, 0))
    return pl.pallas_call(
        functools.partial(coarse_weight_kernel, scale=1.0 / math.sqrt(coarse_cells)),
        grid_spec=pltpu.PrefetchScalarGridSpec(
            num_scalar_prefetch=1,
            grid=(samples,),
            in_specs=[
                pl.BlockSpec((peers // 2, 1, 1, 2, own, wide), lambda s, place: (place[0] % 2, 1, s, 0, 0, 0)),
                row, row,
                pl.BlockSpec((3, c4 // 2, 3 * c4), lambda s, place: (0, place[0] % 2, 0)),
            ],
            out_specs=pl.BlockSpec(shape, lambda s, place: (0, 0, 0)),
            scratch_shapes=[pltpu.VMEM((2 * wide, 3 * c4), BF16), pltpu.VMEM((2, c4 // 2, 3 * c4), F32)],
        ),
        out_shape=jax.ShapeDtypeStruct(shape, BF16),
        compiler_params=params(VMEM),
        cost_estimate=cost(0.4e9, 2e6),
        name="coarse_weight_level",
    )(place, received, from_far, from_near, own_terms)


def coarse_specs(wide, c4, count):
    return [pl.BlockSpec((1, wide, c4), lambda s: (s, 0, 0))] * count


def coarse_input_kernel(chan_ref, weight_ref, first_ref, second_ref, third_ref, fourth_ref, *rest):
    *piece_refs, taps, stage = rest
    wide, c4 = first_ref.shape[1:]
    own = c4 // len(piece_refs)
    rows = (first_ref[0], second_ref[0], third_ref[0], fourth_ref[0])
    fill_coarse_taps(chan_ref[0] % 2 == 1, rows, taps)
    total = None
    for dy in range(3):
        for d in range(3):
            window = taps[dy * wide : (dy + 2) * wide, d * c4 : (d + 1) * c4]
            term = dott(weight_ref[2 - dy, 2 - d], window)
            total = term if total is None else total + term
    stage[...] = total.astype(BF16)
    for k, ref in enumerate(piece_refs):
        at = pl.multiple_of(jnp.bitwise_xor(chan_ref[0], k) * own, own)
        for i in range(2):
            ref[0, i] = stage[pl.ds(at, own), i * wide : (i + 1) * wide]


def coarse_input_level(chan, weight, rows, peers):
    samples, wide, c4 = rows[0].shape
    own = c4 // peers
    return pl.pallas_call(
        coarse_input_kernel,
        grid=(samples,),
        in_specs=[
            pl.BlockSpec(memory_space=pltpu.SMEM),
            pl.BlockSpec(weight.shape, lambda s: (0, 0, 0, 0)),
        ] + coarse_specs(wide, c4, 4),
        out_specs=[pl.BlockSpec((1, 2, own, wide), lambda s: (s, 0, 0, 0))] * peers,
        out_shape=[jax.ShapeDtypeStruct((samples, 2, own, wide), BF16)] * peers,
        scratch_shapes=[pltpu.VMEM((4 * wide, 3 * c4), BF16), pltpu.VMEM((c4, 2 * wide), BF16)],
        compiler_params=params(VMEM),
        cost_estimate=cost(1.3e9, 3e6),
        name="coarse_input_level",
    )(chan, weight, *rows)


def place_kernel(first, count, chan_ref, *refs):
    out_ref = refs[-1]
    if len(refs) > count + 1:
        out_ref[...] = refs[count][...]
    for k in range(count):
        at = jnp.bitwise_xor(chan_ref[0], first + k) * 2
        out_ref[:, pl.ds(at, 2)] = refs[k][...]


def placed(chan, pieces, first, peers, earlier=(), flops=1e6):
    samples, rows, own, wide = pieces[0].shape
    vmem = pl.BlockSpec(memory_space=pltpu.VMEM)
    return pl.pallas_call(
        functools.partial(place_kernel, first, len(pieces)),
        in_specs=[pl.BlockSpec(memory_space=pltpu.SMEM)] + [vmem] * (len(pieces) + len(earlier)),
        out_shape=jax.ShapeDtypeStruct((samples, rows * peers, own, wide), BF16),
        compiler_params=params(VMEM),
        cost_estimate=cost(flops, 1e6),
        name="place",
    )(chan, *pieces, *earlier)


def join_kernel(coarse_ref, coarse_more_ref, fine_ref, fine_more_ref, out_ref):
    count = coarse_ref.shape[0]
    out_ref[:count] = (coarse_ref[...].astype(F32) + coarse_more_ref[...].astype(F32)).astype(BF16)
    fines = fine_ref.shape[0]
    out_ref[count : count + fines] = (fine_ref[...].astype(F32) + fine_more_ref[...].astype(F32)).astype(BF16)
    rest = out_ref.shape[0] - count - fines
    if rest:
        out_ref[count + fines :] = jnp.zeros((rest,) + out_ref.shape[1:], BF16)


def sum_kernel(parts_ref, out_ref):
    total = parts_ref[0].astype(F32)
    for k in range(1, parts_ref.shape[0]):
        total = total + parts_ref[k].astype(F32)
    total = total.astype(BF16)
    for k in range(out_ref.shape[0]):
        out_ref[k] = total


def unpack_kernel(place_ref, parts_ref, *rest):
    fine_ref, coarse_ref, fine_stage, coarse_stage, sems = rest[-5:]
    c4 = coarse_ref.shape[-1]
    sides = c4 // 128
    lines, skips = c4 // 2, (fine_ref.shape[-2] - c4) // 2
    line_tiles, skip_tiles = lines // 16, skips // 16
    core = place_ref[0] % 2
    rows = pl.ds(pl.multiple_of(core * lines, lines), lines)
    skip_rows = pl.ds(pl.multiple_of(c4 + core * skips, skips), skips)

    def take(at, count):
        return parts_ref[at : at + count].astype(F32).reshape(count * 16, 128)

    copies = []

    def send(source, target):
        copies.append(pltpu.make_async_copy(source, target, sems.at[len(copies)]))
        copies[-1].start()

    for tap in range(9):
        for side in range(sides):
            at = (tap * sides + side) * line_tiles
            coarse_stage[tap, :, side * 128 : (side + 1) * 128] = take(at, line_tiles)
        send(coarse_stage.at[tap], coarse_ref.at[tap, rows])
        at = 9 * sides * line_tiles + tap * (line_tiles + skip_tiles)
        fine_stage[tap, :lines] = take(at, line_tiles)
        fine_stage[tap, lines:] = take(at + line_tiles, skip_tiles)
        send(fine_stage.at[tap, pl.ds(0, lines)], fine_ref.at[tap, rows])
        send(fine_stage.at[tap, pl.ds(lines, skips)], fine_ref.at[tap, skip_rows])
    for copy in copies:
        copy.wait()


SWAP = ((0, 1), (1, 0))


def grad_sums(fine_keep, fine_more, coarse_keep, coarse_more):
    chips = 1
    for axis in CHIPS:
        chips *= lax.axis_size(axis)
    fine_keep, fine_more = (a.reshape((-1, 16, 128)) for a in (fine_keep, fine_more))
    count = coarse_keep.shape[0] + fine_keep.shape[0]
    each = -(-count // chips)
    joined = pl.pallas_call(
        join_kernel,
        out_shape=jax.ShapeDtypeStruct((chips * each, 16, 128), BF16),
        compiler_params=params(VMEM),
        cost_estimate=cost(1e6, 3e6),
        name="join",
    )(coarse_keep, coarse_more, fine_keep, fine_more)
    parts = lax.all_to_all(joined.reshape(chips, each, 16, 128), CHIPS, 0, 0, tiled=True)
    summed = pl.pallas_call(
        sum_kernel,
        out_shape=jax.ShapeDtypeStruct((chips, each, 16, 128), BF16),
        compiler_params=params(VMEM),
        cost_estimate=cost(1e6, 1.3e6),
        name="sum_parts",
    )(parts)
    return lax.all_to_all(summed, CHIPS, 0, 0, tiled=True).reshape(chips * each, 16, 128)


def unpacked(place, half, fine_shape, coarse_shape, earlier=()):
    shapes = [jax.ShapeDtypeStruct((9,) + shape[2:], F32) for shape in (fine_shape, coarse_shape)]
    hbm = pl.BlockSpec(memory_space=pltpu.HBM)
    return pl.pallas_call(
        unpack_kernel,
        in_specs=[pl.BlockSpec(memory_space=pltpu.SMEM), pl.BlockSpec(memory_space=pltpu.VMEM)]
        + [hbm] * len(earlier),
        out_specs=[hbm, hbm],
        out_shape=shapes,
        input_output_aliases={2 + i: i for i in range(len(earlier))},
        scratch_shapes=[
            pltpu.VMEM((9, fine_shape[2] // 2, fine_shape[3]), F32),
            pltpu.VMEM((9, coarse_shape[2] // 2, coarse_shape[3]), F32),
            pltpu.SemaphoreType.DMA((27,)),
        ],
        compiler_params=params(VMEM),
        cost_estimate=cost(1, 1),
        name="unpack",
    )(place, half, *earlier)


def start_kernel(
    place_ref, pre_ref, input_ref, cot_ref, fine_pre_ref, pieces_ref, near_ref, far_ref, rows, row_sems, sems
):
    peers, _, samples, lines, _, _ = pieces_ref.shape
    odd = place_ref[0] >= 2
    last = cot_ref.shape[1] - 1
    row_copies = []
    for a, ref in enumerate((cot_ref, fine_pre_ref)):
        for e, line in enumerate((jnp.where(odd, 0, last), jnp.where(odd, last, 0))):
            for s in range(samples):
                row_copies.append(
                    pltpu.make_async_copy(ref.at[s, line], rows.at[a, e, s], row_sems.at[len(row_copies)])
                )
    copies = []
    for c in range(peers):
        for a, ref in enumerate((pre_ref, input_ref)):
            for s in range(samples):
                copies.append(
                    pltpu.make_async_copy(
                        ref.at[s, pl.ds(c * lines, lines)], pieces_ref.at[c, a, s], sems.at[len(copies)]
                    )
                )
    for copy in row_copies + copies:
        copy.start()
    for copy in row_copies:
        copy.wait()
    for e, out_ref in enumerate((near_ref, far_ref)):
        for s in range(samples):
            grad = rows[0, e, s].astype(F32) * silu_grad(rows[1, e, s].astype(F32))
            out_ref[s] = grad.astype(BF16)
    for copy in copies:
        copy.wait()


def start_level(place, pre, values, cot, fine_pre, peers):
    samples, lines, own, wide = pre.shape
    fine_wide, c3 = cot.shape[2:]
    hbm = pl.BlockSpec(memory_space=pltpu.HBM)
    vmem = pl.BlockSpec(memory_space=pltpu.VMEM)
    edge = jax.ShapeDtypeStruct((samples, fine_wide, c3), BF16)
    return pl.pallas_call(
        start_kernel,
        in_specs=[pl.BlockSpec(memory_space=pltpu.SMEM), hbm, hbm, hbm, hbm],
        out_specs=[vmem, vmem, vmem],
        out_shape=[jax.ShapeDtypeStruct((peers, 2, samples, lines // peers, own, wide), BF16), edge, edge],
        scratch_shapes=[
            pltpu.VMEM((2, 2, samples, fine_wide, c3), BF16),
            pltpu.SemaphoreType.DMA((4 * samples,)),
            pltpu.SemaphoreType.DMA((peers * 2 * samples,)),
        ],
        compiler_params=params(VMEM),
        cost_estimate=cost(1e7, 3e6),
        name="start",
    )(place, *(in_hbm(a) for a in (pre, values, cot, fine_pre)))


def swapped(near, far):
    count = 1
    for axis in ALL:
        count *= lax.axis_size(axis)
    inside = [(i, i ^ 1) for i in range(count)]
    outside = [(i, i + 1) for i in range(1, count - 1, 2)]
    outside += [(target, source) for source, target in outside]
    return lax.ppermute(near, ALL, inside), lax.ppermute(far, ALL, outside)


def shards(coarse_input, coarse_pre, skip_feats, fine_pre, fine_cotangent, fine_weight, coarse_weight):
    peers = 1
    for axis in CHAN:
        peers *= lax.axis_size(axis)
    devices = peers
    for axis in ROWS:
        devices *= lax.axis_size(axis)
    samples, lines, wide, own = coarse_input.shape
    core = lax.axis_index("core").astype(jnp.int32)
    chan = lax.axis_index(CHAN).astype(jnp.int32).reshape(1)
    place = (core + 2 * (lax.axis_index("xl").astype(jnp.int32))).reshape(1)
    other_place = (1 - core + 2 * (lax.axis_index("xl").astype(jnp.int32))).reshape(1)

    pieces, edge_near, edge_far = start_level(
        place, coarse_pre.transpose(0, 1, 3, 2), coarse_input.transpose(0, 1, 3, 2), fine_cotangent, fine_pre, peers
    )
    edge_near, edge_far = swapped(edge_near, edge_far)
    received = lax.all_to_all(pieces, CHAN, 0, 0, tiled=True)

    cs = skip_feats.shape[-1]
    fine_cells = fine_pre.shape[0] * fine_pre.shape[1] * fine_pre.shape[2] * devices
    fine_grad, box, edge, pooled, up_weight = box_level(fine_cotangent, fine_pre, fine_weight, cs)
    pooled, box_low, box_high = edge_level(place, edge_near, edge_far, edge, pooled, up_weight)
    grad_skip, skip_keep, skip_send = fine_level(
        place, fine_grad, edge_near, edge_far, skip_feats, fine_weight, fine_cells
    )
    received, skip_keep, skip_send = lax.optimization_barrier((received, skip_keep, skip_send))
    near, far = coarse_grad(place, pooled, received)
    from_near, from_far = swapped(near, far)
    fine_keep, fine_send = up_level(place, received, box, box_low, box_high, skip_keep, skip_send, fine_cells)
    fine_more = lax.ppermute(fine_send, "core", SWAP)
    own_terms = own_weight_level(place, received, far, near)
    from_near, from_far, fine_keep, own_terms = lax.optimization_barrier((from_near, from_far, fine_keep, own_terms))
    rows = (from_far, far, near, from_near)
    coarse_cells = samples * (lines // peers) * wide * devices
    coarse_send = coarse_weight_level(other_place, received, from_far, from_near, own_terms, coarse_cells)
    coarse_more = lax.ppermute(coarse_send, "core", SWAP)
    coarse_keep = coarse_weight_level(place, received, from_far, from_near, own_terms, coarse_cells)
    back = coarse_input_level(chan, coarse_weight, rows, peers)

    def home(k, piece):
        return lax.ppermute(piece, CHAN, [(i, i ^ k) for i in range(peers)])

    mine = grad_sums(fine_keep, fine_more, coarse_keep, coarse_more)
    early = [back[0]] + [home(k, back[k]) for k in range(1, EARLY)]
    grad_input = placed(chan, early, 0, peers, flops=LONG)
    grad_input, *late = lax.optimization_barrier((grad_input, *back[EARLY:]))
    late = [home(EARLY + k, piece) for k, piece in enumerate(late)]
    mine, grad_input = lax.optimization_barrier((mine, grad_input))
    grad_input = placed(chan, late, EARLY, peers, (grad_input,), flops=LONG)
    other = lax.ppermute(mine, "core", SWAP)
    sums = unpacked(place, mine, fine_weight.shape, coarse_weight.shape)
    grad_fine, grad_coarse = unpacked(other_place, other, fine_weight.shape, coarse_weight.shape, sums)
    return (
        grad_skip,
        grad_input.transpose(0, 1, 3, 2),
        grad_fine.reshape(fine_weight.shape),
        grad_coarse.reshape(coarse_weight.shape),
    )


def solution(mesh):
    split = Mesh(mesh.devices.reshape([size for _, size in SPLIT]), tuple(name for name, _ in SPLIT))
    coarse = P(None, ROWS, None, CHAN)
    fine = P(None, ALL, None, None)
    return jax.shard_map(
        shards,
        mesh=split,
        in_specs=(coarse, coarse, fine, fine, fine, P(), P()),
        out_specs=(fine, coarse, P(), P()),
        check_vma=False,
    )
```

```python
import functools
import math

import jax
import jax.numpy as jnp
from jax import lax
from jax.experimental import pallas as pl
from jax.experimental.pallas import tpu as pltpu
from jax.sharding import Mesh
from jax.sharding import PartitionSpec as P

F32 = jnp.float32
BF16 = jnp.bfloat16
MIB = 1 << 20
VMEM = 18
EARLY = 6
LONG = 1e11

SPLIT = (("xh", 2), ("z", 4), ("core", 2), ("y", 4), ("xl", 2))
ROWS = ("xh", "z", "core")
CHAN = ("y", "xl")
ALL = ROWS + CHAN
CHIPS = ("xh", "z", "y", "xl")


def params(limit):
    return pltpu.CompilerParams(vmem_limit_bytes=limit * MIB)


def cost(flops, nbytes):
    return pl.CostEstimate(flops=int(flops), bytes_accessed=int(nbytes), transcendentals=0)


def in_hbm(array):
    return pltpu.with_memory_space_constraint(array, pltpu.HBM)


def silu_grad(value):
    sigma = jax.nn.sigmoid(value)
    return sigma * (1.0 + value * (1.0 - sigma))


def shifted(field):
    extent = field.shape[0]
    index = lax.broadcasted_iota(jnp.int32, field.shape, 0)
    before = jnp.where(index == 0, 0.0, pltpu.roll(field, 1, 0))
    after = jnp.where(index == extent - 1, 0.0, pltpu.roll(field, extent - 1, 0))
    return before, after


def tdot(left, right):
    return lax.dot_general(left, right, (((0,), (0,)), ((), ())), preferred_element_type=F32)


def dott(left, right):
    return lax.dot_general(left, right, (((1,), (1,)), ((), ())), preferred_element_type=F32)


def tiles(block):
    return block.astype(BF16).reshape(block.shape[0] // 16, 16, block.shape[1])


def box_sums(upper, lower, half):
    even = upper[pl.ds(0, half, 2), :] + lower[pl.ds(0, half, 2), :]
    odd = upper[pl.ds(1, half, 2), :] + lower[pl.ds(1, half, 2), :]
    before, _ = shifted(odd)
    _, after = shifted(even)
    return (before + even).astype(BF16), (even + odd).astype(BF16), (odd + after).astype(BF16)


def box_kernel(cot_ref, pre_ref, weight_ref, grad_ref, box_ref, edge_ref, pooled_ref, up_weight, rows32):
    c3 = cot_ref.shape[-1]
    half = pooled_ref.shape[-2]
    reach = 3 * c3

    @pl.when(pl.program_id(0) == 0)
    def _():
        for dy in range(3):
            for d in range(3):
                at = (dy * 3 + d) * c3
                up_weight[at : at + c3, :] = weight_ref[2 - dy, 2 - d].astype(F32).T.astype(BF16)

    for v in range(4):
        grad = (cot_ref[0, v].astype(F32) * silu_grad(pre_ref[0, v].astype(F32))).astype(BF16)
        grad_ref[0, v] = grad
        rows32[v] = grad.astype(F32)
        if v % 3 == 0:
            edge_ref[0, v // 3] = grad
    for v in range(3):
        for d, value in enumerate(box_sums(rows32.at[v], rows32.at[v + 1], half)):
            at = v * reach + d * c3
            box_ref[0, :, at : at + c3] = value
    pooled_ref[0, 0] = jnp.dot(box_ref[0, :, : 2 * reach], up_weight[reach:, :], preferred_element_type=F32)
    pooled_ref[0, 1] = jnp.dot(box_ref[0, :, reach:], up_weight[: 2 * reach, :], preferred_element_type=F32)


def box_level(cot, pre, weight, cs):
    samples, height, wide, c3 = cot.shape
    c4 = weight.shape[2] - cs
    half = wide // 2
    block = pl.BlockSpec((1, height, wide, c3), lambda s: (s, 0, 0, 0))
    return pl.pallas_call(
        box_kernel,
        grid=(samples,),
        in_specs=[block, block, pl.BlockSpec((3, 3, c4, c3), lambda s: (0, 0, 0, 0))],
        out_specs=[
            block,
            pl.BlockSpec((1, half, 9 * c3), lambda s: (s, 0, 0)),
            pl.BlockSpec((1, 2, wide, c3), lambda s: (s, 0, 0, 0)),
            pl.BlockSpec((1, 2, half, c4), lambda s: (s, 0, 0, 0)),
            pl.BlockSpec((9 * c3, c4), lambda s: (0, 0)),
        ],
        out_shape=[
            pltpu.HBM((samples, height, wide, c3), BF16),
            pltpu.HBM((samples, half, 9 * c3), BF16),
            jax.ShapeDtypeStruct((samples, 2, wide, c3), BF16),
            jax.ShapeDtypeStruct((samples, 2, half, c4), F32),
            jax.ShapeDtypeStruct((9 * c3, c4), BF16),
        ],
        scratch_shapes=[pltpu.VMEM((height, wide, c3), F32)],
        compiler_params=params(VMEM),
        cost_estimate=cost(1.2e9, 8e6),
        name="box_level",
    )(in_hbm(cot), in_hbm(pre), in_hbm(weight))


def edge_kernel(
    place_ref, near_ref, far_ref, edge_ref, pooled_ref, low_weight_ref, high_weight_ref,
    out_ref, box_low_ref, box_high_ref, rows32,
):
    half = pooled_ref.shape[-2]
    c3 = edge_ref.shape[-1]
    odd = place_ref[0] >= 2
    near, far = near_ref[0].astype(F32), far_ref[0].astype(F32)
    sides = (
        (jnp.where(odd, near, far), edge_ref[0, 0].astype(F32), low_weight_ref, box_low_ref),
        (edge_ref[0, 1].astype(F32), jnp.where(odd, far, near), high_weight_ref, box_high_ref),
    )
    for i, (upper, lower, weight_ref, box_ref) in enumerate(sides):
        rows32[0] = upper
        rows32[1] = lower
        for d, value in enumerate(box_sums(rows32.at[0], rows32.at[1], half)):
            box_ref[0, :, d * c3 : (d + 1) * c3] = value
        out_ref[0, i] = pooled_ref[0, i] + jnp.dot(box_ref[0], weight_ref[...], preferred_element_type=F32)


def edge_level(place, near, far, edge, pooled, up_weight):
    samples, _, half, c4 = pooled.shape
    _, _, wide, c3 = edge.shape
    row = pl.BlockSpec((1, wide, c3), lambda s: (s, 0, 0))
    whole = pl.BlockSpec((1, 2, half, c4), lambda s: (s, 0, 0, 0))
    box_spec = pl.BlockSpec((1, half, 3 * c3), lambda s: (s, 0, 0))
    box = pltpu.HBM((samples, half, 3 * c3), BF16)
    return pl.pallas_call(
        edge_kernel,
        grid=(samples,),
        in_specs=[
            pl.BlockSpec(memory_space=pltpu.SMEM), row, row,
            pl.BlockSpec((1, 2, wide, c3), lambda s: (s, 0, 0, 0)), whole,
            pl.BlockSpec((3 * c3, c4), lambda s: (0, 0)),
            pl.BlockSpec((3 * c3, c4), lambda s: (2, 0)),
        ],
        out_specs=[whole, box_spec, box_spec],
        out_shape=[pltpu.HBM((samples, 2, half, c4), F32), box, box],
        scratch_shapes=[pltpu.VMEM((2, wide, c3), F32)],
        compiler_params=params(VMEM),
        cost_estimate=cost(LONG, 4e6),
        name="edge_level",
    )(place, in_hbm(near), in_hbm(far), edge, pooled, up_weight, up_weight)


def fine_kernel(
    place_ref, grad_ref, near_ref, far_ref, skip_ref, weight_ref, grad_skip_ref, keep_ref, send_ref, taps, skip_weight, total, *, scale
):
    sample = pl.program_id(0)
    odd = place_ref[0] >= 2
    c3 = grad_ref.shape[-1]
    cs = skip_ref.shape[-1]
    c4 = weight_ref.shape[2] - cs

    @pl.when(sample == 0)
    def _():
        total[...] = jnp.zeros_like(total)
        for u in range(4):
            for d in range(3):
                at = (u * 3 + d) * c3
                for t in range(2):
                    dy = u - t
                    if 0 <= dy <= 2:
                        block = weight_ref[2 - dy, 2 - d, c4:, :].astype(F32).T.astype(BF16)
                    else:
                        block = jnp.zeros((c3, cs), BF16)
                    skip_weight[at : at + c3, t * cs : (t + 1) * cs] = block

    for v in range(6):
        if v == 0:
            grad = jnp.where(odd, near_ref[0], far_ref[0])
        elif v == 5:
            grad = jnp.where(odd, far_ref[0], near_ref[0])
        else:
            grad = grad_ref[0, v - 1]
        before, after = shifted(grad.astype(F32))
        at = v * 3 * c3
        taps[:, at : at + c3] = before.astype(BF16)
        taps[:, at + c3 : at + 2 * c3] = grad
        taps[:, at + 2 * c3 : at + 3 * c3] = after.astype(BF16)

    for pair in range(2):
        window = taps[:, 2 * pair * 3 * c3 : (2 * pair + 4) * 3 * c3]
        back = jnp.dot(window, skip_weight[...], preferred_element_type=F32)
        grad_skip_ref[0, 2 * pair] = back[:, :cs].astype(BF16)
        grad_skip_ref[0, 2 * pair + 1] = back[:, cs:].astype(BF16)
        feats = jnp.concatenate([skip_ref[0, 2 * pair], skip_ref[0, 2 * pair + 1]], axis=1)
        total[...] += tdot(feats, window)

    @pl.when(sample == pl.num_programs(0) - 1)
    def _():
        core = place_ref[0] % 2

        part = cs // 2
        for dy in range(3):
            for d in range(3):
                first = (dy * 3 + d) * c3
                second = ((dy + 1) * 3 + d) * c3
                value = (total[:cs, first : first + c3] + total[cs:, second : second + c3]) * scale
                low, high = value[:part], value[part:]
                tap = (2 - dy) * 3 + 2 - d
                keep_ref[tap] = tiles(jnp.where(core == 0, low, high))
                send_ref[tap] = tiles(jnp.where(core == 0, high, low))


def fine_level(place, grad, near, far, skip, weight, fine_cells):
    samples, height, wide, cs = skip.shape
    c3 = grad.shape[-1]
    part = jax.ShapeDtypeStruct((9, cs // 32, 16, c3), BF16)
    whole = pl.BlockSpec(part.shape, lambda s: (0, 0, 0, 0))
    return pl.pallas_call(
        functools.partial(fine_kernel, scale=1.0 / math.sqrt(fine_cells)),
        grid=(samples,),
        in_specs=[
            pl.BlockSpec(memory_space=pltpu.SMEM),
            pl.BlockSpec((1, height, wide, c3), lambda s: (s, 0, 0, 0)),
            pl.BlockSpec((1, wide, c3), lambda s: (s, 0, 0)),
            pl.BlockSpec((1, wide, c3), lambda s: (s, 0, 0)),
            pl.BlockSpec((1, height, wide, cs), lambda s: (s, 0, 0, 0)),
            pl.BlockSpec(weight.shape, lambda s: (0, 0, 0, 0)),
        ],
        out_specs=[pl.BlockSpec((1, height, wide, cs), lambda s: (s, 0, 0, 0)), whole, whole],
        out_shape=[jax.ShapeDtypeStruct((samples, height, wide, cs), BF16), part, part],
        scratch_shapes=[
            pltpu.VMEM((wide, 18 * c3), BF16),
            pltpu.VMEM((12 * c3, 2 * cs), BF16),
            pltpu.VMEM((2 * cs, 12 * c3), F32),
        ],
        compiler_params=params(VMEM),
        cost_estimate=cost(5e9, 8e6),
        name="fine_level",
    )(place, *(in_hbm(a) for a in (grad, near, far, skip, weight)))


def coarse_grad_kernel(place_ref, pooled_ref, pre_ref, near_ref, far_ref):
    channels, half = pooled_ref.shape[-1], pooled_ref.shape[-2]
    odd = place_ref[0] >= 2
    rows = []
    for i in range(2):
        value = pre_ref[:, 0, 0, i].reshape(channels, half).astype(F32).T
        rows.append((pooled_ref[0, i] * silu_grad(value)).astype(BF16))
    near_ref[0] = jnp.where(odd, rows[0], rows[1])
    far_ref[0] = jnp.where(odd, rows[1], rows[0])


def coarse_grad(place, pooled, received):
    samples, _, half, c4 = pooled.shape
    peers, _, _, _, own, _ = received.shape
    out = jax.ShapeDtypeStruct((samples, half, c4), BF16)
    spec = pl.BlockSpec((1, half, c4), lambda s: (s, 0, 0))
    return pl.pallas_call(
        coarse_grad_kernel,
        grid=(samples,),
        in_specs=[
            pl.BlockSpec(memory_space=pltpu.SMEM),
            pl.BlockSpec((1, 2, half, c4), lambda s: (s, 0, 0, 0)),
            pl.BlockSpec((peers, 1, 1, 2, own, half), lambda s: (0, 0, s, 0, 0, 0)),
        ],
        out_specs=[spec, spec],
        out_shape=[out, out],
        compiler_params=params(VMEM),
        cost_estimate=cost(2e7, 2e6),
        name="coarse_grad",
    )(place, in_hbm(pooled), received)


def up_kernel(
    place_ref, pre_ref, box_ref, box_low_ref, box_high_ref, skip_keep_ref, skip_send_ref, keep_ref, send_ref, total,
    *, scale
):
    sample = pl.program_id(0)
    wide = pre_ref.shape[-1]
    c4 = pre_ref.shape[0] * pre_ref.shape[-2]
    c3 = keep_ref.shape[-1]

    @pl.when(sample == 0)
    def _():
        total[...] = jnp.zeros_like(total)

    reach = 3 * c3
    windows = (
        ((0, box_low_ref[0]), (reach, box_ref[0, :, : 2 * reach])),
        ((0, box_ref[0, :, reach:]), (2 * reach, box_high_ref[0])),
    )
    for i in range(2):
        value = pre_ref[:, 0, 0, i].reshape(c4, wide).astype(F32)
        value = (value * jax.nn.sigmoid(value)).astype(BF16)
        for at, window in windows[i]:
            total[:, at : at + window.shape[1]] += jnp.dot(value, window, preferred_element_type=F32)

    @pl.when(sample == pl.num_programs(0) - 1)
    def _():
        core = place_ref[0] % 2
        part = c4 // 2
        mine = part // 16
        for dy in range(3):
            for d in range(3):
                at = (dy * 3 + d) * c3
                value = total[:, at : at + c3] * scale
                low, high = value[:part], value[part:]
                tap = (2 - dy) * 3 + 2 - d
                keep_ref[tap, :mine] = tiles(jnp.where(core == 0, low, high))
                send_ref[tap, :mine] = tiles(jnp.where(core == 0, high, low))
                keep_ref[tap, mine:] = skip_keep_ref[tap]
                send_ref[tap, mine:] = skip_send_ref[tap]


def up_level(place, received, box, box_low, box_high, skip_keep, skip_send, fine_cells):
    peers, _, samples, _, own, wide = received.shape
    c4 = peers * own
    c3 = box.shape[-1] // 9
    part = jax.ShapeDtypeStruct((9, c4 // 32 + skip_keep.shape[1], 16, c3), BF16)
    whole = pl.BlockSpec(part.shape, lambda s: (0, 0, 0, 0))
    skips = pl.BlockSpec(skip_keep.shape, lambda s: (0, 0, 0, 0))
    return pl.pallas_call(
        functools.partial(up_kernel, scale=1.0 / math.sqrt(fine_cells)),
        grid=(samples,),
        in_specs=[
            pl.BlockSpec(memory_space=pltpu.SMEM),
            pl.BlockSpec((peers, 1, 1, 2, own, wide), lambda s: (0, 0, s, 0, 0, 0)),
            pl.BlockSpec((1, wide, 9 * c3), lambda s: (s, 0, 0)),
            pl.BlockSpec((1, wide, 3 * c3), lambda s: (s, 0, 0)),
            pl.BlockSpec((1, wide, 3 * c3), lambda s: (s, 0, 0)),
            skips, skips,
        ],
        out_specs=[whole, whole],
        out_shape=[part, part],
        scratch_shapes=[pltpu.VMEM((c4, 9 * c3), F32)],
        compiler_params=params(VMEM),
        cost_estimate=cost(1e9, 5e6),
        name="up_level",
    )(place, received, box, box_low, box_high, skip_keep, skip_send)


def fill_coarse_taps(odd, rows, taps):
    wide, c4 = rows[0].shape

    def fill(order):
        for v, row in zip(order, rows):
            before, after = shifted(row.astype(F32))
            lines = slice(v * wide, (v + 1) * wide)
            taps[lines, :c4] = before.astype(BF16)
            taps[lines, c4 : 2 * c4] = row
            taps[lines, 2 * c4 :] = after.astype(BF16)

    count = len(rows)
    pl.when(odd)(lambda: fill(range(count - 1, -1, -1)))
    pl.when(jnp.logical_not(odd))(lambda: fill(range(count)))


def dot32(left, right):
    return jnp.dot(left, right, preferred_element_type=F32)


def own_weight_kernel(place_ref, input_ref, far_ref, near_ref, out_ref, taps):
    wide = input_ref.shape[-1]
    c4 = far_ref.shape[-1]

    @pl.when(pl.program_id(0) == 0)
    def _():
        out_ref[...] = jnp.zeros_like(out_ref)

    fill_coarse_taps(place_ref[0] >= 2, (far_ref[0], near_ref[0]), taps)
    first, second = (input_ref[:, 0, 0, i].reshape(c4, wide) for i in range(2))
    out_ref[0] += dot32(second, taps[:wide, :])
    out_ref[1] += dot32(jnp.concatenate([first, second], axis=1), taps[...])
    out_ref[2] += dot32(first, taps[wide:, :])


def own_weight_level(place, received, far, near):
    peers, _, samples, _, own, wide = received.shape
    c4 = peers * own
    row = pl.BlockSpec((1, wide, c4), lambda s: (s, 0, 0))
    return pl.pallas_call(
        own_weight_kernel,
        grid=(samples,),
        in_specs=[
            pl.BlockSpec(memory_space=pltpu.SMEM),
            pl.BlockSpec((peers, 1, 1, 2, own, wide), lambda s: (0, 1, s, 0, 0, 0)),
            row, row,
        ],
        out_specs=pl.BlockSpec((3, c4, 3 * c4), lambda s: (0, 0, 0)),
        out_shape=jax.ShapeDtypeStruct((3, c4, 3 * c4), F32),
        scratch_shapes=[pltpu.VMEM((2 * wide, 3 * c4), BF16)],
        compiler_params=params(VMEM),
        cost_estimate=cost(LONG, 4e6),
        name="own_weight_level",
    )(place, received, far, near)


def coarse_weight_kernel(place_ref, input_ref, from_far_ref, from_near_ref, own_ref, out_ref, taps, total, *, scale):
    sample = pl.program_id(0)
    wide = input_ref.shape[-1]
    part = input_ref.shape[0] * input_ref.shape[-2]
    c4 = from_far_ref.shape[-1]

    fill_coarse_taps(place_ref[0] >= 2, (from_far_ref[0], from_near_ref[0]), taps)
    terms = [dot32(input_ref[:, 0, 0, i].reshape(part, wide), taps[i * wide : (i + 1) * wide, :]) for i in range(2)]

    @pl.when(sample == 0)
    def _():
        for i, term in enumerate(terms):
            total[i] = term

    @pl.when(sample > 0)
    def _():
        for i, term in enumerate(terms):
            total[i] += term

    @pl.when(sample == pl.num_programs(0) - 1)
    def _():
        count = part // 16
        for dy in range(3):
            for d in range(3):
                for side in range(c4 // 128):
                    at = d * c4 + side * 128
                    value = own_ref[dy, :, at : at + 128]
                    if dy != 1:
                        value = value + total[dy // 2, :, at : at + 128]
                    tap = ((2 - dy) * 3 + 2 - d) * (c4 // 128) + side
                    out_ref[tap * count : (tap + 1) * count] = tiles(value * scale)


def coarse_weight_level(place, received, from_far, from_near, own_terms, coarse_cells):
    peers, _, samples, _, own, wide = received.shape
    c4 = peers * own
    shape = (9 * (c4 // 128) * (c4 // 32), 16, 128)
    row = pl.BlockSpec((1, wide, c4), lambda s, place: (s, 0, 0))
    return pl.pallas_call(
        functools.partial(coarse_weight_kernel, scale=1.0 / math.sqrt(coarse_cells)),
        grid_spec=pltpu.PrefetchScalarGridSpec(
            num_scalar_prefetch=1,
            grid=(samples,),
            in_specs=[
                pl.BlockSpec((peers // 2, 1, 1, 2, own, wide), lambda s, place: (place[0] % 2, 1, s, 0, 0, 0)),
                row, row,
                pl.BlockSpec((3, c4 // 2, 3 * c4), lambda s, place: (0, place[0] % 2, 0)),
            ],
            out_specs=pl.BlockSpec(shape, lambda s, place: (0, 0, 0)),
            scratch_shapes=[pltpu.VMEM((2 * wide, 3 * c4), BF16), pltpu.VMEM((2, c4 // 2, 3 * c4), F32)],
        ),
        out_shape=jax.ShapeDtypeStruct(shape, BF16),
        compiler_params=params(VMEM),
        cost_estimate=cost(0.4e9, 2e6),
        name="coarse_weight_level",
    )(place, received, from_far, from_near, own_terms)


def coarse_specs(wide, c4, count):
    return [pl.BlockSpec((1, wide, c4), lambda s: (s, 0, 0))] * count


def coarse_input_kernel(chan_ref, weight_ref, first_ref, second_ref, third_ref, fourth_ref, *rest):
    *piece_refs, taps, stage = rest
    wide, c4 = first_ref.shape[1:]
    own = c4 // len(piece_refs)
    rows = (first_ref[0], second_ref[0], third_ref[0], fourth_ref[0])
    fill_coarse_taps(chan_ref[0] % 2 == 1, rows, taps)
    total = None
    for dy in range(3):
        for d in range(3):
            window = taps[dy * wide : (dy + 2) * wide, d * c4 : (d + 1) * c4]
            term = dott(weight_ref[2 - dy, 2 - d], window)
            total = term if total is None else total + term
    stage[...] = total.astype(BF16)
    for k, ref in enumerate(piece_refs):
        at = pl.multiple_of(jnp.bitwise_xor(chan_ref[0], k) * own, own)
        for i in range(2):
            ref[0, i] = stage[pl.ds(at, own), i * wide : (i + 1) * wide]


def coarse_input_level(chan, weight, rows, peers):
    samples, wide, c4 = rows[0].shape
    own = c4 // peers
    return pl.pallas_call(
        coarse_input_kernel,
        grid=(samples,),
        in_specs=[
            pl.BlockSpec(memory_space=pltpu.SMEM),
            pl.BlockSpec(weight.shape, lambda s: (0, 0, 0, 0)),
        ] + coarse_specs(wide, c4, 4),
        out_specs=[pl.BlockSpec((1, 2, own, wide), lambda s: (s, 0, 0, 0))] * peers,
        out_shape=[jax.ShapeDtypeStruct((samples, 2, own, wide), BF16)] * peers,
        scratch_shapes=[pltpu.VMEM((4 * wide, 3 * c4), BF16), pltpu.VMEM((c4, 2 * wide), BF16)],
        compiler_params=params(VMEM),
        cost_estimate=cost(1.3e9, 3e6),
        name="coarse_input_level",
    )(chan, weight, *rows)


def place_kernel(first, count, chan_ref, *refs):
    out_ref = refs[-1]
    if len(refs) > count + 1:
        out_ref[...] = refs[count][...]
    for k in range(count):
        at = jnp.bitwise_xor(chan_ref[0], first + k) * 2
        out_ref[:, pl.ds(at, 2)] = refs[k][...]


def placed(chan, pieces, first, peers, earlier=(), flops=1e6):
    samples, rows, own, wide = pieces[0].shape
    vmem = pl.BlockSpec(memory_space=pltpu.VMEM)
    return pl.pallas_call(
        functools.partial(place_kernel, first, len(pieces)),
        in_specs=[pl.BlockSpec(memory_space=pltpu.SMEM)] + [vmem] * (len(pieces) + len(earlier)),
        out_shape=jax.ShapeDtypeStruct((samples, rows * peers, own, wide), BF16),
        compiler_params=params(VMEM),
        cost_estimate=cost(flops, 1e6),
        name="place",
    )(chan, *pieces, *earlier)


def join_kernel(first, *refs):
    *part_refs, out_ref, stage, sems = refs
    one, more = part_refs[:2]
    count = one.shape[0]
    copies = []
    for at in range(0, stage.shape[0], 36):
        size = min(36, stage.shape[0] - at)
        held = max(min(size, count - at), 0)
        if held:
            lines = slice(at, at + held)
            stage[lines] = (one[lines].astype(F32) + more[lines].astype(F32)).astype(BF16)
        if held < size:
            stage[at + held : at + size] = jnp.zeros((size - held,) + stage.shape[1:], BF16)
        copies.append(
            pltpu.make_async_copy(
                stage.at[pl.ds(at, size)], out_ref.at[pl.ds(first + at, size)], sems.at[len(copies)]
            )
        )
        copies[-1].start()
    for copy in copies:
        copy.wait()


def joined(one, more, first, size, total, earlier=()):
    hbm = pl.BlockSpec(memory_space=pltpu.HBM)
    vmem = pl.BlockSpec(memory_space=pltpu.VMEM)
    return pl.pallas_call(
        functools.partial(join_kernel, first),
        in_specs=[vmem, vmem] + [hbm] * len(earlier),
        out_specs=hbm,
        out_shape=jax.ShapeDtypeStruct((total, 16, 128), BF16),
        input_output_aliases={2: 0} if earlier else {},
        scratch_shapes=[pltpu.VMEM((size, 16, 128), BF16), pltpu.SemaphoreType.DMA((-(-size // 36),))],
        compiler_params=params(VMEM),
        cost_estimate=cost(1e6, 2e6),
        name="join",
    )(one, more, *earlier)


def sum_kernel(parts_ref, out_ref):
    total = parts_ref[0].astype(F32)
    for k in range(1, parts_ref.shape[0]):
        total = total + parts_ref[k].astype(F32)
    total = total.astype(BF16)
    for k in range(out_ref.shape[0]):
        out_ref[k] = total


def unpack_kernel(place_ref, parts_ref, *rest):
    fine_ref, coarse_ref, fine_stage, coarse_stage, sems = rest[-5:]
    c4 = coarse_ref.shape[-1]
    sides = c4 // 128
    lines, skips = c4 // 2, (fine_ref.shape[-2] - c4) // 2
    line_tiles, skip_tiles = lines // 16, skips // 16
    core = place_ref[0] % 2
    rows = pl.ds(pl.multiple_of(core * lines, lines), lines)
    skip_rows = pl.ds(pl.multiple_of(c4 + core * skips, skips), skips)

    def take(at, count):
        return parts_ref[at : at + count].astype(F32).reshape(count * 16, 128)

    copies = []

    def send(source, target):
        copies.append(pltpu.make_async_copy(source, target, sems.at[len(copies)]))
        copies[-1].start()

    for tap in range(9):
        for side in range(sides):
            at = (tap * sides + side) * line_tiles
            coarse_stage[tap, :, side * 128 : (side + 1) * 128] = take(at, line_tiles)
        send(coarse_stage.at[tap], coarse_ref.at[tap, rows])
        at = 9 * sides * line_tiles + tap * (line_tiles + skip_tiles)
        fine_stage[tap, :lines] = take(at, line_tiles)
        fine_stage[tap, lines:] = take(at + line_tiles, skip_tiles)
        send(fine_stage.at[tap, pl.ds(0, lines)], fine_ref.at[tap, rows])
        send(fine_stage.at[tap, pl.ds(lines, skips)], fine_ref.at[tap, skip_rows])
    for copy in copies:
        copy.wait()


SWAP = ((0, 1), (1, 0))


def grad_sums(parts, chips):
    each = parts.shape[0] // chips
    parts = lax.all_to_all(parts.reshape(chips, each, 16, 128), CHIPS, 0, 0, tiled=True)
    summed = pl.pallas_call(
        sum_kernel,
        out_shape=jax.ShapeDtypeStruct((chips, each, 16, 128), BF16),
        compiler_params=params(VMEM),
        cost_estimate=cost(1e6, 1.3e6),
        name="sum_parts",
    )(parts)
    return lax.all_to_all(summed, CHIPS, 0, 0, tiled=True).reshape(chips * each, 16, 128)


def unpacked(place, half, fine_shape, coarse_shape, earlier=()):
    shapes = [jax.ShapeDtypeStruct((9,) + shape[2:], F32) for shape in (fine_shape, coarse_shape)]
    hbm = pl.BlockSpec(memory_space=pltpu.HBM)
    return pl.pallas_call(
        unpack_kernel,
        in_specs=[pl.BlockSpec(memory_space=pltpu.SMEM), pl.BlockSpec(memory_space=pltpu.VMEM)]
        + [hbm] * len(earlier),
        out_specs=[hbm, hbm],
        out_shape=shapes,
        input_output_aliases={2 + i: i for i in range(len(earlier))},
        scratch_shapes=[
            pltpu.VMEM((9, fine_shape[2] // 2, fine_shape[3]), F32),
            pltpu.VMEM((9, coarse_shape[2] // 2, coarse_shape[3]), F32),
            pltpu.SemaphoreType.DMA((27,)),
        ],
        compiler_params=params(VMEM),
        cost_estimate=cost(1, 1),
        name="unpack",
    )(place, half, *earlier)


def start_kernel(
    place_ref, pre_ref, input_ref, cot_ref, fine_pre_ref, pieces_ref, near_ref, far_ref, rows, row_sems, sems
):
    peers, _, samples, lines, _, _ = pieces_ref.shape
    odd = place_ref[0] >= 2
    last = cot_ref.shape[1] - 1
    row_copies = []
    for a, ref in enumerate((cot_ref, fine_pre_ref)):
        for e, line in enumerate((jnp.where(odd, 0, last), jnp.where(odd, last, 0))):
            for s in range(samples):
                row_copies.append(
                    pltpu.make_async_copy(ref.at[s, line], rows.at[a, e, s], row_sems.at[len(row_copies)])
                )
    copies = []
    for c in range(peers):
        for a, ref in enumerate((pre_ref, input_ref)):
            for s in range(samples):
                copies.append(
                    pltpu.make_async_copy(
                        ref.at[s, pl.ds(c * lines, lines)], pieces_ref.at[c, a, s], sems.at[len(copies)]
                    )
                )
    for copy in row_copies + copies:
        copy.start()
    for copy in row_copies:
        copy.wait()
    for e, out_ref in enumerate((near_ref, far_ref)):
        for s in range(samples):
            grad = rows[0, e, s].astype(F32) * silu_grad(rows[1, e, s].astype(F32))
            out_ref[s] = grad.astype(BF16)
    for copy in copies:
        copy.wait()


def start_level(place, pre, values, cot, fine_pre, peers):
    samples, lines, own, wide = pre.shape
    fine_wide, c3 = cot.shape[2:]
    hbm = pl.BlockSpec(memory_space=pltpu.HBM)
    vmem = pl.BlockSpec(memory_space=pltpu.VMEM)
    edge = jax.ShapeDtypeStruct((samples, fine_wide, c3), BF16)
    return pl.pallas_call(
        start_kernel,
        in_specs=[pl.BlockSpec(memory_space=pltpu.SMEM), hbm, hbm, hbm, hbm],
        out_specs=[vmem, vmem, vmem],
        out_shape=[jax.ShapeDtypeStruct((peers, 2, samples, lines // peers, own, wide), BF16), edge, edge],
        scratch_shapes=[
            pltpu.VMEM((2, 2, samples, fine_wide, c3), BF16),
            pltpu.SemaphoreType.DMA((4 * samples,)),
            pltpu.SemaphoreType.DMA((peers * 2 * samples,)),
        ],
        compiler_params=params(VMEM),
        cost_estimate=cost(1e7, 3e6),
        name="start",
    )(place, *(in_hbm(a) for a in (pre, values, cot, fine_pre)))


def swapped(near, far):
    count = 1
    for axis in ALL:
        count *= lax.axis_size(axis)
    inside = [(i, i ^ 1) for i in range(count)]
    outside = [(i, i + 1) for i in range(1, count - 1, 2)]
    outside += [(target, source) for source, target in outside]
    return lax.ppermute(near, ALL, inside), lax.ppermute(far, ALL, outside)


def shards(coarse_input, coarse_pre, skip_feats, fine_pre, fine_cotangent, fine_weight, coarse_weight):
    peers = 1
    for axis in CHAN:
        peers *= lax.axis_size(axis)
    devices = peers
    for axis in ROWS:
        devices *= lax.axis_size(axis)
    samples, lines, wide, own = coarse_input.shape
    core = lax.axis_index("core").astype(jnp.int32)
    chan = lax.axis_index(CHAN).astype(jnp.int32).reshape(1)
    place = (core + 2 * (lax.axis_index("xl").astype(jnp.int32))).reshape(1)
    other_place = (1 - core + 2 * (lax.axis_index("xl").astype(jnp.int32))).reshape(1)

    pieces, edge_near, edge_far = start_level(
        place, coarse_pre.transpose(0, 1, 3, 2), coarse_input.transpose(0, 1, 3, 2), fine_cotangent, fine_pre, peers
    )
    edge_near, edge_far = swapped(edge_near, edge_far)
    received = lax.all_to_all(pieces, CHAN, 0, 0, tiled=True)

    cs = skip_feats.shape[-1]
    fine_cells = fine_pre.shape[0] * fine_pre.shape[1] * fine_pre.shape[2] * devices
    fine_grad, box, edge, pooled, up_weight = box_level(fine_cotangent, fine_pre, fine_weight, cs)
    pooled, box_low, box_high = edge_level(place, edge_near, edge_far, edge, pooled, up_weight)
    grad_skip, skip_keep, skip_send = fine_level(
        place, fine_grad, edge_near, edge_far, skip_feats, fine_weight, fine_cells
    )
    received, skip_keep, skip_send = lax.optimization_barrier((received, skip_keep, skip_send))
    near, far = coarse_grad(place, pooled, received)
    from_near, from_far = swapped(near, far)
    fine_keep, fine_send = up_level(place, received, box, box_low, box_high, skip_keep, skip_send, fine_cells)
    fine_more = lax.ppermute(fine_send, "core", SWAP)
    own_terms = own_weight_level(place, received, far, near)
    chips = devices // lax.axis_size("core")
    fine_keep, fine_more = (a.reshape((-1, 16, 128)) for a in (fine_keep, fine_more))
    coarse_count = 9 * (fine_weight.shape[2] - cs) ** 2 // (2 * 16 * 128)
    total = -(-(coarse_count + fine_keep.shape[0]) // chips) * chips
    sums = joined(fine_keep, fine_more, coarse_count, total - coarse_count, total)
    from_near, from_far, sums, own_terms = lax.optimization_barrier((from_near, from_far, sums, own_terms))
    rows = (from_far, far, near, from_near)
    coarse_cells = samples * (lines // peers) * wide * devices
    coarse_send = coarse_weight_level(other_place, received, from_far, from_near, own_terms, coarse_cells)
    coarse_more = lax.ppermute(coarse_send, "core", SWAP)
    coarse_keep = coarse_weight_level(place, received, from_far, from_near, own_terms, coarse_cells)
    back = coarse_input_level(chan, coarse_weight, rows, peers)

    def home(k, piece):
        return lax.ppermute(piece, CHAN, [(i, i ^ k) for i in range(peers)])

    sums = joined(coarse_keep, coarse_more, 0, coarse_count, total, (sums,))
    mine = grad_sums(sums, chips)
    early = [back[0]] + [home(k, back[k]) for k in range(1, EARLY)]
    grad_input = placed(chan, early, 0, peers, flops=LONG)
    grad_input, *late = lax.optimization_barrier((grad_input, *back[EARLY:]))
    late = [home(EARLY + k, piece) for k, piece in enumerate(late)]
    mine, grad_input = lax.optimization_barrier((mine, grad_input))
    grad_input = placed(chan, late, EARLY, peers, (grad_input,), flops=LONG)
    other = lax.ppermute(mine, "core", SWAP)
    sums = unpacked(place, mine, fine_weight.shape, coarse_weight.shape)
    grad_fine, grad_coarse = unpacked(other_place, other, fine_weight.shape, coarse_weight.shape, sums)
    return (
        grad_skip,
        grad_input.transpose(0, 1, 3, 2),
        grad_fine.reshape(fine_weight.shape),
        grad_coarse.reshape(coarse_weight.shape),
    )


def solution(mesh):
    split = Mesh(mesh.devices.reshape([size for _, size in SPLIT]), tuple(name for name, _ in SPLIT))
    coarse = P(None, ROWS, None, CHAN)
    fine = P(None, ALL, None, None)
    return jax.shard_map(
        shards,
        mesh=split,
        in_specs=(coarse, coarse, fine, fine, fine, P(), P()),
        out_specs=(fine, coarse, P(), P()),
        check_vma=False,
    )
```

```python
import functools
import math

import jax
import jax.numpy as jnp
from jax import lax
from jax.experimental import pallas as pl
from jax.experimental.pallas import tpu as pltpu
from jax.sharding import Mesh
from jax.sharding import PartitionSpec as P

F32 = jnp.float32
BF16 = jnp.bfloat16
MIB = 1 << 20
VMEM = 18
LATE = (6, 7)
LONG = 1e11

SPLIT = (("xh", 2), ("z", 4), ("core", 2), ("y", 4), ("xl", 2))
ROWS = ("xh", "z", "core")
CHAN = ("y", "xl")
ALL = ROWS + CHAN
CHIPS = ("xh", "z", "y", "xl")


def params(limit):
    return pltpu.CompilerParams(vmem_limit_bytes=limit * MIB)


def cost(flops, nbytes):
    return pl.CostEstimate(flops=int(flops), bytes_accessed=int(nbytes), transcendentals=0)


def in_hbm(array):
    return pltpu.with_memory_space_constraint(array, pltpu.HBM)


def silu_grad(value):
    sigma = jax.nn.sigmoid(value)
    return sigma * (1.0 + value * (1.0 - sigma))


def shifted(field):
    extent = field.shape[0]
    index = lax.broadcasted_iota(jnp.int32, field.shape, 0)
    before = jnp.where(index == 0, 0.0, pltpu.roll(field, 1, 0))
    after = jnp.where(index == extent - 1, 0.0, pltpu.roll(field, extent - 1, 0))
    return before, after


def tdot(left, right):
    return lax.dot_general(left, right, (((0,), (0,)), ((), ())), preferred_element_type=F32)


def dott(left, right):
    return lax.dot_general(left, right, (((1,), (1,)), ((), ())), preferred_element_type=F32)


def tiles(block):
    return block.astype(BF16).reshape(block.shape[0] // 16, 16, block.shape[1])


def box_sums(upper, lower, half):
    even = upper[pl.ds(0, half, 2), :] + lower[pl.ds(0, half, 2), :]
    odd = upper[pl.ds(1, half, 2), :] + lower[pl.ds(1, half, 2), :]
    before, _ = shifted(odd)
    _, after = shifted(even)
    return (before + even).astype(BF16), (even + odd).astype(BF16), (odd + after).astype(BF16)


def box_kernel(cot_ref, pre_ref, weight_ref, grad_ref, box_ref, edge_ref, pooled_ref, up_weight, rows32):
    c3 = cot_ref.shape[-1]
    half = pooled_ref.shape[-2]
    reach = 3 * c3

    @pl.when(pl.program_id(0) == 0)
    def _():
        for dy in range(3):
            for d in range(3):
                at = (dy * 3 + d) * c3
                up_weight[at : at + c3, :] = weight_ref[2 - dy, 2 - d].astype(F32).T.astype(BF16)

    for v in range(4):
        grad = (cot_ref[0, v].astype(F32) * silu_grad(pre_ref[0, v].astype(F32))).astype(BF16)
        grad_ref[0, v] = grad
        rows32[v] = grad.astype(F32)
        if v % 3 == 0:
            edge_ref[0, v // 3] = grad
    for v in range(3):
        for d, value in enumerate(box_sums(rows32.at[v], rows32.at[v + 1], half)):
            at = v * reach + d * c3
            box_ref[0, :, at : at + c3] = value
    pooled_ref[0, 0] = jnp.dot(box_ref[0, :, : 2 * reach], up_weight[reach:, :], preferred_element_type=F32)
    pooled_ref[0, 1] = jnp.dot(box_ref[0, :, reach:], up_weight[: 2 * reach, :], preferred_element_type=F32)


def box_level(cot, pre, weight, cs):
    samples, height, wide, c3 = cot.shape
    c4 = weight.shape[2] - cs
    half = wide // 2
    block = pl.BlockSpec((1, height, wide, c3), lambda s: (s, 0, 0, 0))
    return pl.pallas_call(
        box_kernel,
        grid=(samples,),
        in_specs=[block, block, pl.BlockSpec((3, 3, c4, c3), lambda s: (0, 0, 0, 0))],
        out_specs=[
            block,
            pl.BlockSpec((1, half, 9 * c3), lambda s: (s, 0, 0)),
            pl.BlockSpec((1, 2, wide, c3), lambda s: (s, 0, 0, 0)),
            pl.BlockSpec((1, 2, half, c4), lambda s: (s, 0, 0, 0)),
            pl.BlockSpec((9 * c3, c4), lambda s: (0, 0)),
        ],
        out_shape=[
            pltpu.HBM((samples, height, wide, c3), BF16),
            pltpu.HBM((samples, half, 9 * c3), BF16),
            jax.ShapeDtypeStruct((samples, 2, wide, c3), BF16),
            jax.ShapeDtypeStruct((samples, 2, half, c4), F32),
            jax.ShapeDtypeStruct((9 * c3, c4), BF16),
        ],
        scratch_shapes=[pltpu.VMEM((height, wide, c3), F32)],
        compiler_params=params(VMEM),
        cost_estimate=cost(1.2e9, 8e6),
        name="box_level",
    )(in_hbm(cot), in_hbm(pre), in_hbm(weight))


def edge_kernel(
    place_ref, near_ref, far_ref, edge_ref, pooled_ref, low_weight_ref, high_weight_ref,
    out_ref, box_low_ref, box_high_ref, rows32,
):
    half = pooled_ref.shape[-2]
    c3 = edge_ref.shape[-1]
    odd = place_ref[0] >= 2
    near, far = near_ref[0].astype(F32), far_ref[0].astype(F32)
    sides = (
        (jnp.where(odd, near, far), edge_ref[0, 0].astype(F32), low_weight_ref, box_low_ref),
        (edge_ref[0, 1].astype(F32), jnp.where(odd, far, near), high_weight_ref, box_high_ref),
    )
    for i, (upper, lower, weight_ref, box_ref) in enumerate(sides):
        rows32[0] = upper
        rows32[1] = lower
        for d, value in enumerate(box_sums(rows32.at[0], rows32.at[1], half)):
            box_ref[0, :, d * c3 : (d + 1) * c3] = value
        out_ref[0, i] = pooled_ref[0, i] + jnp.dot(box_ref[0], weight_ref[...], preferred_element_type=F32)


def edge_level(place, near, far, edge, pooled, up_weight):
    samples, _, half, c4 = pooled.shape
    _, _, wide, c3 = edge.shape
    row = pl.BlockSpec((1, wide, c3), lambda s: (s, 0, 0))
    whole = pl.BlockSpec((1, 2, half, c4), lambda s: (s, 0, 0, 0))
    box_spec = pl.BlockSpec((1, half, 3 * c3), lambda s: (s, 0, 0))
    box = pltpu.HBM((samples, half, 3 * c3), BF16)
    return pl.pallas_call(
        edge_kernel,
        grid=(samples,),
        in_specs=[
            pl.BlockSpec(memory_space=pltpu.SMEM), row, row,
            pl.BlockSpec((1, 2, wide, c3), lambda s: (s, 0, 0, 0)), whole,
            pl.BlockSpec((3 * c3, c4), lambda s: (0, 0)),
            pl.BlockSpec((3 * c3, c4), lambda s: (2, 0)),
        ],
        out_specs=[whole, box_spec, box_spec],
        out_shape=[jax.ShapeDtypeStruct((samples, 2, half, c4), F32), box, box],
        scratch_shapes=[pltpu.VMEM((2, wide, c3), F32)],
        compiler_params=params(VMEM),
        cost_estimate=cost(LONG, 4e6),
        name="edge_level",
    )(place, near, far, edge, pooled, up_weight, up_weight)


def fine_kernel(
    place_ref, grad_ref, near_ref, far_ref, skip_ref, weight_ref, grad_skip_ref, keep_ref, send_ref, taps, skip_weight, total, *, scale
):
    sample = pl.program_id(0)
    odd = place_ref[0] >= 2
    c3 = grad_ref.shape[-1]
    cs = skip_ref.shape[-1]
    c4 = weight_ref.shape[2] - cs

    @pl.when(sample == 0)
    def _():
        total[...] = jnp.zeros_like(total)
        for u in range(4):
            for d in range(3):
                at = (u * 3 + d) * c3
                for t in range(2):
                    dy = u - t
                    if 0 <= dy <= 2:
                        block = weight_ref[2 - dy, 2 - d, c4:, :].astype(F32).T.astype(BF16)
                    else:
                        block = jnp.zeros((c3, cs), BF16)
                    skip_weight[at : at + c3, t * cs : (t + 1) * cs] = block

    for v in range(6):
        if v == 0:
            grad = jnp.where(odd, near_ref[0], far_ref[0])
        elif v == 5:
            grad = jnp.where(odd, far_ref[0], near_ref[0])
        else:
            grad = grad_ref[0, v - 1]
        before, after = shifted(grad.astype(F32))
        at = v * 3 * c3
        taps[:, at : at + c3] = before.astype(BF16)
        taps[:, at + c3 : at + 2 * c3] = grad
        taps[:, at + 2 * c3 : at + 3 * c3] = after.astype(BF16)

    for pair in range(2):
        window = taps[:, 2 * pair * 3 * c3 : (2 * pair + 4) * 3 * c3]
        back = jnp.dot(window, skip_weight[...], preferred_element_type=F32)
        grad_skip_ref[0, 2 * pair] = back[:, :cs].astype(BF16)
        grad_skip_ref[0, 2 * pair + 1] = back[:, cs:].astype(BF16)
        feats = jnp.concatenate([skip_ref[0, 2 * pair], skip_ref[0, 2 * pair + 1]], axis=1)
        total[...] += tdot(feats, window)

    @pl.when(sample == pl.num_programs(0) - 1)
    def _():
        core = place_ref[0] % 2

        part = cs // 2
        for dy in range(3):
            for d in range(3):
                first = (dy * 3 + d) * c3
                second = ((dy + 1) * 3 + d) * c3
                value = (total[:cs, first : first + c3] + total[cs:, second : second + c3]) * scale
                low, high = value[:part], value[part:]
                tap = (2 - dy) * 3 + 2 - d
                keep_ref[tap] = tiles(jnp.where(core == 0, low, high))
                send_ref[tap] = tiles(jnp.where(core == 0, high, low))


def fine_level(place, grad, near, far, skip, weight, fine_cells):
    samples, height, wide, cs = skip.shape
    c3 = grad.shape[-1]
    part = jax.ShapeDtypeStruct((9, cs // 32, 16, c3), BF16)
    whole = pl.BlockSpec(part.shape, lambda s: (0, 0, 0, 0))
    return pl.pallas_call(
        functools.partial(fine_kernel, scale=1.0 / math.sqrt(fine_cells)),
        grid=(samples,),
        in_specs=[
            pl.BlockSpec(memory_space=pltpu.SMEM),
            pl.BlockSpec((1, height, wide, c3), lambda s: (s, 0, 0, 0)),
            pl.BlockSpec((1, wide, c3), lambda s: (s, 0, 0)),
            pl.BlockSpec((1, wide, c3), lambda s: (s, 0, 0)),
            pl.BlockSpec((1, height, wide, cs), lambda s: (s, 0, 0, 0)),
            pl.BlockSpec(weight.shape, lambda s: (0, 0, 0, 0)),
        ],
        out_specs=[pl.BlockSpec((1, height, wide, cs), lambda s: (s, 0, 0, 0)), whole, whole],
        out_shape=[jax.ShapeDtypeStruct((samples, height, wide, cs), BF16), part, part],
        scratch_shapes=[
            pltpu.VMEM((wide, 18 * c3), BF16),
            pltpu.VMEM((12 * c3, 2 * cs), BF16),
            pltpu.VMEM((2 * cs, 12 * c3), F32),
        ],
        compiler_params=params(VMEM),
        cost_estimate=cost(5e9, 8e6),
        name="fine_level",
    )(place, in_hbm(grad), near, far, in_hbm(skip), in_hbm(weight))


def coarse_grad_kernel(place_ref, pooled_ref, pre_ref, near_ref, far_ref):
    channels, half = pooled_ref.shape[-1], pooled_ref.shape[-2]
    odd = place_ref[0] >= 2
    rows = []
    for i in range(2):
        value = pre_ref[:, 0, 0, i].reshape(channels, half).astype(F32).T
        rows.append((pooled_ref[0, i] * silu_grad(value)).astype(BF16))
    near_ref[0] = jnp.where(odd, rows[0], rows[1])
    far_ref[0] = jnp.where(odd, rows[1], rows[0])


def coarse_grad(place, pooled, received):
    samples, _, half, c4 = pooled.shape
    peers, _, _, _, own, _ = received.shape
    out = jax.ShapeDtypeStruct((samples, half, c4), BF16)
    spec = pl.BlockSpec((1, half, c4), lambda s: (s, 0, 0))
    return pl.pallas_call(
        coarse_grad_kernel,
        grid=(samples,),
        in_specs=[
            pl.BlockSpec(memory_space=pltpu.SMEM),
            pl.BlockSpec((1, 2, half, c4), lambda s: (s, 0, 0, 0)),
            pl.BlockSpec((peers, 1, 1, 2, own, half), lambda s: (0, 0, s, 0, 0, 0)),
        ],
        out_specs=[spec, spec],
        out_shape=[out, out],
        compiler_params=params(VMEM),
        cost_estimate=cost(2e7, 2e6),
        name="coarse_grad",
    )(place, pooled, received)


def up_kernel(
    place_ref, pre_ref, box_ref, box_low_ref, box_high_ref, skip_keep_ref, skip_send_ref, keep_ref, send_ref, total,
    *, scale
):
    sample = pl.program_id(0)
    wide = pre_ref.shape[-1]
    c4 = pre_ref.shape[0] * pre_ref.shape[-2]
    c3 = keep_ref.shape[-1]

    @pl.when(sample == 0)
    def _():
        total[...] = jnp.zeros_like(total)

    reach = 3 * c3
    windows = (
        ((0, box_low_ref[0]), (reach, box_ref[0, :, : 2 * reach])),
        ((0, box_ref[0, :, reach:]), (2 * reach, box_high_ref[0])),
    )
    for i in range(2):
        value = pre_ref[:, 0, 0, i].reshape(c4, wide).astype(F32)
        value = (value * jax.nn.sigmoid(value)).astype(BF16)
        for at, window in windows[i]:
            total[:, at : at + window.shape[1]] += jnp.dot(value, window, preferred_element_type=F32)

    @pl.when(sample == pl.num_programs(0) - 1)
    def _():
        core = place_ref[0] % 2
        part = c4 // 2
        mine = part // 16
        for dy in range(3):
            for d in range(3):
                at = (dy * 3 + d) * c3
                value = total[:, at : at + c3] * scale
                low, high = value[:part], value[part:]
                tap = (2 - dy) * 3 + 2 - d
                keep_ref[tap, :mine] = tiles(jnp.where(core == 0, low, high))
                send_ref[tap, :mine] = tiles(jnp.where(core == 0, high, low))
                keep_ref[tap, mine:] = skip_keep_ref[tap]
                send_ref[tap, mine:] = skip_send_ref[tap]


def up_level(place, received, box, box_low, box_high, skip_keep, skip_send, fine_cells):
    peers, _, samples, _, own, wide = received.shape
    c4 = peers * own
    c3 = box.shape[-1] // 9
    part = jax.ShapeDtypeStruct((9, c4 // 32 + skip_keep.shape[1], 16, c3), BF16)
    whole = pl.BlockSpec(part.shape, lambda s: (0, 0, 0, 0))
    skips = pl.BlockSpec(skip_keep.shape, lambda s: (0, 0, 0, 0))
    return pl.pallas_call(
        functools.partial(up_kernel, scale=1.0 / math.sqrt(fine_cells)),
        grid=(samples,),
        in_specs=[
            pl.BlockSpec(memory_space=pltpu.SMEM),
            pl.BlockSpec((peers, 1, 1, 2, own, wide), lambda s: (0, 0, s, 0, 0, 0)),
            pl.BlockSpec((1, wide, 9 * c3), lambda s: (s, 0, 0)),
            pl.BlockSpec((1, wide, 3 * c3), lambda s: (s, 0, 0)),
            pl.BlockSpec((1, wide, 3 * c3), lambda s: (s, 0, 0)),
            skips, skips,
        ],
        out_specs=[whole, whole],
        out_shape=[part, part],
        scratch_shapes=[pltpu.VMEM((c4, 9 * c3), F32)],
        compiler_params=params(VMEM),
        cost_estimate=cost(1e9, 5e6),
        name="up_level",
    )(place, received, box, box_low, box_high, skip_keep, skip_send)


def fill_coarse_taps(odd, rows, taps):
    wide, c4 = rows[0].shape

    def fill(order):
        for v, row in zip(order, rows):
            before, after = shifted(row.astype(F32))
            lines = slice(v * wide, (v + 1) * wide)
            taps[lines, :c4] = before.astype(BF16)
            taps[lines, c4 : 2 * c4] = row
            taps[lines, 2 * c4 :] = after.astype(BF16)

    count = len(rows)
    pl.when(odd)(lambda: fill(range(count - 1, -1, -1)))
    pl.when(jnp.logical_not(odd))(lambda: fill(range(count)))


def dot32(left, right):
    return jnp.dot(left, right, preferred_element_type=F32)


def own_weight_kernel(place_ref, input_ref, far_ref, near_ref, out_ref, taps):
    wide = input_ref.shape[-1]
    c4 = far_ref.shape[-1]

    @pl.when(pl.program_id(0) == 0)
    def _():
        out_ref[...] = jnp.zeros_like(out_ref)

    fill_coarse_taps(place_ref[0] >= 2, (far_ref[0], near_ref[0]), taps)
    first, second = (input_ref[:, 0, 0, i].reshape(c4, wide) for i in range(2))
    out_ref[0] += dot32(second, taps[:wide, :])
    out_ref[1] += dot32(jnp.concatenate([first, second], axis=1), taps[...])
    out_ref[2] += dot32(first, taps[wide:, :])


def own_weight_level(place, received, far, near):
    peers, _, samples, _, own, wide = received.shape
    c4 = peers * own
    row = pl.BlockSpec((1, wide, c4), lambda s: (s, 0, 0))
    return pl.pallas_call(
        own_weight_kernel,
        grid=(samples,),
        in_specs=[
            pl.BlockSpec(memory_space=pltpu.SMEM),
            pl.BlockSpec((peers, 1, 1, 2, own, wide), lambda s: (0, 1, s, 0, 0, 0)),
            row, row,
        ],
        out_specs=pl.BlockSpec((3, c4, 3 * c4), lambda s: (0, 0, 0)),
        out_shape=jax.ShapeDtypeStruct((3, c4, 3 * c4), F32),
        scratch_shapes=[pltpu.VMEM((2 * wide, 3 * c4), BF16)],
        compiler_params=params(VMEM),
        cost_estimate=cost(LONG, 4e6),
        name="own_weight_level",
    )(place, received, far, near)


def coarse_weight_kernel(place_ref, input_ref, from_far_ref, from_near_ref, own_ref, out_ref, taps, total, *, scale):
    sample = pl.program_id(0)
    wide = input_ref.shape[-1]
    part = input_ref.shape[0] * input_ref.shape[-2]
    c4 = from_far_ref.shape[-1]

    fill_coarse_taps(place_ref[0] >= 2, (from_far_ref[0], from_near_ref[0]), taps)
    terms = [dot32(input_ref[:, 0, 0, i].reshape(part, wide), taps[i * wide : (i + 1) * wide, :]) for i in range(2)]

    @pl.when(sample == 0)
    def _():
        for i, term in enumerate(terms):
            total[i] = term

    @pl.when(sample > 0)
    def _():
        for i, term in enumerate(terms):
            total[i] += term

    @pl.when(sample == pl.num_programs(0) - 1)
    def _():
        count = part // 16
        for dy in range(3):
            for d in range(3):
                for side in range(c4 // 128):
                    at = d * c4 + side * 128
                    value = own_ref[dy, :, at : at + 128]
                    if dy != 1:
                        value = value + total[dy // 2, :, at : at + 128]
                    tap = ((2 - dy) * 3 + 2 - d) * (c4 // 128) + side
                    out_ref[tap * count : (tap + 1) * count] = tiles(value * scale)


def coarse_weight_level(place, received, from_far, from_near, own_terms, coarse_cells):
    peers, _, samples, _, own, wide = received.shape
    c4 = peers * own
    shape = (9 * (c4 // 128) * (c4 // 32), 16, 128)
    row = pl.BlockSpec((1, wide, c4), lambda s, place: (s, 0, 0))
    return pl.pallas_call(
        functools.partial(coarse_weight_kernel, scale=1.0 / math.sqrt(coarse_cells)),
        grid_spec=pltpu.PrefetchScalarGridSpec(
            num_scalar_prefetch=1,
            grid=(samples,),
            in_specs=[
                pl.BlockSpec((peers // 2, 1, 1, 2, own, wide), lambda s, place: (place[0] % 2, 1, s, 0, 0, 0)),
                row, row,
                pl.BlockSpec((3, c4 // 2, 3 * c4), lambda s, place: (0, place[0] % 2, 0)),
            ],
            out_specs=pl.BlockSpec(shape, lambda s, place: (0, 0, 0)),
            scratch_shapes=[pltpu.VMEM((2 * wide, 3 * c4), BF16), pltpu.VMEM((2, c4 // 2, 3 * c4), F32)],
        ),
        out_shape=jax.ShapeDtypeStruct(shape, BF16),
        compiler_params=params(VMEM),
        cost_estimate=cost(0.4e9, 2e6),
        name="coarse_weight_level",
    )(place, received, from_far, from_near, own_terms)


def coarse_specs(wide, c4, count):
    return [pl.BlockSpec((1, wide, c4), lambda s: (s, 0, 0))] * count


def coarse_input_kernel(chan_ref, weight_ref, first_ref, second_ref, third_ref, fourth_ref, *rest):
    *piece_refs, taps, stage = rest
    wide, c4 = first_ref.shape[1:]
    own = c4 // len(piece_refs)
    rows = (first_ref[0], second_ref[0], third_ref[0], fourth_ref[0])
    fill_coarse_taps(chan_ref[0] % 2 == 1, rows, taps)
    total = None
    for dy in range(3):
        for d in range(3):
            window = taps[dy * wide : (dy + 2) * wide, d * c4 : (d + 1) * c4]
            term = dott(weight_ref[2 - dy, 2 - d], window)
            total = term if total is None else total + term
    stage[...] = total.astype(BF16)
    for k, ref in enumerate(piece_refs):
        at = pl.multiple_of(jnp.bitwise_xor(chan_ref[0], k) * own, own)
        for i in range(2):
            ref[0, i] = stage[pl.ds(at, own), i * wide : (i + 1) * wide]


def coarse_input_level(chan, weight, rows, peers):
    samples, wide, c4 = rows[0].shape
    own = c4 // peers
    return pl.pallas_call(
        coarse_input_kernel,
        grid=(samples,),
        in_specs=[
            pl.BlockSpec(memory_space=pltpu.SMEM),
            pl.BlockSpec(weight.shape, lambda s: (0, 0, 0, 0)),
        ] + coarse_specs(wide, c4, 4),
        out_specs=[pl.BlockSpec((1, 2, own, wide), lambda s: (s, 0, 0, 0))] * peers,
        out_shape=[jax.ShapeDtypeStruct((samples, 2, own, wide), BF16)] * peers,
        scratch_shapes=[pltpu.VMEM((4 * wide, 3 * c4), BF16), pltpu.VMEM((c4, 2 * wide), BF16)],
        compiler_params=params(VMEM),
        cost_estimate=cost(1.3e9, 3e6),
        name="coarse_input_level",
    )(chan, weight, *rows)


def place_kernel(partners, chan_ref, *refs):
    out_ref = refs[-1]
    if len(refs) > len(partners) + 1:
        out_ref[...] = refs[len(partners)][...]
    for k, ref in zip(partners, refs):
        at = jnp.bitwise_xor(chan_ref[0], k) * 2
        out_ref[:, pl.ds(at, 2)] = ref[...]


def placed(chan, pieces, partners, peers, earlier=(), flops=1e6):
    samples, rows, own, wide = pieces[0].shape
    vmem = pl.BlockSpec(memory_space=pltpu.VMEM)
    return pl.pallas_call(
        functools.partial(place_kernel, partners),
        in_specs=[pl.BlockSpec(memory_space=pltpu.SMEM)] + [vmem] * (len(pieces) + len(earlier)),
        out_shape=jax.ShapeDtypeStruct((samples, rows * peers, own, wide), BF16),
        compiler_params=params(VMEM),
        cost_estimate=cost(flops, 1e6),
        name="place",
    )(chan, *pieces, *earlier)


def join_kernel(first, *refs):
    *part_refs, out_ref, stage, sems = refs
    one, more = part_refs[:2]
    count = one.shape[0]
    copies = []
    for at in range(0, stage.shape[0], 36):
        size = min(36, stage.shape[0] - at)
        held = max(min(size, count - at), 0)
        if held:
            lines = slice(at, at + held)
            stage[lines] = (one[lines].astype(F32) + more[lines].astype(F32)).astype(BF16)
        if held < size:
            stage[at + held : at + size] = jnp.zeros((size - held,) + stage.shape[1:], BF16)
        copies.append(
            pltpu.make_async_copy(
                stage.at[pl.ds(at, size)], out_ref.at[pl.ds(first + at, size)], sems.at[len(copies)]
            )
        )
        copies[-1].start()
    for copy in copies:
        copy.wait()


def joined(one, more, first, size, total, earlier=()):
    hbm = pl.BlockSpec(memory_space=pltpu.HBM)
    vmem = pl.BlockSpec(memory_space=pltpu.VMEM)
    return pl.pallas_call(
        functools.partial(join_kernel, first),
        in_specs=[vmem, vmem] + [hbm] * len(earlier),
        out_specs=hbm,
        out_shape=jax.ShapeDtypeStruct((total, 16, 128), BF16),
        input_output_aliases={2: 0} if earlier else {},
        scratch_shapes=[pltpu.VMEM((size, 16, 128), BF16), pltpu.SemaphoreType.DMA((-(-size // 36),))],
        compiler_params=params(VMEM),
        cost_estimate=cost(1e6, 2e6),
        name="join",
    )(one, more, *earlier)


def sum_kernel(parts_ref, out_ref):
    total = parts_ref[0].astype(F32)
    for k in range(1, parts_ref.shape[0]):
        total = total + parts_ref[k].astype(F32)
    total = total.astype(BF16)
    for k in range(out_ref.shape[0]):
        out_ref[k] = total


def unpack_kernel(place_ref, parts_ref, *rest):
    fine_ref, coarse_ref, fine_stage, coarse_stage, sems = rest[-5:]
    c4 = coarse_ref.shape[-1]
    sides = c4 // 128
    lines, skips = c4 // 2, (fine_ref.shape[-2] - c4) // 2
    line_tiles, skip_tiles = lines // 16, skips // 16
    core = place_ref[0] % 2
    rows = pl.ds(pl.multiple_of(core * lines, lines), lines)
    skip_rows = pl.ds(pl.multiple_of(c4 + core * skips, skips), skips)

    def take(at, count):
        return parts_ref[at : at + count].astype(F32).reshape(count * 16, 128)

    copies = []

    def send(source, target):
        copies.append(pltpu.make_async_copy(source, target, sems.at[len(copies)]))
        copies[-1].start()

    for tap in range(9):
        for side in range(sides):
            at = (tap * sides + side) * line_tiles
            coarse_stage[tap, :, side * 128 : (side + 1) * 128] = take(at, line_tiles)
        send(coarse_stage.at[tap], coarse_ref.at[tap, rows])
        at = 9 * sides * line_tiles + tap * (line_tiles + skip_tiles)
        fine_stage[tap, :lines] = take(at, line_tiles)
        fine_stage[tap, lines:] = take(at + line_tiles, skip_tiles)
        send(fine_stage.at[tap, pl.ds(0, lines)], fine_ref.at[tap, rows])
        send(fine_stage.at[tap, pl.ds(lines, skips)], fine_ref.at[tap, skip_rows])
    for copy in copies:
        copy.wait()


SWAP = ((0, 1), (1, 0))


def grad_sums(parts, chips):
    each = parts.shape[0] // chips
    parts = lax.all_to_all(parts.reshape(chips, each, 16, 128), CHIPS, 0, 0, tiled=True)
    summed = pl.pallas_call(
        sum_kernel,
        out_shape=jax.ShapeDtypeStruct((chips, each, 16, 128), BF16),
        compiler_params=params(VMEM),
        cost_estimate=cost(1e6, 1.3e6),
        name="sum_parts",
    )(parts)
    return lax.all_to_all(summed, CHIPS, 0, 0, tiled=True).reshape(chips * each, 16, 128)


def unpacked(place, half, fine_shape, coarse_shape, earlier=()):
    shapes = [jax.ShapeDtypeStruct((9,) + shape[2:], F32) for shape in (fine_shape, coarse_shape)]
    hbm = pl.BlockSpec(memory_space=pltpu.HBM)
    return pl.pallas_call(
        unpack_kernel,
        in_specs=[pl.BlockSpec(memory_space=pltpu.SMEM), pl.BlockSpec(memory_space=pltpu.VMEM)]
        + [hbm] * len(earlier),
        out_specs=[hbm, hbm],
        out_shape=shapes,
        input_output_aliases={2 + i: i for i in range(len(earlier))},
        scratch_shapes=[
            pltpu.VMEM((9, fine_shape[2] // 2, fine_shape[3]), F32),
            pltpu.VMEM((9, coarse_shape[2] // 2, coarse_shape[3]), F32),
            pltpu.SemaphoreType.DMA((27,)),
        ],
        compiler_params=params(VMEM),
        cost_estimate=cost(1, 1),
        name="unpack",
    )(place, half, *earlier)


def start_kernel(
    place_ref, pre_ref, input_ref, cot_ref, fine_pre_ref, pieces_ref, near_ref, far_ref, rows, row_sems, sems
):
    peers, _, samples, lines, _, _ = pieces_ref.shape
    odd = place_ref[0] >= 2
    last = cot_ref.shape[1] - 1
    row_copies = []
    for a, ref in enumerate((cot_ref, fine_pre_ref)):
        for e, line in enumerate((jnp.where(odd, 0, last), jnp.where(odd, last, 0))):
            for s in range(samples):
                row_copies.append(
                    pltpu.make_async_copy(ref.at[s, line], rows.at[a, e, s], row_sems.at[len(row_copies)])
                )
    copies = []
    for c in range(peers):
        for a, ref in enumerate((pre_ref, input_ref)):
            for s in range(samples):
                copies.append(
                    pltpu.make_async_copy(
                        ref.at[s, pl.ds(c * lines, lines)], pieces_ref.at[c, a, s], sems.at[len(copies)]
                    )
                )
    for copy in row_copies + copies:
        copy.start()
    for copy in row_copies:
        copy.wait()
    for e, out_ref in enumerate((near_ref, far_ref)):
        for s in range(samples):
            grad = rows[0, e, s].astype(F32) * silu_grad(rows[1, e, s].astype(F32))
            out_ref[s] = grad.astype(BF16)
    for copy in copies:
        copy.wait()


def start_level(place, pre, values, cot, fine_pre, peers):
    samples, lines, own, wide = pre.shape
    fine_wide, c3 = cot.shape[2:]
    hbm = pl.BlockSpec(memory_space=pltpu.HBM)
    vmem = pl.BlockSpec(memory_space=pltpu.VMEM)
    edge = jax.ShapeDtypeStruct((samples, fine_wide, c3), BF16)
    return pl.pallas_call(
        start_kernel,
        in_specs=[pl.BlockSpec(memory_space=pltpu.SMEM), hbm, hbm, hbm, hbm],
        out_specs=[vmem, vmem, vmem],
        out_shape=[jax.ShapeDtypeStruct((peers, 2, samples, lines // peers, own, wide), BF16), edge, edge],
        scratch_shapes=[
            pltpu.VMEM((2, 2, samples, fine_wide, c3), BF16),
            pltpu.SemaphoreType.DMA((4 * samples,)),
            pltpu.SemaphoreType.DMA((peers * 2 * samples,)),
        ],
        compiler_params=params(VMEM),
        cost_estimate=cost(1e7, 3e6),
        name="start",
    )(place, *(in_hbm(a) for a in (pre, values, cot, fine_pre)))


def swapped(near, far):
    count = 1
    for axis in ALL:
        count *= lax.axis_size(axis)
    inside = [(i, i ^ 1) for i in range(count)]
    outside = [(i, i + 1) for i in range(1, count - 1, 2)]
    outside += [(target, source) for source, target in outside]
    return lax.ppermute(near, ALL, inside), lax.ppermute(far, ALL, outside)


def shards(coarse_input, coarse_pre, skip_feats, fine_pre, fine_cotangent, fine_weight, coarse_weight):
    peers = 1
    for axis in CHAN:
        peers *= lax.axis_size(axis)
    devices = peers
    for axis in ROWS:
        devices *= lax.axis_size(axis)
    samples, lines, wide, own = coarse_input.shape
    core = lax.axis_index("core").astype(jnp.int32)
    chan = lax.axis_index(CHAN).astype(jnp.int32).reshape(1)
    place = (core + 2 * (lax.axis_index("xl").astype(jnp.int32))).reshape(1)
    other_place = (1 - core + 2 * (lax.axis_index("xl").astype(jnp.int32))).reshape(1)

    pieces, edge_near, edge_far = start_level(
        place, coarse_pre.transpose(0, 1, 3, 2), coarse_input.transpose(0, 1, 3, 2), fine_cotangent, fine_pre, peers
    )
    edge_near, edge_far = swapped(edge_near, edge_far)
    received = lax.all_to_all(pieces, CHAN, 0, 0, tiled=True)

    cs = skip_feats.shape[-1]
    fine_cells = fine_pre.shape[0] * fine_pre.shape[1] * fine_pre.shape[2] * devices
    fine_grad, box, edge, pooled, up_weight = box_level(fine_cotangent, fine_pre, fine_weight, cs)
    pooled, box_low, box_high = edge_level(place, edge_near, edge_far, edge, pooled, up_weight)
    grad_skip, skip_keep, skip_send = fine_level(
        place, fine_grad, edge_near, edge_far, skip_feats, fine_weight, fine_cells
    )
    received, skip_keep, skip_send = lax.optimization_barrier((received, skip_keep, skip_send))
    near, far = coarse_grad(place, pooled, received)
    from_near, from_far = swapped(near, far)
    fine_keep, fine_send = up_level(place, received, box, box_low, box_high, skip_keep, skip_send, fine_cells)
    fine_more = lax.ppermute(fine_send, "core", SWAP)
    own_terms = own_weight_level(place, received, far, near)
    chips = devices // lax.axis_size("core")
    fine_keep, fine_more = (a.reshape((-1, 16, 128)) for a in (fine_keep, fine_more))
    coarse_count = 9 * (fine_weight.shape[2] - cs) ** 2 // (2 * 16 * 128)
    total = -(-(coarse_count + fine_keep.shape[0]) // chips) * chips
    sums = joined(fine_keep, fine_more, coarse_count, total - coarse_count, total)
    from_near, from_far, sums, own_terms = lax.optimization_barrier((from_near, from_far, sums, own_terms))
    rows = (from_far, far, near, from_near)
    coarse_cells = samples * (lines // peers) * wide * devices
    coarse_send = coarse_weight_level(other_place, received, from_far, from_near, own_terms, coarse_cells)
    coarse_more = lax.ppermute(coarse_send, "core", SWAP)
    coarse_keep = coarse_weight_level(place, received, from_far, from_near, own_terms, coarse_cells)
    back = coarse_input_level(chan, coarse_weight, rows, peers)

    def home(k, piece):
        return lax.ppermute(piece, CHAN, [(i, i ^ k) for i in range(peers)])

    sums = joined(coarse_keep, coarse_more, 0, coarse_count, total, (sums,))
    mine = grad_sums(sums, chips)
    early = [k for k in range(peers) if k not in LATE]
    grad_input = placed(chan, [home(k, back[k]) if k else back[k] for k in early], early, peers, flops=LONG)
    grad_input, *late = lax.optimization_barrier((grad_input, *(back[k] for k in LATE)))
    late = [home(k, piece) for k, piece in zip(LATE, late)]
    mine, grad_input = lax.optimization_barrier((mine, grad_input))
    grad_input = placed(chan, late, LATE, peers, (grad_input,), flops=LONG)
    other = lax.ppermute(mine, "core", SWAP)
    sums = unpacked(place, mine, fine_weight.shape, coarse_weight.shape)
    grad_fine, grad_coarse = unpacked(other_place, other, fine_weight.shape, coarse_weight.shape, sums)
    return (
        grad_skip,
        grad_input.transpose(0, 1, 3, 2),
        grad_fine.reshape(fine_weight.shape),
        grad_coarse.reshape(coarse_weight.shape),
    )


def solution(mesh):
    split = Mesh(mesh.devices.reshape([size for _, size in SPLIT]), tuple(name for name, _ in SPLIT))
    coarse = P(None, ROWS, None, CHAN)
    fine = P(None, ALL, None, None)
    return jax.shard_map(
        shards,
        mesh=split,
        in_specs=(coarse, coarse, fine, fine, fine, P(), P()),
        out_specs=(fine, coarse, P(), P()),
        check_vma=False,
    )
```

```python
import functools
import math

import jax
import jax.numpy as jnp
from jax import lax
from jax.experimental import pallas as pl
from jax.experimental.pallas import tpu as pltpu
from jax.sharding import Mesh
from jax.sharding import PartitionSpec as P

F32 = jnp.float32
BF16 = jnp.bfloat16
MIB = 1 << 20
VMEM = 18
LATE = (6, 7)
LONG = 1e11

SPLIT = (("xh", 2), ("z", 4), ("core", 2), ("y", 4), ("xl", 2))
ROWS = ("xh", "z", "core")
CHAN = ("y", "xl")
ALL = ROWS + CHAN
CHIPS = ("xh", "z", "y", "xl")


def params(limit):
    return pltpu.CompilerParams(vmem_limit_bytes=limit * MIB)


def cost(flops, nbytes):
    return pl.CostEstimate(flops=int(flops), bytes_accessed=int(nbytes), transcendentals=0)


def in_hbm(array):
    return pltpu.with_memory_space_constraint(array, pltpu.HBM)


def silu_grad(value):
    sigma = jax.nn.sigmoid(value)
    return sigma * (1.0 + value * (1.0 - sigma))


def shifted(field):
    extent = field.shape[0]
    index = lax.broadcasted_iota(jnp.int32, field.shape, 0)
    before = jnp.where(index == 0, 0.0, pltpu.roll(field, 1, 0))
    after = jnp.where(index == extent - 1, 0.0, pltpu.roll(field, extent - 1, 0))
    return before, after


def tdot(left, right):
    return lax.dot_general(left, right, (((0,), (0,)), ((), ())), preferred_element_type=F32)


def dott(left, right):
    return lax.dot_general(left, right, (((1,), (1,)), ((), ())), preferred_element_type=F32)


def tiles(block):
    return block.astype(BF16).reshape(block.shape[0] // 16, 16, block.shape[1])


def box_sums(upper, lower, half):
    even = upper[pl.ds(0, half, 2), :] + lower[pl.ds(0, half, 2), :]
    odd = upper[pl.ds(1, half, 2), :] + lower[pl.ds(1, half, 2), :]
    before, _ = shifted(odd)
    _, after = shifted(even)
    return (before + even).astype(BF16), (even + odd).astype(BF16), (odd + after).astype(BF16)


def box_kernel(cot_ref, pre_ref, weight_ref, grad_ref, box_ref, edge_ref, pooled_ref, up_weight, rows32):
    c3 = cot_ref.shape[-1]
    half = pooled_ref.shape[-2]
    reach = 3 * c3

    @pl.when(pl.program_id(0) == 0)
    def _():
        for dy in range(3):
            for d in range(3):
                at = (dy * 3 + d) * c3
                up_weight[at : at + c3, :] = weight_ref[2 - dy, 2 - d].astype(F32).T.astype(BF16)

    for v in range(4):
        grad = (cot_ref[0, v].astype(F32) * silu_grad(pre_ref[0, v].astype(F32))).astype(BF16)
        grad_ref[0, v] = grad
        rows32[v] = grad.astype(F32)
        if v % 3 == 0:
            edge_ref[0, v // 3] = grad
    for v in range(3):
        for d, value in enumerate(box_sums(rows32.at[v], rows32.at[v + 1], half)):
            at = v * reach + d * c3
            box_ref[0, :, at : at + c3] = value
    pooled_ref[0, 0] = jnp.dot(box_ref[0, :, : 2 * reach], up_weight[reach:, :], preferred_element_type=F32)
    pooled_ref[0, 1] = jnp.dot(box_ref[0, :, reach:], up_weight[: 2 * reach, :], preferred_element_type=F32)


def box_level(cot, pre, weight, cs):
    samples, height, wide, c3 = cot.shape
    c4 = weight.shape[2] - cs
    half = wide // 2
    block = pl.BlockSpec((1, height, wide, c3), lambda s: (s, 0, 0, 0))
    return pl.pallas_call(
        box_kernel,
        grid=(samples,),
        in_specs=[block, block, pl.BlockSpec((3, 3, c4, c3), lambda s: (0, 0, 0, 0))],
        out_specs=[
            block,
            pl.BlockSpec((1, half, 9 * c3), lambda s: (s, 0, 0)),
            pl.BlockSpec((1, 2, wide, c3), lambda s: (s, 0, 0, 0)),
            pl.BlockSpec((1, 2, half, c4), lambda s: (s, 0, 0, 0)),
            pl.BlockSpec((9 * c3, c4), lambda s: (0, 0)),
        ],
        out_shape=[
            pltpu.HBM((samples, height, wide, c3), BF16),
            pltpu.HBM((samples, half, 9 * c3), BF16),
            jax.ShapeDtypeStruct((samples, 2, wide, c3), BF16),
            jax.ShapeDtypeStruct((samples, 2, half, c4), F32),
            jax.ShapeDtypeStruct((9 * c3, c4), BF16),
        ],
        scratch_shapes=[pltpu.VMEM((height, wide, c3), F32)],
        compiler_params=params(VMEM),
        cost_estimate=cost(1.2e9, 8e6),
        name="box_level",
    )(in_hbm(cot), in_hbm(pre), in_hbm(weight))


def edge_kernel(
    place_ref, near_ref, far_ref, edge_ref, pooled_ref, low_weight_ref, high_weight_ref,
    out_ref, box_low_ref, box_high_ref, rows32,
):
    half = pooled_ref.shape[-2]
    c3 = edge_ref.shape[-1]
    odd = place_ref[0] >= 2
    near, far = near_ref[0].astype(F32), far_ref[0].astype(F32)
    sides = (
        (jnp.where(odd, near, far), edge_ref[0, 0].astype(F32), low_weight_ref, box_low_ref),
        (edge_ref[0, 1].astype(F32), jnp.where(odd, far, near), high_weight_ref, box_high_ref),
    )
    for i, (upper, lower, weight_ref, box_ref) in enumerate(sides):
        rows32[0] = upper
        rows32[1] = lower
        for d, value in enumerate(box_sums(rows32.at[0], rows32.at[1], half)):
            box_ref[0, :, d * c3 : (d + 1) * c3] = value
        out_ref[0, i] = pooled_ref[0, i] + jnp.dot(box_ref[0], weight_ref[...], preferred_element_type=F32)


def edge_level(place, near, far, edge, pooled, up_weight):
    samples, _, half, c4 = pooled.shape
    _, _, wide, c3 = edge.shape
    row = pl.BlockSpec((1, wide, c3), lambda s: (s, 0, 0))
    whole = pl.BlockSpec((1, 2, half, c4), lambda s: (s, 0, 0, 0))
    box_spec = pl.BlockSpec((1, half, 3 * c3), lambda s: (s, 0, 0))
    box = pltpu.HBM((samples, half, 3 * c3), BF16)
    return pl.pallas_call(
        edge_kernel,
        grid=(samples,),
        in_specs=[
            pl.BlockSpec(memory_space=pltpu.SMEM), row, row,
            pl.BlockSpec((1, 2, wide, c3), lambda s: (s, 0, 0, 0)), whole,
            pl.BlockSpec((3 * c3, c4), lambda s: (0, 0)),
            pl.BlockSpec((3 * c3, c4), lambda s: (2, 0)),
        ],
        out_specs=[whole, box_spec, box_spec],
        out_shape=[jax.ShapeDtypeStruct((samples, 2, half, c4), F32), box, box],
        scratch_shapes=[pltpu.VMEM((2, wide, c3), F32)],
        compiler_params=params(VMEM),
        cost_estimate=cost(LONG, 4e6),
        name="edge_level",
    )(place, near, far, edge, pooled, up_weight, up_weight)


def fine_kernel(
    place_ref, grad_ref, near_ref, far_ref, skip_ref, weight_ref, grad_skip_ref, keep_ref, send_ref, taps, skip_weight, total, *, scale
):
    sample = pl.program_id(0)
    odd = place_ref[0] >= 2
    c3 = grad_ref.shape[-1]
    cs = skip_ref.shape[-1]
    c4 = weight_ref.shape[2] - cs

    @pl.when(sample == 0)
    def _():
        total[...] = jnp.zeros_like(total)
        for u in range(4):
            for d in range(3):
                at = (u * 3 + d) * c3
                for t in range(2):
                    dy = u - t
                    if 0 <= dy <= 2:
                        block = weight_ref[2 - dy, 2 - d, c4:, :].astype(F32).T.astype(BF16)
                    else:
                        block = jnp.zeros((c3, cs), BF16)
                    skip_weight[at : at + c3, t * cs : (t + 1) * cs] = block

    for v in range(6):
        if v == 0:
            grad = jnp.where(odd, near_ref[0], far_ref[0])
        elif v == 5:
            grad = jnp.where(odd, far_ref[0], near_ref[0])
        else:
            grad = grad_ref[0, v - 1]
        before, after = shifted(grad.astype(F32))
        at = v * 3 * c3
        taps[:, at : at + c3] = before.astype(BF16)
        taps[:, at + c3 : at + 2 * c3] = grad
        taps[:, at + 2 * c3 : at + 3 * c3] = after.astype(BF16)

    for pair in range(2):
        window = taps[:, 2 * pair * 3 * c3 : (2 * pair + 4) * 3 * c3]
        back = jnp.dot(window, skip_weight[...], preferred_element_type=F32)
        grad_skip_ref[0, 2 * pair] = back[:, :cs].astype(BF16)
        grad_skip_ref[0, 2 * pair + 1] = back[:, cs:].astype(BF16)
        feats = jnp.concatenate([skip_ref[0, 2 * pair], skip_ref[0, 2 * pair + 1]], axis=1)
        total[...] += tdot(feats, window)

    @pl.when(sample == pl.num_programs(0) - 1)
    def _():
        core = place_ref[0] % 2

        part = cs // 2
        for dy in range(3):
            for d in range(3):
                first = (dy * 3 + d) * c3
                second = ((dy + 1) * 3 + d) * c3
                value = (total[:cs, first : first + c3] + total[cs:, second : second + c3]) * scale
                low, high = value[:part], value[part:]
                tap = (2 - dy) * 3 + 2 - d
                keep_ref[tap] = tiles(jnp.where(core == 0, low, high))
                send_ref[tap] = tiles(jnp.where(core == 0, high, low))


def fine_level(place, grad, near, far, skip, weight, fine_cells):
    samples, height, wide, cs = skip.shape
    c3 = grad.shape[-1]
    part = jax.ShapeDtypeStruct((9, cs // 32, 16, c3), BF16)
    whole = pl.BlockSpec(part.shape, lambda s: (0, 0, 0, 0))
    return pl.pallas_call(
        functools.partial(fine_kernel, scale=1.0 / math.sqrt(fine_cells)),
        grid=(samples,),
        in_specs=[
            pl.BlockSpec(memory_space=pltpu.SMEM),
            pl.BlockSpec((1, height, wide, c3), lambda s: (s, 0, 0, 0)),
            pl.BlockSpec((1, wide, c3), lambda s: (s, 0, 0)),
            pl.BlockSpec((1, wide, c3), lambda s: (s, 0, 0)),
            pl.BlockSpec((1, height, wide, cs), lambda s: (s, 0, 0, 0)),
            pl.BlockSpec(weight.shape, lambda s: (0, 0, 0, 0)),
        ],
        out_specs=[pl.BlockSpec((1, height, wide, cs), lambda s: (s, 0, 0, 0)), whole, whole],
        out_shape=[jax.ShapeDtypeStruct((samples, height, wide, cs), BF16), part, part],
        scratch_shapes=[
            pltpu.VMEM((wide, 18 * c3), BF16),
            pltpu.VMEM((12 * c3, 2 * cs), BF16),
            pltpu.VMEM((2 * cs, 12 * c3), F32),
        ],
        compiler_params=params(VMEM),
        cost_estimate=cost(5e9, 8e6),
        name="fine_level",
    )(place, in_hbm(grad), near, far, in_hbm(skip), in_hbm(weight))


def coarse_grad_kernel(place_ref, pooled_ref, pre_ref, near_ref, far_ref):
    channels, half = pooled_ref.shape[-1], pooled_ref.shape[-2]
    odd = place_ref[0] >= 2
    rows = []
    for i in range(2):
        value = pre_ref[:, 0, 0, i].reshape(channels, half).astype(F32).T
        rows.append((pooled_ref[0, i] * silu_grad(value)).astype(BF16))
    near_ref[0] = jnp.where(odd, rows[0], rows[1])
    far_ref[0] = jnp.where(odd, rows[1], rows[0])


def coarse_grad(place, pooled, received):
    samples, _, half, c4 = pooled.shape
    peers, _, _, _, own, _ = received.shape
    out = jax.ShapeDtypeStruct((samples, half, c4), BF16)
    spec = pl.BlockSpec((1, half, c4), lambda s: (s, 0, 0))
    return pl.pallas_call(
        coarse_grad_kernel,
        grid=(samples,),
        in_specs=[
            pl.BlockSpec(memory_space=pltpu.SMEM),
            pl.BlockSpec((1, 2, half, c4), lambda s: (s, 0, 0, 0)),
            pl.BlockSpec((peers, 1, 1, 2, own, half), lambda s: (0, 0, s, 0, 0, 0)),
        ],
        out_specs=[spec, spec],
        out_shape=[out, out],
        compiler_params=params(VMEM),
        cost_estimate=cost(2e7, 2e6),
        name="coarse_grad",
    )(place, pooled, received)


def up_kernel(
    place_ref, pre_ref, box_ref, box_low_ref, box_high_ref, skip_keep_ref, skip_send_ref, keep_ref, send_ref, total,
    *, scale
):
    sample = pl.program_id(0)
    wide = pre_ref.shape[-1]
    c4 = pre_ref.shape[0] * pre_ref.shape[-2]
    c3 = keep_ref.shape[-1]

    @pl.when(sample == 0)
    def _():
        total[...] = jnp.zeros_like(total)

    reach = 3 * c3
    windows = (
        ((0, box_low_ref[0]), (reach, box_ref[0, :, : 2 * reach])),
        ((0, box_ref[0, :, reach:]), (2 * reach, box_high_ref[0])),
    )
    for i in range(2):
        value = pre_ref[:, 0, 0, i].reshape(c4, wide).astype(F32)
        value = (value * jax.nn.sigmoid(value)).astype(BF16)
        for at, window in windows[i]:
            total[:, at : at + window.shape[1]] += jnp.dot(value, window, preferred_element_type=F32)

    @pl.when(sample == pl.num_programs(0) - 1)
    def _():
        core = place_ref[0] % 2
        part = c4 // 2
        mine = part // 16
        for dy in range(3):
            for d in range(3):
                at = (dy * 3 + d) * c3
                value = total[:, at : at + c3] * scale
                low, high = value[:part], value[part:]
                tap = (2 - dy) * 3 + 2 - d
                keep_ref[tap, :mine] = tiles(jnp.where(core == 0, low, high))
                send_ref[tap, :mine] = tiles(jnp.where(core == 0, high, low))
                keep_ref[tap, mine:] = skip_keep_ref[tap]
                send_ref[tap, mine:] = skip_send_ref[tap]


def up_level(place, received, box, box_low, box_high, skip_keep, skip_send, fine_cells):
    peers, _, samples, _, own, wide = received.shape
    c4 = peers * own
    c3 = box.shape[-1] // 9
    part = jax.ShapeDtypeStruct((9, c4 // 32 + skip_keep.shape[1], 16, c3), BF16)
    whole = pl.BlockSpec(part.shape, lambda s: (0, 0, 0, 0))
    skips = pl.BlockSpec(skip_keep.shape, lambda s: (0, 0, 0, 0))
    return pl.pallas_call(
        functools.partial(up_kernel, scale=1.0 / math.sqrt(fine_cells)),
        grid=(samples,),
        in_specs=[
            pl.BlockSpec(memory_space=pltpu.SMEM),
            pl.BlockSpec((peers, 1, 1, 2, own, wide), lambda s: (0, 0, s, 0, 0, 0)),
            pl.BlockSpec((1, wide, 9 * c3), lambda s: (s, 0, 0)),
            pl.BlockSpec((1, wide, 3 * c3), lambda s: (s, 0, 0)),
            pl.BlockSpec((1, wide, 3 * c3), lambda s: (s, 0, 0)),
            skips, skips,
        ],
        out_specs=[whole, whole],
        out_shape=[part, part],
        scratch_shapes=[pltpu.VMEM((c4, 9 * c3), F32)],
        compiler_params=params(VMEM),
        cost_estimate=cost(1e9, 5e6),
        name="up_level",
    )(place, received, box, box_low, box_high, skip_keep, skip_send)


def fill_coarse_taps(odd, rows, taps):
    wide, c4 = rows[0].shape

    def fill(order):
        for v, row in zip(order, rows):
            before, after = shifted(row.astype(F32))
            lines = slice(v * wide, (v + 1) * wide)
            taps[lines, :c4] = before.astype(BF16)
            taps[lines, c4 : 2 * c4] = row
            taps[lines, 2 * c4 :] = after.astype(BF16)

    count = len(rows)
    pl.when(odd)(lambda: fill(range(count - 1, -1, -1)))
    pl.when(jnp.logical_not(odd))(lambda: fill(range(count)))


def dot32(left, right):
    return jnp.dot(left, right, preferred_element_type=F32)


def own_weight_kernel(place_ref, input_ref, far_ref, near_ref, out_ref, taps):
    wide = input_ref.shape[-1]
    c4 = far_ref.shape[-1]

    @pl.when(pl.program_id(0) == 0)
    def _():
        out_ref[...] = jnp.zeros_like(out_ref)

    fill_coarse_taps(place_ref[0] >= 2, (far_ref[0], near_ref[0]), taps)
    first, second = (input_ref[:, 0, 0, i].reshape(c4, wide) for i in range(2))
    out_ref[0] += dot32(second, taps[:wide, :])
    out_ref[1] += dot32(jnp.concatenate([first, second], axis=1), taps[...])
    out_ref[2] += dot32(first, taps[wide:, :])


def own_weight_level(place, received, far, near):
    peers, _, samples, _, own, wide = received.shape
    c4 = peers * own
    row = pl.BlockSpec((1, wide, c4), lambda s: (s, 0, 0))
    return pl.pallas_call(
        own_weight_kernel,
        grid=(samples,),
        in_specs=[
            pl.BlockSpec(memory_space=pltpu.SMEM),
            pl.BlockSpec((peers, 1, 1, 2, own, wide), lambda s: (0, 1, s, 0, 0, 0)),
            row, row,
        ],
        out_specs=pl.BlockSpec((3, c4, 3 * c4), lambda s: (0, 0, 0)),
        out_shape=jax.ShapeDtypeStruct((3, c4, 3 * c4), F32),
        scratch_shapes=[pltpu.VMEM((2 * wide, 3 * c4), BF16)],
        compiler_params=params(VMEM),
        cost_estimate=cost(LONG, 4e6),
        name="own_weight_level",
    )(place, received, far, near)


def coarse_weight_kernel(place_ref, input_ref, from_far_ref, from_near_ref, own_ref, out_ref, taps, total, *, scale):
    sample = pl.program_id(0)
    wide = input_ref.shape[-1]
    part = input_ref.shape[0] * input_ref.shape[-2]
    c4 = from_far_ref.shape[-1]

    fill_coarse_taps(place_ref[0] >= 2, (from_far_ref[0], from_near_ref[0]), taps)
    terms = [dot32(input_ref[:, 0, 0, i].reshape(part, wide), taps[i * wide : (i + 1) * wide, :]) for i in range(2)]

    @pl.when(sample == 0)
    def _():
        for i, term in enumerate(terms):
            total[i] = term

    @pl.when(sample > 0)
    def _():
        for i, term in enumerate(terms):
            total[i] += term

    @pl.when(sample == pl.num_programs(0) - 1)
    def _():
        count = part // 16
        for dy in range(3):
            for d in range(3):
                for side in range(c4 // 128):
                    at = d * c4 + side * 128
                    value = own_ref[dy, :, at : at + 128]
                    if dy != 1:
                        value = value + total[dy // 2, :, at : at + 128]
                    tap = ((2 - dy) * 3 + 2 - d) * (c4 // 128) + side
                    out_ref[tap * count : (tap + 1) * count] = tiles(value * scale)


def coarse_weight_level(place, received, from_far, from_near, own_terms, coarse_cells):
    peers, _, samples, _, own, wide = received.shape
    c4 = peers * own
    shape = (9 * (c4 // 128) * (c4 // 32), 16, 128)
    row = pl.BlockSpec((1, wide, c4), lambda s, place: (s, 0, 0))
    return pl.pallas_call(
        functools.partial(coarse_weight_kernel, scale=1.0 / math.sqrt(coarse_cells)),
        grid_spec=pltpu.PrefetchScalarGridSpec(
            num_scalar_prefetch=1,
            grid=(samples,),
            in_specs=[
                pl.BlockSpec((peers // 2, 1, 1, 2, own, wide), lambda s, place: (place[0] % 2, 1, s, 0, 0, 0)),
                row, row,
                pl.BlockSpec((3, c4 // 2, 3 * c4), lambda s, place: (0, place[0] % 2, 0)),
            ],
            out_specs=pl.BlockSpec(shape, lambda s, place: (0, 0, 0)),
            scratch_shapes=[pltpu.VMEM((2 * wide, 3 * c4), BF16), pltpu.VMEM((2, c4 // 2, 3 * c4), F32)],
        ),
        out_shape=jax.ShapeDtypeStruct(shape, BF16),
        compiler_params=params(VMEM),
        cost_estimate=cost(0.4e9, 2e6),
        name="coarse_weight_level",
    )(place, received, from_far, from_near, own_terms)


def coarse_specs(wide, c4, count):
    return [pl.BlockSpec((1, wide, c4), lambda s: (s, 0, 0))] * count


def coarse_input_kernel(chan_ref, weight_ref, first_ref, second_ref, third_ref, fourth_ref, *rest):
    *piece_refs, taps, stage = rest
    wide, c4 = first_ref.shape[1:]
    own = c4 // len(piece_refs)
    rows = (first_ref[0], second_ref[0], third_ref[0], fourth_ref[0])
    fill_coarse_taps(chan_ref[0] % 2 == 1, rows, taps)
    total = None
    for dy in range(3):
        for d in range(3):
            window = taps[dy * wide : (dy + 2) * wide, d * c4 : (d + 1) * c4]
            term = dott(weight_ref[2 - dy, 2 - d], window)
            total = term if total is None else total + term
    stage[...] = total.astype(BF16)
    for k, ref in enumerate(piece_refs):
        at = pl.multiple_of(jnp.bitwise_xor(chan_ref[0], k) * own, own)
        for i in range(2):
            ref[0, i] = stage[pl.ds(at, own), i * wide : (i + 1) * wide]


def coarse_input_level(chan, weight, rows, peers):
    samples, wide, c4 = rows[0].shape
    own = c4 // peers
    return pl.pallas_call(
        coarse_input_kernel,
        grid=(samples,),
        in_specs=[
            pl.BlockSpec(memory_space=pltpu.SMEM),
            pl.BlockSpec(weight.shape, lambda s: (0, 0, 0, 0)),
        ] + coarse_specs(wide, c4, 4),
        out_specs=[pl.BlockSpec((1, 2, own, wide), lambda s: (s, 0, 0, 0))] * peers,
        out_shape=[jax.ShapeDtypeStruct((samples, 2, own, wide), BF16)] * peers,
        scratch_shapes=[pltpu.VMEM((4 * wide, 3 * c4), BF16), pltpu.VMEM((c4, 2 * wide), BF16)],
        compiler_params=params(VMEM),
        cost_estimate=cost(1.3e9, 3e6),
        name="coarse_input_level",
    )(chan, weight, *rows)


def place_kernel(partners, chan_ref, *refs):
    out_ref = refs[-1]
    if len(refs) > len(partners) + 1:
        out_ref[...] = refs[len(partners)][...]
    for k, ref in zip(partners, refs):
        at = jnp.bitwise_xor(chan_ref[0], k) * 2
        out_ref[:, pl.ds(at, 2)] = ref[...]


def placed(chan, pieces, partners, peers, earlier=(), flops=1e6):
    samples, rows, own, wide = pieces[0].shape
    vmem = pl.BlockSpec(memory_space=pltpu.VMEM)
    return pl.pallas_call(
        functools.partial(place_kernel, partners),
        in_specs=[pl.BlockSpec(memory_space=pltpu.SMEM)] + [vmem] * (len(pieces) + len(earlier)),
        out_shape=jax.ShapeDtypeStruct((samples, rows * peers, own, wide), BF16),
        compiler_params=params(VMEM),
        cost_estimate=cost(flops, 1e6),
        name="place",
    )(chan, *pieces, *earlier)


def join_kernel(first, *refs):
    *part_refs, out_ref, stage, sems = refs
    one, more = part_refs[:2]
    count = one.shape[0]
    copies = []
    for at in range(0, stage.shape[0], 36):
        size = min(36, stage.shape[0] - at)
        held = max(min(size, count - at), 0)
        if held:
            lines = slice(at, at + held)
            stage[lines] = (one[lines].astype(F32) + more[lines].astype(F32)).astype(BF16)
        if held < size:
            stage[at + held : at + size] = jnp.zeros((size - held,) + stage.shape[1:], BF16)
        copies.append(
            pltpu.make_async_copy(
                stage.at[pl.ds(at, size)], out_ref.at[pl.ds(first + at, size)], sems.at[len(copies)]
            )
        )
        copies[-1].start()
    for copy in copies:
        copy.wait()


def joined(one, more, first, size, total, earlier=()):
    hbm = pl.BlockSpec(memory_space=pltpu.HBM)
    vmem = pl.BlockSpec(memory_space=pltpu.VMEM)
    return pl.pallas_call(
        functools.partial(join_kernel, first),
        in_specs=[vmem, vmem] + [hbm] * len(earlier),
        out_specs=hbm,
        out_shape=jax.ShapeDtypeStruct((total, 16, 128), BF16),
        input_output_aliases={2: 0} if earlier else {},
        scratch_shapes=[pltpu.VMEM((size, 16, 128), BF16), pltpu.SemaphoreType.DMA((-(-size // 36),))],
        compiler_params=params(VMEM),
        cost_estimate=cost(1e6, 2e6),
        name="join",
    )(one, more, *earlier)


def sum_kernel(parts_ref, out_ref):
    total = parts_ref[0].astype(F32)
    for k in range(1, parts_ref.shape[0]):
        total = total + parts_ref[k].astype(F32)
    total = total.astype(BF16)
    for k in range(out_ref.shape[0]):
        out_ref[k] = total


def unpack_kernel(place_ref, parts_ref, *rest):
    fine_ref, coarse_ref, fine_stage, coarse_stage, sems = rest[-5:]
    c4 = coarse_ref.shape[-1]
    sides = c4 // 128
    lines, skips = c4 // 2, (fine_ref.shape[-2] - c4) // 2
    line_tiles, skip_tiles = lines // 16, skips // 16
    core = place_ref[0] % 2
    rows = pl.ds(pl.multiple_of(core * lines, lines), lines)
    skip_rows = pl.ds(pl.multiple_of(c4 + core * skips, skips), skips)

    def take(at, count):
        return parts_ref[at : at + count].astype(F32).reshape(count * 16, 128)

    copies = []

    def send(source, target):
        copies.append(pltpu.make_async_copy(source, target, sems.at[len(copies)]))
        copies[-1].start()

    for tap in range(9):
        for side in range(sides):
            at = (tap * sides + side) * line_tiles
            coarse_stage[tap, :, side * 128 : (side + 1) * 128] = take(at, line_tiles)
        send(coarse_stage.at[tap], coarse_ref.at[tap, rows])
        at = 9 * sides * line_tiles + tap * (line_tiles + skip_tiles)
        fine_stage[tap, :lines] = take(at, line_tiles)
        fine_stage[tap, lines:] = take(at + line_tiles, skip_tiles)
        send(fine_stage.at[tap, pl.ds(0, lines)], fine_ref.at[tap, rows])
        send(fine_stage.at[tap, pl.ds(lines, skips)], fine_ref.at[tap, skip_rows])
    for copy in copies:
        copy.wait()


SWAP = ((0, 1), (1, 0))


def grad_sums(parts, chips):
    each = parts.shape[0] // chips
    parts = lax.all_to_all(parts.reshape(chips, each, 16, 128), CHIPS, 0, 0, tiled=True)
    summed = pl.pallas_call(
        sum_kernel,
        out_shape=jax.ShapeDtypeStruct((chips, each, 16, 128), BF16),
        compiler_params=params(VMEM),
        cost_estimate=cost(1e6, 1.3e6),
        name="sum_parts",
    )(parts)
    return lax.all_to_all(summed, CHIPS, 0, 0, tiled=True).reshape(chips * each, 16, 128)


def unpacked(place, half, fine_shape, coarse_shape, earlier=()):
    shapes = [jax.ShapeDtypeStruct((9,) + shape[2:], F32) for shape in (fine_shape, coarse_shape)]
    hbm = pl.BlockSpec(memory_space=pltpu.HBM)
    return pl.pallas_call(
        unpack_kernel,
        in_specs=[pl.BlockSpec(memory_space=pltpu.SMEM), pl.BlockSpec(memory_space=pltpu.VMEM)]
        + [hbm] * len(earlier),
        out_specs=[hbm, hbm],
        out_shape=shapes,
        input_output_aliases={2 + i: i for i in range(len(earlier))},
        scratch_shapes=[
            pltpu.VMEM((9, fine_shape[2] // 2, fine_shape[3]), F32),
            pltpu.VMEM((9, coarse_shape[2] // 2, coarse_shape[3]), F32),
            pltpu.SemaphoreType.DMA((27,)),
        ],
        compiler_params=params(VMEM),
        cost_estimate=cost(1, 1),
        name="unpack",
    )(place, half, *earlier)


def start_kernel(place_ref, cot_ref, pre_ref, near_ref, far_ref, rows, sems):
    samples = cot_ref.shape[0]
    odd = place_ref[0] >= 2
    last = cot_ref.shape[1] - 1
    ends = (jnp.where(odd, 0, last), jnp.where(odd, last, 0))
    copies = [
        [
            pltpu.make_async_copy(ref.at[s, line], rows.at[a, e, s], sems.at[a, e, s])
            for a, ref in enumerate((cot_ref, pre_ref))
        ]
        for e, line in enumerate(ends) for s in range(samples)
    ]
    for pair in copies:
        for copy in pair:
            copy.start()
    for k, pair in enumerate(copies):
        for copy in pair:
            copy.wait()
        e, s = divmod(k, samples)
        grad = rows[0, e, s].astype(F32) * silu_grad(rows[1, e, s].astype(F32))
        (near_ref, far_ref)[e][s] = grad.astype(BF16)


def start_level(place, cot, fine_pre):
    samples, _, wide, c3 = cot.shape
    hbm = pl.BlockSpec(memory_space=pltpu.HBM)
    vmem = pl.BlockSpec(memory_space=pltpu.VMEM)
    edge = jax.ShapeDtypeStruct((samples, wide, c3), BF16)
    return pl.pallas_call(
        start_kernel,
        in_specs=[pl.BlockSpec(memory_space=pltpu.SMEM), hbm, hbm],
        out_specs=[vmem, vmem],
        out_shape=[edge, edge],
        scratch_shapes=[
            pltpu.VMEM((2, 2, samples, wide, c3), BF16),
            pltpu.SemaphoreType.DMA((2, 2, samples)),
        ],
        compiler_params=params(VMEM),
        cost_estimate=cost(1e7, 2e6),
        name="start",
    )(place, in_hbm(cot), in_hbm(fine_pre))


def swapped(near, far):
    count = 1
    for axis in ALL:
        count *= lax.axis_size(axis)
    inside = [(i, i ^ 1) for i in range(count)]
    outside = [(i, i + 1) for i in range(1, count - 1, 2)]
    outside += [(target, source) for source, target in outside]
    return lax.ppermute(near, ALL, inside), lax.ppermute(far, ALL, outside)


def shards(coarse_input, coarse_pre, skip_feats, fine_pre, fine_cotangent, fine_weight, coarse_weight):
    peers = 1
    for axis in CHAN:
        peers *= lax.axis_size(axis)
    devices = peers
    for axis in ROWS:
        devices *= lax.axis_size(axis)
    samples, lines, wide, own = coarse_input.shape
    core = lax.axis_index("core").astype(jnp.int32)
    chan = lax.axis_index(CHAN).astype(jnp.int32).reshape(1)
    place = (core + 2 * (lax.axis_index("xl").astype(jnp.int32))).reshape(1)
    other_place = (1 - core + 2 * (lax.axis_index("xl").astype(jnp.int32))).reshape(1)

    edge_near, edge_far = start_level(place, fine_cotangent, fine_pre)
    pieces = jnp.stack([coarse_pre, coarse_input]).reshape(2, samples, peers, lines // peers, wide, own)
    pieces = pieces.transpose(2, 0, 1, 3, 5, 4)
    edge_near, edge_far = swapped(edge_near, edge_far)
    received = lax.all_to_all(pieces, CHAN, 0, 0, tiled=True)

    cs = skip_feats.shape[-1]
    fine_cells = fine_pre.shape[0] * fine_pre.shape[1] * fine_pre.shape[2] * devices
    fine_grad, box, edge, pooled, up_weight = box_level(fine_cotangent, fine_pre, fine_weight, cs)
    pooled, box_low, box_high = edge_level(place, edge_near, edge_far, edge, pooled, up_weight)
    grad_skip, skip_keep, skip_send = fine_level(
        place, fine_grad, edge_near, edge_far, skip_feats, fine_weight, fine_cells
    )
    received, skip_keep, skip_send = lax.optimization_barrier((received, skip_keep, skip_send))
    near, far = coarse_grad(place, pooled, received)
    from_near, from_far = swapped(near, far)
    fine_keep, fine_send = up_level(place, received, box, box_low, box_high, skip_keep, skip_send, fine_cells)
    fine_more = lax.ppermute(fine_send, "core", SWAP)
    own_terms = own_weight_level(place, received, far, near)
    chips = devices // lax.axis_size("core")
    fine_keep, fine_more = (a.reshape((-1, 16, 128)) for a in (fine_keep, fine_more))
    coarse_count = 9 * (fine_weight.shape[2] - cs) ** 2 // (2 * 16 * 128)
    total = -(-(coarse_count + fine_keep.shape[0]) // chips) * chips
    sums = joined(fine_keep, fine_more, coarse_count, total - coarse_count, total)
    from_near, from_far, sums, own_terms = lax.optimization_barrier((from_near, from_far, sums, own_terms))
    rows = (from_far, far, near, from_near)
    coarse_cells = samples * (lines // peers) * wide * devices
    coarse_send = coarse_weight_level(other_place, received, from_far, from_near, own_terms, coarse_cells)
    coarse_more = lax.ppermute(coarse_send, "core", SWAP)
    coarse_keep = coarse_weight_level(place, received, from_far, from_near, own_terms, coarse_cells)
    back = coarse_input_level(chan, coarse_weight, rows, peers)

    def home(k, piece):
        return lax.ppermute(piece, CHAN, [(i, i ^ k) for i in range(peers)])

    sums = joined(coarse_keep, coarse_more, 0, coarse_count, total, (sums,))
    mine = grad_sums(sums, chips)
    early = [k for k in range(peers) if k not in LATE]
    grad_input = placed(chan, [home(k, back[k]) if k else back[k] for k in early], early, peers, flops=LONG)
    grad_input, *late = lax.optimization_barrier((grad_input, *(back[k] for k in LATE)))
    late = [home(k, piece) for k, piece in zip(LATE, late)]
    mine, grad_input = lax.optimization_barrier((mine, grad_input))
    grad_input = placed(chan, late, LATE, peers, (grad_input,), flops=LONG)
    other = lax.ppermute(mine, "core", SWAP)
    sums = unpacked(place, mine, fine_weight.shape, coarse_weight.shape)
    grad_fine, grad_coarse = unpacked(other_place, other, fine_weight.shape, coarse_weight.shape, sums)
    return (
        grad_skip,
        grad_input.transpose(0, 1, 3, 2),
        grad_fine.reshape(fine_weight.shape),
        grad_coarse.reshape(coarse_weight.shape),
    )


def solution(mesh):
    split = Mesh(mesh.devices.reshape([size for _, size in SPLIT]), tuple(name for name, _ in SPLIT))
    coarse = P(None, ROWS, None, CHAN)
    fine = P(None, ALL, None, None)
    return jax.shard_map(
        shards,
        mesh=split,
        in_specs=(coarse, coarse, fine, fine, fine, P(), P()),
        out_specs=(fine, coarse, P(), P()),
        check_vma=False,
    )
```

```python
import functools
import math

import jax
import jax.numpy as jnp
from jax import lax
from jax.experimental import pallas as pl
from jax.experimental.pallas import tpu as pltpu
from jax.sharding import Mesh
from jax.sharding import PartitionSpec as P

F32 = jnp.float32
BF16 = jnp.bfloat16
MIB = 1 << 20
VMEM = 18
LATE = (6, 7)
LONG = 1e11

SPLIT = (("xh", 2), ("z", 4), ("core", 2), ("y", 4), ("xl", 2))
ROWS = ("xh", "z", "core")
CHAN = ("y", "xl")
ALL = ROWS + CHAN
CHIPS = ("xh", "z", "y", "xl")


def params(limit):
    return pltpu.CompilerParams(vmem_limit_bytes=limit * MIB)


def cost(flops, nbytes):
    return pl.CostEstimate(flops=int(flops), bytes_accessed=int(nbytes), transcendentals=0)


def in_hbm(array):
    return pltpu.with_memory_space_constraint(array, pltpu.HBM)


def silu_grad(value):
    sigma = jax.nn.sigmoid(value)
    return sigma * (1.0 + value * (1.0 - sigma))


def shifted(field):
    extent = field.shape[0]
    index = lax.broadcasted_iota(jnp.int32, field.shape, 0)
    before = jnp.where(index == 0, 0.0, pltpu.roll(field, 1, 0))
    after = jnp.where(index == extent - 1, 0.0, pltpu.roll(field, extent - 1, 0))
    return before, after


def tdot(left, right):
    return lax.dot_general(left, right, (((0,), (0,)), ((), ())), preferred_element_type=F32)


def dott(left, right):
    return lax.dot_general(left, right, (((1,), (1,)), ((), ())), preferred_element_type=F32)


def tiles(block):
    return block.astype(BF16).reshape(block.shape[0] // 16, 16, block.shape[1])


def box_sums(upper, lower, half):
    even = upper[pl.ds(0, half, 2), :] + lower[pl.ds(0, half, 2), :]
    odd = upper[pl.ds(1, half, 2), :] + lower[pl.ds(1, half, 2), :]
    before, _ = shifted(odd)
    _, after = shifted(even)
    return (before + even).astype(BF16), (even + odd).astype(BF16), (odd + after).astype(BF16)


def box_kernel(cot_ref, pre_ref, weight_ref, grad_ref, box_ref, edge_ref, pooled_ref, up_weight, rows32):
    c3 = cot_ref.shape[-1]
    half = pooled_ref.shape[-2]
    reach = 3 * c3

    @pl.when(pl.program_id(0) == 0)
    def _():
        for dy in range(3):
            for d in range(3):
                at = (dy * 3 + d) * c3
                up_weight[at : at + c3, :] = weight_ref[2 - dy, 2 - d].astype(F32).T.astype(BF16)

    for v in range(4):
        grad = (cot_ref[0, v].astype(F32) * silu_grad(pre_ref[0, v].astype(F32))).astype(BF16)
        grad_ref[0, v] = grad
        rows32[v] = grad.astype(F32)
        if v % 3 == 0:
            edge_ref[0, v // 3] = grad
    for v in range(3):
        for d, value in enumerate(box_sums(rows32.at[v], rows32.at[v + 1], half)):
            at = v * reach + d * c3
            box_ref[0, :, at : at + c3] = value
    pooled_ref[0, 0] = jnp.dot(box_ref[0, :, : 2 * reach], up_weight[reach:, :], preferred_element_type=F32)
    pooled_ref[0, 1] = jnp.dot(box_ref[0, :, reach:], up_weight[: 2 * reach, :], preferred_element_type=F32)


def box_level(cot, pre, weight, cs):
    samples, height, wide, c3 = cot.shape
    c4 = weight.shape[2] - cs
    half = wide // 2
    block = pl.BlockSpec((1, height, wide, c3), lambda s: (s, 0, 0, 0))
    return pl.pallas_call(
        box_kernel,
        grid=(samples,),
        in_specs=[block, block, pl.BlockSpec((3, 3, c4, c3), lambda s: (0, 0, 0, 0))],
        out_specs=[
            block,
            pl.BlockSpec((1, half, 9 * c3), lambda s: (s, 0, 0)),
            pl.BlockSpec((1, 2, wide, c3), lambda s: (s, 0, 0, 0)),
            pl.BlockSpec((1, 2, half, c4), lambda s: (s, 0, 0, 0)),
            pl.BlockSpec((9 * c3, c4), lambda s: (0, 0)),
        ],
        out_shape=[
            pltpu.HBM((samples, height, wide, c3), BF16),
            pltpu.HBM((samples, half, 9 * c3), BF16),
            jax.ShapeDtypeStruct((samples, 2, wide, c3), BF16),
            jax.ShapeDtypeStruct((samples, 2, half, c4), F32),
            jax.ShapeDtypeStruct((9 * c3, c4), BF16),
        ],
        scratch_shapes=[pltpu.VMEM((height, wide, c3), F32)],
        compiler_params=params(VMEM),
        cost_estimate=cost(1.2e9, 8e6),
        name="box_level",
    )(in_hbm(cot), in_hbm(pre), in_hbm(weight))


def edge_kernel(
    place_ref, near_ref, far_ref, edge_ref, pooled_ref, low_weight_ref, high_weight_ref,
    out_ref, box_low_ref, box_high_ref, rows32,
):
    half = pooled_ref.shape[-2]
    c3 = edge_ref.shape[-1]
    odd = place_ref[0] >= 2
    near, far = near_ref[0].astype(F32), far_ref[0].astype(F32)
    sides = (
        (jnp.where(odd, near, far), edge_ref[0, 0].astype(F32), low_weight_ref, box_low_ref),
        (edge_ref[0, 1].astype(F32), jnp.where(odd, far, near), high_weight_ref, box_high_ref),
    )
    for i, (upper, lower, weight_ref, box_ref) in enumerate(sides):
        rows32[0] = upper
        rows32[1] = lower
        for d, value in enumerate(box_sums(rows32.at[0], rows32.at[1], half)):
            box_ref[0, :, d * c3 : (d + 1) * c3] = value
        out_ref[0, i] = pooled_ref[0, i] + jnp.dot(box_ref[0], weight_ref[...], preferred_element_type=F32)


def edge_level(place, near, far, edge, pooled, up_weight):
    samples, _, half, c4 = pooled.shape
    _, _, wide, c3 = edge.shape
    row = pl.BlockSpec((1, wide, c3), lambda s: (s, 0, 0))
    whole = pl.BlockSpec((1, 2, half, c4), lambda s: (s, 0, 0, 0))
    box_spec = pl.BlockSpec((1, half, 3 * c3), lambda s: (s, 0, 0))
    box = pltpu.HBM((samples, half, 3 * c3), BF16)
    return pl.pallas_call(
        edge_kernel,
        grid=(samples,),
        in_specs=[
            pl.BlockSpec(memory_space=pltpu.SMEM), row, row,
            pl.BlockSpec((1, 2, wide, c3), lambda s: (s, 0, 0, 0)), whole,
            pl.BlockSpec((3 * c3, c4), lambda s: (0, 0)),
            pl.BlockSpec((3 * c3, c4), lambda s: (2, 0)),
        ],
        out_specs=[whole, box_spec, box_spec],
        out_shape=[jax.ShapeDtypeStruct((samples, 2, half, c4), F32), box, box],
        scratch_shapes=[pltpu.VMEM((2, wide, c3), F32)],
        compiler_params=params(VMEM),
        cost_estimate=cost(LONG, 4e6),
        name="edge_level",
    )(place, near, far, edge, pooled, up_weight, up_weight)


def fine_kernel(
    place_ref, grad_ref, near_ref, far_ref, skip_ref, weight_ref, grad_skip_ref, keep_ref, send_ref, taps, skip_weight, total, *, scale
):
    sample = pl.program_id(0)
    odd = place_ref[0] >= 2
    c3 = grad_ref.shape[-1]
    cs = skip_ref.shape[-1]
    c4 = weight_ref.shape[2] - cs

    @pl.when(sample == 0)
    def _():
        total[...] = jnp.zeros_like(total)
        for u in range(4):
            for d in range(3):
                at = (u * 3 + d) * c3
                for t in range(2):
                    dy = u - t
                    if 0 <= dy <= 2:
                        block = weight_ref[2 - dy, 2 - d, c4:, :].astype(F32).T.astype(BF16)
                    else:
                        block = jnp.zeros((c3, cs), BF16)
                    skip_weight[at : at + c3, t * cs : (t + 1) * cs] = block

    for v in range(6):
        if v == 0:
            grad = jnp.where(odd, near_ref[0], far_ref[0])
        elif v == 5:
            grad = jnp.where(odd, far_ref[0], near_ref[0])
        else:
            grad = grad_ref[0, v - 1]
        before, after = shifted(grad.astype(F32))
        at = v * 3 * c3
        taps[:, at : at + c3] = before.astype(BF16)
        taps[:, at + c3 : at + 2 * c3] = grad
        taps[:, at + 2 * c3 : at + 3 * c3] = after.astype(BF16)

    for pair in range(2):
        window = taps[:, 2 * pair * 3 * c3 : (2 * pair + 4) * 3 * c3]
        back = jnp.dot(window, skip_weight[...], preferred_element_type=F32)
        grad_skip_ref[0, 2 * pair] = back[:, :cs].astype(BF16)
        grad_skip_ref[0, 2 * pair + 1] = back[:, cs:].astype(BF16)
        feats = jnp.concatenate([skip_ref[0, 2 * pair], skip_ref[0, 2 * pair + 1]], axis=1)
        total[...] += tdot(feats, window)

    @pl.when(sample == pl.num_programs(0) - 1)
    def _():
        core = place_ref[0] % 2

        part = cs // 2
        for dy in range(3):
            for d in range(3):
                first = (dy * 3 + d) * c3
                second = ((dy + 1) * 3 + d) * c3
                value = (total[:cs, first : first + c3] + total[cs:, second : second + c3]) * scale
                low, high = value[:part], value[part:]
                tap = (2 - dy) * 3 + 2 - d
                keep_ref[tap] = tiles(jnp.where(core == 0, low, high))
                send_ref[tap] = tiles(jnp.where(core == 0, high, low))


def fine_level(place, grad, near, far, skip, weight, fine_cells):
    samples, height, wide, cs = skip.shape
    c3 = grad.shape[-1]
    part = jax.ShapeDtypeStruct((9, cs // 32, 16, c3), BF16)
    whole = pl.BlockSpec(part.shape, lambda s: (0, 0, 0, 0))
    return pl.pallas_call(
        functools.partial(fine_kernel, scale=1.0 / math.sqrt(fine_cells)),
        grid=(samples,),
        in_specs=[
            pl.BlockSpec(memory_space=pltpu.SMEM),
            pl.BlockSpec((1, height, wide, c3), lambda s: (s, 0, 0, 0)),
            pl.BlockSpec((1, wide, c3), lambda s: (s, 0, 0)),
            pl.BlockSpec((1, wide, c3), lambda s: (s, 0, 0)),
            pl.BlockSpec((1, height, wide, cs), lambda s: (s, 0, 0, 0)),
            pl.BlockSpec(weight.shape, lambda s: (0, 0, 0, 0)),
        ],
        out_specs=[pl.BlockSpec((1, height, wide, cs), lambda s: (s, 0, 0, 0)), whole, whole],
        out_shape=[jax.ShapeDtypeStruct((samples, height, wide, cs), BF16), part, part],
        scratch_shapes=[
            pltpu.VMEM((wide, 18 * c3), BF16),
            pltpu.VMEM((12 * c3, 2 * cs), BF16),
            pltpu.VMEM((2 * cs, 12 * c3), F32),
        ],
        compiler_params=params(VMEM),
        cost_estimate=cost(5e9, 8e6),
        name="fine_level",
    )(place, in_hbm(grad), near, far, in_hbm(skip), in_hbm(weight))


def coarse_grad_kernel(place_ref, pooled_ref, pre_ref, near_ref, far_ref):
    channels, half = pooled_ref.shape[-1], pooled_ref.shape[-2]
    odd = place_ref[0] >= 2
    rows = []
    for i in range(2):
        value = pre_ref[:, 0, 0, i].reshape(channels, half).astype(F32).T
        rows.append((pooled_ref[0, i] * silu_grad(value)).astype(BF16))
    near_ref[0] = jnp.where(odd, rows[0], rows[1])
    far_ref[0] = jnp.where(odd, rows[1], rows[0])


def coarse_grad(place, pooled, received):
    samples, _, half, c4 = pooled.shape
    peers, _, _, _, own, _ = received.shape
    out = jax.ShapeDtypeStruct((samples, half, c4), BF16)
    spec = pl.BlockSpec((1, half, c4), lambda s: (s, 0, 0))
    return pl.pallas_call(
        coarse_grad_kernel,
        grid=(samples,),
        in_specs=[
            pl.BlockSpec(memory_space=pltpu.SMEM),
            pl.BlockSpec((1, 2, half, c4), lambda s: (s, 0, 0, 0)),
            pl.BlockSpec((peers, 1, 1, 2, own, half), lambda s: (0, 0, s, 0, 0, 0)),
        ],
        out_specs=[spec, spec],
        out_shape=[out, out],
        compiler_params=params(VMEM),
        cost_estimate=cost(2e7, 2e6),
        name="coarse_grad",
    )(place, pooled, received)


def up_kernel(
    place_ref, pre_ref, box_ref, box_low_ref, box_high_ref, skip_keep_ref, skip_send_ref, keep_ref, send_ref, total,
    *, scale
):
    sample = pl.program_id(0)
    wide = pre_ref.shape[-1]
    c4 = pre_ref.shape[0] * pre_ref.shape[-2]
    c3 = keep_ref.shape[-1]

    @pl.when(sample == 0)
    def _():
        total[...] = jnp.zeros_like(total)

    reach = 3 * c3
    windows = (
        ((0, box_low_ref[0]), (reach, box_ref[0, :, : 2 * reach])),
        ((0, box_ref[0, :, reach:]), (2 * reach, box_high_ref[0])),
    )
    for i in range(2):
        value = pre_ref[:, 0, 0, i].reshape(c4, wide).astype(F32)
        value = (value * jax.nn.sigmoid(value)).astype(BF16)
        for at, window in windows[i]:
            total[:, at : at + window.shape[1]] += jnp.dot(value, window, preferred_element_type=F32)

    @pl.when(sample == pl.num_programs(0) - 1)
    def _():
        core = place_ref[0] % 2
        part = c4 // 2
        mine = part // 16
        for dy in range(3):
            for d in range(3):
                at = (dy * 3 + d) * c3
                value = total[:, at : at + c3] * scale
                low, high = value[:part], value[part:]
                tap = (2 - dy) * 3 + 2 - d
                keep_ref[tap, :mine] = tiles(jnp.where(core == 0, low, high))
                send_ref[tap, :mine] = tiles(jnp.where(core == 0, high, low))
                keep_ref[tap, mine:] = skip_keep_ref[tap]
                send_ref[tap, mine:] = skip_send_ref[tap]


def up_level(place, received, box, box_low, box_high, skip_keep, skip_send, fine_cells):
    peers, _, samples, _, own, wide = received.shape
    c4 = peers * own
    c3 = box.shape[-1] // 9
    part = jax.ShapeDtypeStruct((9, c4 // 32 + skip_keep.shape[1], 16, c3), BF16)
    whole = pl.BlockSpec(part.shape, lambda s: (0, 0, 0, 0))
    skips = pl.BlockSpec(skip_keep.shape, lambda s: (0, 0, 0, 0))
    return pl.pallas_call(
        functools.partial(up_kernel, scale=1.0 / math.sqrt(fine_cells)),
        grid=(samples,),
        in_specs=[
            pl.BlockSpec(memory_space=pltpu.SMEM),
            pl.BlockSpec((peers, 1, 1, 2, own, wide), lambda s: (0, 0, s, 0, 0, 0)),
            pl.BlockSpec((1, wide, 9 * c3), lambda s: (s, 0, 0)),
            pl.BlockSpec((1, wide, 3 * c3), lambda s: (s, 0, 0)),
            pl.BlockSpec((1, wide, 3 * c3), lambda s: (s, 0, 0)),
            skips, skips,
        ],
        out_specs=[whole, whole],
        out_shape=[part, part],
        scratch_shapes=[pltpu.VMEM((c4, 9 * c3), F32)],
        compiler_params=params(VMEM),
        cost_estimate=cost(1e9, 5e6),
        name="up_level",
    )(place, received, box, box_low, box_high, skip_keep, skip_send)


def fill_coarse_taps(odd, rows, taps):
    wide, c4 = rows[0].shape

    def fill(order):
        for v, row in zip(order, rows):
            before, after = shifted(row.astype(F32))
            lines = slice(v * wide, (v + 1) * wide)
            taps[lines, :c4] = before.astype(BF16)
            taps[lines, c4 : 2 * c4] = row
            taps[lines, 2 * c4 :] = after.astype(BF16)

    count = len(rows)
    pl.when(odd)(lambda: fill(range(count - 1, -1, -1)))
    pl.when(jnp.logical_not(odd))(lambda: fill(range(count)))


def dot32(left, right):
    return jnp.dot(left, right, preferred_element_type=F32)


def own_weight_kernel(place_ref, input_ref, far_ref, near_ref, out_ref, taps):
    wide = input_ref.shape[-1]
    c4 = far_ref.shape[-1]

    @pl.when(pl.program_id(0) == 0)
    def _():
        out_ref[...] = jnp.zeros_like(out_ref)

    fill_coarse_taps(place_ref[0] >= 2, (far_ref[0], near_ref[0]), taps)
    first, second = (input_ref[:, 0, 0, i].reshape(c4, wide) for i in range(2))
    out_ref[0] += dot32(second, taps[:wide, :])
    out_ref[1] += dot32(jnp.concatenate([first, second], axis=1), taps[...])
    out_ref[2] += dot32(first, taps[wide:, :])


def own_weight_level(place, received, far, near):
    peers, _, samples, _, own, wide = received.shape
    c4 = peers * own
    row = pl.BlockSpec((1, wide, c4), lambda s: (s, 0, 0))
    return pl.pallas_call(
        own_weight_kernel,
        grid=(samples,),
        in_specs=[
            pl.BlockSpec(memory_space=pltpu.SMEM),
            pl.BlockSpec((peers, 1, 1, 2, own, wide), lambda s: (0, 1, s, 0, 0, 0)),
            row, row,
        ],
        out_specs=pl.BlockSpec((3, c4, 3 * c4), lambda s: (0, 0, 0)),
        out_shape=jax.ShapeDtypeStruct((3, c4, 3 * c4), F32),
        scratch_shapes=[pltpu.VMEM((2 * wide, 3 * c4), BF16)],
        compiler_params=params(VMEM),
        cost_estimate=cost(LONG, 4e6),
        name="own_weight_level",
    )(place, received, far, near)


def coarse_weight_kernel(place_ref, input_ref, from_far_ref, from_near_ref, own_ref, out_ref, taps, total, *, scale):
    sample = pl.program_id(0)
    wide = input_ref.shape[-1]
    part = input_ref.shape[0] * input_ref.shape[-2]
    c4 = from_far_ref.shape[-1]

    fill_coarse_taps(place_ref[0] >= 2, (from_far_ref[0], from_near_ref[0]), taps)
    terms = [dot32(input_ref[:, 0, 0, i].reshape(part, wide), taps[i * wide : (i + 1) * wide, :]) for i in range(2)]

    @pl.when(sample == 0)
    def _():
        for i, term in enumerate(terms):
            total[i] = term

    @pl.when(sample > 0)
    def _():
        for i, term in enumerate(terms):
            total[i] += term

    @pl.when(sample == pl.num_programs(0) - 1)
    def _():
        count = part // 16
        for dy in range(3):
            for d in range(3):
                for side in range(c4 // 128):
                    at = d * c4 + side * 128
                    value = own_ref[dy, :, at : at + 128]
                    if dy != 1:
                        value = value + total[dy // 2, :, at : at + 128]
                    tap = ((2 - dy) * 3 + 2 - d) * (c4 // 128) + side
                    out_ref[tap * count : (tap + 1) * count] = tiles(value * scale)


def coarse_weight_level(place, received, from_far, from_near, own_terms, coarse_cells):
    peers, _, samples, _, own, wide = received.shape
    c4 = peers * own
    shape = (9 * (c4 // 128) * (c4 // 32), 16, 128)
    row = pl.BlockSpec((1, wide, c4), lambda s, place: (s, 0, 0))
    return pl.pallas_call(
        functools.partial(coarse_weight_kernel, scale=1.0 / math.sqrt(coarse_cells)),
        grid_spec=pltpu.PrefetchScalarGridSpec(
            num_scalar_prefetch=1,
            grid=(samples,),
            in_specs=[
                pl.BlockSpec((peers // 2, 1, 1, 2, own, wide), lambda s, place: (place[0] % 2, 1, s, 0, 0, 0)),
                row, row,
                pl.BlockSpec((3, c4 // 2, 3 * c4), lambda s, place: (0, place[0] % 2, 0)),
            ],
            out_specs=pl.BlockSpec(shape, lambda s, place: (0, 0, 0)),
            scratch_shapes=[pltpu.VMEM((2 * wide, 3 * c4), BF16), pltpu.VMEM((2, c4 // 2, 3 * c4), F32)],
        ),
        out_shape=jax.ShapeDtypeStruct(shape, BF16),
        compiler_params=params(VMEM),
        cost_estimate=cost(0.4e9, 2e6),
        name="coarse_weight_level",
    )(place, received, from_far, from_near, own_terms)


def coarse_specs(wide, c4, count):
    return [pl.BlockSpec((1, wide, c4), lambda s: (s, 0, 0))] * count


def coarse_input_kernel(chan_ref, weight_ref, first_ref, second_ref, third_ref, fourth_ref, *rest):
    *piece_refs, taps, stage = rest
    wide, c4 = first_ref.shape[1:]
    own = c4 // len(piece_refs)
    rows = (first_ref[0], second_ref[0], third_ref[0], fourth_ref[0])
    fill_coarse_taps(chan_ref[0] % 2 == 1, rows, taps)
    total = None
    for dy in range(3):
        for d in range(3):
            window = taps[dy * wide : (dy + 2) * wide, d * c4 : (d + 1) * c4]
            term = dott(weight_ref[2 - dy, 2 - d], window)
            total = term if total is None else total + term
    stage[...] = total.astype(BF16)
    for k, ref in enumerate(piece_refs):
        at = pl.multiple_of(jnp.bitwise_xor(chan_ref[0], k) * own, own)
        for i in range(2):
            ref[0, i] = stage[pl.ds(at, own), i * wide : (i + 1) * wide]


def coarse_input_level(chan, weight, rows, peers):
    samples, wide, c4 = rows[0].shape
    own = c4 // peers
    return pl.pallas_call(
        coarse_input_kernel,
        grid=(samples,),
        in_specs=[
            pl.BlockSpec(memory_space=pltpu.SMEM),
            pl.BlockSpec(weight.shape, lambda s: (0, 0, 0, 0)),
        ] + coarse_specs(wide, c4, 4),
        out_specs=[pl.BlockSpec((1, 2, own, wide), lambda s: (s, 0, 0, 0))] * peers,
        out_shape=[jax.ShapeDtypeStruct((samples, 2, own, wide), BF16)] * peers,
        scratch_shapes=[pltpu.VMEM((4 * wide, 3 * c4), BF16), pltpu.VMEM((c4, 2 * wide), BF16)],
        compiler_params=params(VMEM),
        cost_estimate=cost(1.3e9, 3e6),
        name="coarse_input_level",
    )(chan, weight, *rows)


def place_kernel(partners, chan_ref, *refs):
    out_ref = refs[-1]
    if len(refs) > len(partners) + 1:
        out_ref[...] = refs[len(partners)][...]
    for k, ref in zip(partners, refs):
        at = jnp.bitwise_xor(chan_ref[0], k) * 2
        out_ref[:, pl.ds(at, 2)] = ref[...]


def placed(chan, pieces, partners, peers, earlier=(), flops=1e6):
    samples, rows, own, wide = pieces[0].shape
    vmem = pl.BlockSpec(memory_space=pltpu.VMEM)
    return pl.pallas_call(
        functools.partial(place_kernel, partners),
        in_specs=[pl.BlockSpec(memory_space=pltpu.SMEM)] + [vmem] * (len(pieces) + len(earlier)),
        out_shape=jax.ShapeDtypeStruct((samples, rows * peers, own, wide), BF16),
        compiler_params=params(VMEM),
        cost_estimate=cost(flops, 1e6),
        name="place",
    )(chan, *pieces, *earlier)


def join_kernel(first, *refs):
    *part_refs, out_ref, stage, sems = refs
    one, more = part_refs[:2]
    count = one.shape[0]
    copies = []
    for at in range(0, stage.shape[0], 36):
        size = min(36, stage.shape[0] - at)
        held = max(min(size, count - at), 0)
        if held:
            lines = slice(at, at + held)
            stage[lines] = (one[lines].astype(F32) + more[lines].astype(F32)).astype(BF16)
        if held < size:
            stage[at + held : at + size] = jnp.zeros((size - held,) + stage.shape[1:], BF16)
        copies.append(
            pltpu.make_async_copy(
                stage.at[pl.ds(at, size)], out_ref.at[pl.ds(first + at, size)], sems.at[len(copies)]
            )
        )
        copies[-1].start()
    for copy in copies:
        copy.wait()


def joined(one, more, first, size, total, earlier=()):
    hbm = pl.BlockSpec(memory_space=pltpu.HBM)
    vmem = pl.BlockSpec(memory_space=pltpu.VMEM)
    return pl.pallas_call(
        functools.partial(join_kernel, first),
        in_specs=[vmem, vmem] + [hbm] * len(earlier),
        out_specs=hbm,
        out_shape=jax.ShapeDtypeStruct((total, 16, 128), BF16),
        input_output_aliases={2: 0} if earlier else {},
        scratch_shapes=[pltpu.VMEM((size, 16, 128), BF16), pltpu.SemaphoreType.DMA((-(-size // 36),))],
        compiler_params=params(VMEM),
        cost_estimate=cost(1e6, 2e6),
        name="join",
    )(one, more, *earlier)


def sum_kernel(parts_ref, out_ref):
    total = parts_ref[0].astype(F32)
    for k in range(1, parts_ref.shape[0]):
        total = total + parts_ref[k].astype(F32)
    total = total.astype(BF16)
    for k in range(out_ref.shape[0]):
        out_ref[k] = total


def unpack_kernel(place_ref, parts_ref, *rest):
    fine_ref, coarse_ref, fine_stage, coarse_stage, sems = rest[-5:]
    c4 = coarse_ref.shape[-1]
    sides = c4 // 128
    lines, skips = c4 // 2, (fine_ref.shape[-2] - c4) // 2
    line_tiles, skip_tiles = lines // 16, skips // 16
    core = place_ref[0] % 2
    rows = pl.ds(pl.multiple_of(core * lines, lines), lines)
    skip_rows = pl.ds(pl.multiple_of(c4 + core * skips, skips), skips)

    def take(at, count):
        return parts_ref[at : at + count].astype(F32).reshape(count * 16, 128)

    copies = []

    def send(source, target):
        copies.append(pltpu.make_async_copy(source, target, sems.at[len(copies)]))
        copies[-1].start()

    for tap in range(9):
        for side in range(sides):
            at = (tap * sides + side) * line_tiles
            coarse_stage[tap, :, side * 128 : (side + 1) * 128] = take(at, line_tiles)
        send(coarse_stage.at[tap], coarse_ref.at[tap, rows])
        at = 9 * sides * line_tiles + tap * (line_tiles + skip_tiles)
        fine_stage[tap, :lines] = take(at, line_tiles)
        fine_stage[tap, lines:] = take(at + line_tiles, skip_tiles)
        send(fine_stage.at[tap, pl.ds(0, lines)], fine_ref.at[tap, rows])
        send(fine_stage.at[tap, pl.ds(lines, skips)], fine_ref.at[tap, skip_rows])
    for copy in copies:
        copy.wait()


SWAP = ((0, 1), (1, 0))


def grad_sums(parts, chips):
    each = parts.shape[0] // chips
    parts = lax.all_to_all(parts.reshape(chips, each, 16, 128), CHIPS, 0, 0, tiled=True)
    summed = pl.pallas_call(
        sum_kernel,
        out_shape=jax.ShapeDtypeStruct((chips, each, 16, 128), BF16),
        compiler_params=params(VMEM),
        cost_estimate=cost(1e6, 1.3e6),
        name="sum_parts",
    )(parts)
    return lax.all_to_all(summed, CHIPS, 0, 0, tiled=True).reshape(chips * each, 16, 128)


def unpacked(place, half, fine_shape, coarse_shape, earlier=()):
    shapes = [jax.ShapeDtypeStruct((9,) + shape[2:], F32) for shape in (fine_shape, coarse_shape)]
    hbm = pl.BlockSpec(memory_space=pltpu.HBM)
    return pl.pallas_call(
        unpack_kernel,
        in_specs=[pl.BlockSpec(memory_space=pltpu.SMEM), pl.BlockSpec(memory_space=pltpu.VMEM)]
        + [hbm] * len(earlier),
        out_specs=[hbm, hbm],
        out_shape=shapes,
        input_output_aliases={2 + i: i for i in range(len(earlier))},
        scratch_shapes=[
            pltpu.VMEM((9, fine_shape[2] // 2, fine_shape[3]), F32),
            pltpu.VMEM((9, coarse_shape[2] // 2, coarse_shape[3]), F32),
            pltpu.SemaphoreType.DMA((27,)),
        ],
        compiler_params=params(VMEM),
        cost_estimate=cost(1, 1),
        name="unpack",
    )(place, half, *earlier)


def start_kernel(place_ref, cot_ref, pre_ref, near_ref, far_ref, rows, sems):
    samples = cot_ref.shape[0]
    odd = place_ref[0] >= 2
    last = cot_ref.shape[1] - 1
    ends = (jnp.where(odd, 0, last), jnp.where(odd, last, 0))
    copies = [
        [
            pltpu.make_async_copy(ref.at[s, line], rows.at[a, e, s], sems.at[a, e, s])
            for a, ref in enumerate((cot_ref, pre_ref))
        ]
        for e, line in enumerate(ends) for s in range(samples)
    ]
    for pair in copies:
        for copy in pair:
            copy.start()
    for k, pair in enumerate(copies):
        for copy in pair:
            copy.wait()
        e, s = divmod(k, samples)
        grad = rows[0, e, s].astype(F32) * silu_grad(rows[1, e, s].astype(F32))
        (near_ref, far_ref)[e][s] = grad.astype(BF16)


def start_level(place, cot, fine_pre):
    samples, _, wide, c3 = cot.shape
    hbm = pl.BlockSpec(memory_space=pltpu.HBM)
    vmem = pl.BlockSpec(memory_space=pltpu.VMEM)
    edge = jax.ShapeDtypeStruct((samples, wide, c3), BF16)
    return pl.pallas_call(
        start_kernel,
        in_specs=[pl.BlockSpec(memory_space=pltpu.SMEM), hbm, hbm],
        out_specs=[vmem, vmem],
        out_shape=[edge, edge],
        scratch_shapes=[
            pltpu.VMEM((2, 2, samples, wide, c3), BF16),
            pltpu.SemaphoreType.DMA((2, 2, samples)),
        ],
        compiler_params=params(VMEM),
        cost_estimate=cost(1e7, 2e6),
        name="start",
    )(place, in_hbm(cot), in_hbm(fine_pre))


def swapped(near, far):
    count = 1
    for axis in ALL:
        count *= lax.axis_size(axis)
    inside = [(i, i ^ 1) for i in range(count)]
    outside = [(i, i + 1) for i in range(1, count - 1, 2)]
    outside += [(target, source) for source, target in outside]
    return lax.ppermute(near, ALL, inside), lax.ppermute(far, ALL, outside)


def shards(coarse_input, coarse_pre, skip_feats, fine_pre, fine_cotangent, fine_weight, coarse_weight):
    peers = 1
    for axis in CHAN:
        peers *= lax.axis_size(axis)
    devices = peers
    for axis in ROWS:
        devices *= lax.axis_size(axis)
    samples, lines, wide, own = coarse_input.shape
    core = lax.axis_index("core").astype(jnp.int32)
    chan = lax.axis_index(CHAN).astype(jnp.int32).reshape(1)
    place = (core + 2 * (lax.axis_index("xl").astype(jnp.int32))).reshape(1)
    other_place = (1 - core + 2 * (lax.axis_index("xl").astype(jnp.int32))).reshape(1)

    edge_near, edge_far = start_level(place, fine_cotangent, fine_pre)
    pieces = jnp.stack([coarse_pre, coarse_input]).reshape(2, samples, peers, lines // peers, wide, own)
    pieces = pieces.transpose(2, 0, 1, 3, 5, 4)
    pieces, edge_far = lax.optimization_barrier((pieces, edge_far))
    edge_near, edge_far = swapped(edge_near, edge_far)
    received = lax.all_to_all(pieces, CHAN, 0, 0, tiled=True)

    cs = skip_feats.shape[-1]
    fine_cells = fine_pre.shape[0] * fine_pre.shape[1] * fine_pre.shape[2] * devices
    fine_grad, box, edge, pooled, up_weight = box_level(fine_cotangent, fine_pre, fine_weight, cs)
    pooled, box_low, box_high = edge_level(place, edge_near, edge_far, edge, pooled, up_weight)
    grad_skip, skip_keep, skip_send = fine_level(
        place, fine_grad, edge_near, edge_far, skip_feats, fine_weight, fine_cells
    )
    received, skip_keep, skip_send = lax.optimization_barrier((received, skip_keep, skip_send))
    near, far = coarse_grad(place, pooled, received)
    from_near, from_far = swapped(near, far)
    fine_keep, fine_send = up_level(place, received, box, box_low, box_high, skip_keep, skip_send, fine_cells)
    fine_more = lax.ppermute(fine_send, "core", SWAP)
    own_terms = own_weight_level(place, received, far, near)
    chips = devices // lax.axis_size("core")
    fine_keep, fine_more = (a.reshape((-1, 16, 128)) for a in (fine_keep, fine_more))
    coarse_count = 9 * (fine_weight.shape[2] - cs) ** 2 // (2 * 16 * 128)
    total = -(-(coarse_count + fine_keep.shape[0]) // chips) * chips
    sums = joined(fine_keep, fine_more, coarse_count, total - coarse_count, total)
    from_near, from_far, sums, own_terms = lax.optimization_barrier((from_near, from_far, sums, own_terms))
    rows = (from_far, far, near, from_near)
    coarse_cells = samples * (lines // peers) * wide * devices
    coarse_send = coarse_weight_level(other_place, received, from_far, from_near, own_terms, coarse_cells)
    coarse_more = lax.ppermute(coarse_send, "core", SWAP)
    coarse_keep = coarse_weight_level(place, received, from_far, from_near, own_terms, coarse_cells)
    back = coarse_input_level(chan, coarse_weight, rows, peers)

    def home(k, piece):
        return lax.ppermute(piece, CHAN, [(i, i ^ k) for i in range(peers)])

    sums = joined(coarse_keep, coarse_more, 0, coarse_count, total, (sums,))
    mine = grad_sums(sums, chips)
    early = [k for k in range(peers) if k not in LATE]
    grad_input = placed(chan, [home(k, back[k]) if k else back[k] for k in early], early, peers, flops=LONG)
    grad_input, *late = lax.optimization_barrier((grad_input, *(back[k] for k in LATE)))
    late = [home(k, piece) for k, piece in zip(LATE, late)]
    mine, grad_input = lax.optimization_barrier((mine, grad_input))
    grad_input = placed(chan, late, LATE, peers, (grad_input,), flops=LONG)
    other = lax.ppermute(mine, "core", SWAP)
    sums = unpacked(place, mine, fine_weight.shape, coarse_weight.shape)
    grad_fine, grad_coarse = unpacked(other_place, other, fine_weight.shape, coarse_weight.shape, sums)
    return (
        grad_skip,
        grad_input.transpose(0, 1, 3, 2),
        grad_fine.reshape(fine_weight.shape),
        grad_coarse.reshape(coarse_weight.shape),
    )


def solution(mesh):
    split = Mesh(mesh.devices.reshape([size for _, size in SPLIT]), tuple(name for name, _ in SPLIT))
    coarse = P(None, ROWS, None, CHAN)
    fine = P(None, ALL, None, None)
    return jax.shard_map(
        shards,
        mesh=split,
        in_specs=(coarse, coarse, fine, fine, fine, P(), P()),
        out_specs=(fine, coarse, P(), P()),
        check_vma=False,
    )
```

```python
import functools
import math

import jax
import jax.numpy as jnp
from jax import lax
from jax.experimental import pallas as pl
from jax.experimental.pallas import tpu as pltpu
from jax.sharding import Mesh
from jax.sharding import PartitionSpec as P

F32 = jnp.float32
BF16 = jnp.bfloat16
MIB = 1 << 20
VMEM = 18
LATE = (2, 6)
LONG = 1e11

SPLIT = (("xh", 2), ("z", 4), ("core", 2), ("y", 4), ("xl", 2))
ROWS = ("xh", "z", "core")
CHAN = ("y", "xl")
ALL = ROWS + CHAN
CHIPS = ("xh", "z", "y", "xl")


def params(limit):
    return pltpu.CompilerParams(vmem_limit_bytes=limit * MIB)


def cost(flops, nbytes):
    return pl.CostEstimate(flops=int(flops), bytes_accessed=int(nbytes), transcendentals=0)


def in_hbm(array):
    return pltpu.with_memory_space_constraint(array, pltpu.HBM)


def silu_grad(value):
    sigma = jax.nn.sigmoid(value)
    return sigma * (1.0 + value * (1.0 - sigma))


def shifted(field):
    extent = field.shape[0]
    index = lax.broadcasted_iota(jnp.int32, field.shape, 0)
    before = jnp.where(index == 0, 0.0, pltpu.roll(field, 1, 0))
    after = jnp.where(index == extent - 1, 0.0, pltpu.roll(field, extent - 1, 0))
    return before, after


def tdot(left, right):
    return lax.dot_general(left, right, (((0,), (0,)), ((), ())), preferred_element_type=F32)


def dott(left, right):
    return lax.dot_general(left, right, (((1,), (1,)), ((), ())), preferred_element_type=F32)


def tiles(block):
    return block.astype(BF16).reshape(block.shape[0] // 16, 16, block.shape[1])


def box_sums(upper, lower, half):
    even = upper[pl.ds(0, half, 2), :] + lower[pl.ds(0, half, 2), :]
    odd = upper[pl.ds(1, half, 2), :] + lower[pl.ds(1, half, 2), :]
    before, _ = shifted(odd)
    _, after = shifted(even)
    return (before + even).astype(BF16), (even + odd).astype(BF16), (odd + after).astype(BF16)


def box_kernel(cot_ref, pre_ref, weight_ref, grad_ref, box_ref, edge_ref, pooled_ref, up_weight, rows32):
    c3 = cot_ref.shape[-1]
    half = pooled_ref.shape[-2]
    reach = 3 * c3

    @pl.when(pl.program_id(0) == 0)
    def _():
        for dy in range(3):
            for d in range(3):
                at = (dy * 3 + d) * c3
                up_weight[at : at + c3, :] = weight_ref[2 - dy, 2 - d].astype(F32).T.astype(BF16)

    for v in range(4):
        grad = (cot_ref[0, v].astype(F32) * silu_grad(pre_ref[0, v].astype(F32))).astype(BF16)
        grad_ref[0, v] = grad
        rows32[v] = grad.astype(F32)
        if v % 3 == 0:
            edge_ref[0, v // 3] = grad
    for v in range(3):
        for d, value in enumerate(box_sums(rows32.at[v], rows32.at[v + 1], half)):
            at = v * reach + d * c3
            box_ref[0, :, at : at + c3] = value
    pooled_ref[0, 0] = jnp.dot(box_ref[0, :, : 2 * reach], up_weight[reach:, :], preferred_element_type=F32)
    pooled_ref[0, 1] = jnp.dot(box_ref[0, :, reach:], up_weight[: 2 * reach, :], preferred_element_type=F32)


def box_level(cot, pre, weight, cs):
    samples, height, wide, c3 = cot.shape
    c4 = weight.shape[2] - cs
    half = wide // 2
    block = pl.BlockSpec((1, height, wide, c3), lambda s: (s, 0, 0, 0))
    return pl.pallas_call(
        box_kernel,
        grid=(samples,),
        in_specs=[block, block, pl.BlockSpec((3, 3, c4, c3), lambda s: (0, 0, 0, 0))],
        out_specs=[
            block,
            pl.BlockSpec((1, half, 9 * c3), lambda s: (s, 0, 0)),
            pl.BlockSpec((1, 2, wide, c3), lambda s: (s, 0, 0, 0)),
            pl.BlockSpec((1, 2, half, c4), lambda s: (s, 0, 0, 0)),
            pl.BlockSpec((9 * c3, c4), lambda s: (0, 0)),
        ],
        out_shape=[
            pltpu.HBM((samples, height, wide, c3), BF16),
            pltpu.HBM((samples, half, 9 * c3), BF16),
            jax.ShapeDtypeStruct((samples, 2, wide, c3), BF16),
            jax.ShapeDtypeStruct((samples, 2, half, c4), F32),
            jax.ShapeDtypeStruct((9 * c3, c4), BF16),
        ],
        scratch_shapes=[pltpu.VMEM((height, wide, c3), F32)],
        compiler_params=params(VMEM),
        cost_estimate=cost(1.2e9, 8e6),
        name="box_level",
    )(in_hbm(cot), in_hbm(pre), in_hbm(weight))


def edge_kernel(
    place_ref, near_ref, far_ref, edge_ref, pooled_ref, low_weight_ref, high_weight_ref,
    out_ref, box_low_ref, box_high_ref, rows32,
):
    half = pooled_ref.shape[-2]
    c3 = edge_ref.shape[-1]
    odd = place_ref[0] >= 2
    near, far = near_ref[0].astype(F32), far_ref[0].astype(F32)
    sides = (
        (jnp.where(odd, near, far), edge_ref[0, 0].astype(F32), low_weight_ref, box_low_ref),
        (edge_ref[0, 1].astype(F32), jnp.where(odd, far, near), high_weight_ref, box_high_ref),
    )
    for i, (upper, lower, weight_ref, box_ref) in enumerate(sides):
        rows32[0] = upper
        rows32[1] = lower
        for d, value in enumerate(box_sums(rows32.at[0], rows32.at[1], half)):
            box_ref[0, :, d * c3 : (d + 1) * c3] = value
        out_ref[0, i] = pooled_ref[0, i] + jnp.dot(box_ref[0], weight_ref[...], preferred_element_type=F32)


def edge_level(place, near, far, edge, pooled, up_weight):
    samples, _, half, c4 = pooled.shape
    _, _, wide, c3 = edge.shape
    row = pl.BlockSpec((1, wide, c3), lambda s: (s, 0, 0))
    whole = pl.BlockSpec((1, 2, half, c4), lambda s: (s, 0, 0, 0))
    box_spec = pl.BlockSpec((1, half, 3 * c3), lambda s: (s, 0, 0))
    box = pltpu.HBM((samples, half, 3 * c3), BF16)
    return pl.pallas_call(
        edge_kernel,
        grid=(samples,),
        in_specs=[
            pl.BlockSpec(memory_space=pltpu.SMEM), row, row,
            pl.BlockSpec((1, 2, wide, c3), lambda s: (s, 0, 0, 0)), whole,
            pl.BlockSpec((3 * c3, c4), lambda s: (0, 0)),
            pl.BlockSpec((3 * c3, c4), lambda s: (2, 0)),
        ],
        out_specs=[whole, box_spec, box_spec],
        out_shape=[jax.ShapeDtypeStruct((samples, 2, half, c4), F32), box, box],
        scratch_shapes=[pltpu.VMEM((2, wide, c3), F32)],
        compiler_params=params(VMEM),
        cost_estimate=cost(LONG, 4e6),
        name="edge_level",
    )(place, near, far, edge, pooled, up_weight, up_weight)


def fine_kernel(
    place_ref, grad_ref, near_ref, far_ref, skip_ref, weight_ref, grad_skip_ref, keep_ref, send_ref, taps, skip_weight, total, *, scale
):
    sample = pl.program_id(0)
    odd = place_ref[0] >= 2
    c3 = grad_ref.shape[-1]
    cs = skip_ref.shape[-1]
    c4 = weight_ref.shape[2] - cs

    @pl.when(sample == 0)
    def _():
        total[...] = jnp.zeros_like(total)
        for u in range(4):
            for d in range(3):
                at = (u * 3 + d) * c3
                for t in range(2):
                    dy = u - t
                    if 0 <= dy <= 2:
                        block = weight_ref[2 - dy, 2 - d, c4:, :].astype(F32).T.astype(BF16)
                    else:
                        block = jnp.zeros((c3, cs), BF16)
                    skip_weight[at : at + c3, t * cs : (t + 1) * cs] = block

    for v in range(6):
        if v == 0:
            grad = jnp.where(odd, near_ref[0], far_ref[0])
        elif v == 5:
            grad = jnp.where(odd, far_ref[0], near_ref[0])
        else:
            grad = grad_ref[0, v - 1]
        before, after = shifted(grad.astype(F32))
        at = v * 3 * c3
        taps[:, at : at + c3] = before.astype(BF16)
        taps[:, at + c3 : at + 2 * c3] = grad
        taps[:, at + 2 * c3 : at + 3 * c3] = after.astype(BF16)

    for pair in range(2):
        window = taps[:, 2 * pair * 3 * c3 : (2 * pair + 4) * 3 * c3]
        back = jnp.dot(window, skip_weight[...], preferred_element_type=F32)
        grad_skip_ref[0, 2 * pair] = back[:, :cs].astype(BF16)
        grad_skip_ref[0, 2 * pair + 1] = back[:, cs:].astype(BF16)
        feats = jnp.concatenate([skip_ref[0, 2 * pair], skip_ref[0, 2 * pair + 1]], axis=1)
        total[...] += tdot(feats, window)

    @pl.when(sample == pl.num_programs(0) - 1)
    def _():
        core = place_ref[0] % 2

        part = cs // 2
        for dy in range(3):
            for d in range(3):
                first = (dy * 3 + d) * c3
                second = ((dy + 1) * 3 + d) * c3
                value = (total[:cs, first : first + c3] + total[cs:, second : second + c3]) * scale
                low, high = value[:part], value[part:]
                tap = (2 - dy) * 3 + 2 - d
                keep_ref[tap] = tiles(jnp.where(core == 0, low, high))
                send_ref[tap] = tiles(jnp.where(core == 0, high, low))


def fine_level(place, grad, near, far, skip, weight, fine_cells):
    samples, height, wide, cs = skip.shape
    c3 = grad.shape[-1]
    part = jax.ShapeDtypeStruct((9, cs // 32, 16, c3), BF16)
    whole = pl.BlockSpec(part.shape, lambda s: (0, 0, 0, 0))
    return pl.pallas_call(
        functools.partial(fine_kernel, scale=1.0 / math.sqrt(fine_cells)),
        grid=(samples,),
        in_specs=[
            pl.BlockSpec(memory_space=pltpu.SMEM),
            pl.BlockSpec((1, height, wide, c3), lambda s: (s, 0, 0, 0)),
            pl.BlockSpec((1, wide, c3), lambda s: (s, 0, 0)),
            pl.BlockSpec((1, wide, c3), lambda s: (s, 0, 0)),
            pl.BlockSpec((1, height, wide, cs), lambda s: (s, 0, 0, 0)),
            pl.BlockSpec(weight.shape, lambda s: (0, 0, 0, 0)),
        ],
        out_specs=[pl.BlockSpec((1, height, wide, cs), lambda s: (s, 0, 0, 0)), whole, whole],
        out_shape=[jax.ShapeDtypeStruct((samples, height, wide, cs), BF16), part, part],
        scratch_shapes=[
            pltpu.VMEM((wide, 18 * c3), BF16),
            pltpu.VMEM((12 * c3, 2 * cs), BF16),
            pltpu.VMEM((2 * cs, 12 * c3), F32),
        ],
        compiler_params=params(VMEM),
        cost_estimate=cost(5e9, 8e6),
        name="fine_level",
    )(place, in_hbm(grad), near, far, in_hbm(skip), in_hbm(weight))


def coarse_grad_kernel(place_ref, pooled_ref, pre_ref, near_ref, far_ref):
    channels, half = pooled_ref.shape[-1], pooled_ref.shape[-2]
    odd = place_ref[0] >= 2
    rows = []
    for i in range(2):
        value = pre_ref[:, 0, 0, i].reshape(channels, half).astype(F32).T
        rows.append((pooled_ref[0, i] * silu_grad(value)).astype(BF16))
    near_ref[0] = jnp.where(odd, rows[0], rows[1])
    far_ref[0] = jnp.where(odd, rows[1], rows[0])


def coarse_grad(place, pooled, received):
    samples, _, half, c4 = pooled.shape
    peers, _, _, _, own, _ = received.shape
    out = jax.ShapeDtypeStruct((samples, half, c4), BF16)
    spec = pl.BlockSpec((1, half, c4), lambda s: (s, 0, 0))
    return pl.pallas_call(
        coarse_grad_kernel,
        grid=(samples,),
        in_specs=[
            pl.BlockSpec(memory_space=pltpu.SMEM),
            pl.BlockSpec((1, 2, half, c4), lambda s: (s, 0, 0, 0)),
            pl.BlockSpec((peers, 1, 1, 2, own, half), lambda s: (0, 0, s, 0, 0, 0)),
        ],
        out_specs=[spec, spec],
        out_shape=[out, out],
        compiler_params=params(VMEM),
        cost_estimate=cost(2e7, 2e6),
        name="coarse_grad",
    )(place, pooled, received)


def up_kernel(
    place_ref, pre_ref, box_ref, box_low_ref, box_high_ref, skip_keep_ref, skip_send_ref, keep_ref, send_ref, total,
    *, scale
):
    sample = pl.program_id(0)
    wide = pre_ref.shape[-1]
    c4 = pre_ref.shape[0] * pre_ref.shape[-2]
    c3 = keep_ref.shape[-1]

    @pl.when(sample == 0)
    def _():
        total[...] = jnp.zeros_like(total)

    reach = 3 * c3
    windows = (
        ((0, box_low_ref[0]), (reach, box_ref[0, :, : 2 * reach])),
        ((0, box_ref[0, :, reach:]), (2 * reach, box_high_ref[0])),
    )
    for i in range(2):
        value = pre_ref[:, 0, 0, i].reshape(c4, wide).astype(F32)
        value = (value * jax.nn.sigmoid(value)).astype(BF16)
        for at, window in windows[i]:
            total[:, at : at + window.shape[1]] += jnp.dot(value, window, preferred_element_type=F32)

    @pl.when(sample == pl.num_programs(0) - 1)
    def _():
        core = place_ref[0] % 2
        part = c4 // 2
        mine = part // 16
        for dy in range(3):
            for d in range(3):
                at = (dy * 3 + d) * c3
                value = total[:, at : at + c3] * scale
                low, high = value[:part], value[part:]
                tap = (2 - dy) * 3 + 2 - d
                keep_ref[tap, :mine] = tiles(jnp.where(core == 0, low, high))
                send_ref[tap, :mine] = tiles(jnp.where(core == 0, high, low))
                keep_ref[tap, mine:] = skip_keep_ref[tap]
                send_ref[tap, mine:] = skip_send_ref[tap]


def up_level(place, received, box, box_low, box_high, skip_keep, skip_send, fine_cells):
    peers, _, samples, _, own, wide = received.shape
    c4 = peers * own
    c3 = box.shape[-1] // 9
    part = jax.ShapeDtypeStruct((9, c4 // 32 + skip_keep.shape[1], 16, c3), BF16)
    whole = pl.BlockSpec(part.shape, lambda s: (0, 0, 0, 0))
    skips = pl.BlockSpec(skip_keep.shape, lambda s: (0, 0, 0, 0))
    return pl.pallas_call(
        functools.partial(up_kernel, scale=1.0 / math.sqrt(fine_cells)),
        grid=(samples,),
        in_specs=[
            pl.BlockSpec(memory_space=pltpu.SMEM),
            pl.BlockSpec((peers, 1, 1, 2, own, wide), lambda s: (0, 0, s, 0, 0, 0)),
            pl.BlockSpec((1, wide, 9 * c3), lambda s: (s, 0, 0)),
            pl.BlockSpec((1, wide, 3 * c3), lambda s: (s, 0, 0)),
            pl.BlockSpec((1, wide, 3 * c3), lambda s: (s, 0, 0)),
            skips, skips,
        ],
        out_specs=[whole, whole],
        out_shape=[part, part],
        scratch_shapes=[pltpu.VMEM((c4, 9 * c3), F32)],
        compiler_params=params(VMEM),
        cost_estimate=cost(1e9, 5e6),
        name="up_level",
    )(place, received, box, box_low, box_high, skip_keep, skip_send)


def fill_coarse_taps(odd, rows, taps):
    wide, c4 = rows[0].shape

    def fill(order):
        for v, row in zip(order, rows):
            before, after = shifted(row.astype(F32))
            lines = slice(v * wide, (v + 1) * wide)
            taps[lines, :c4] = before.astype(BF16)
            taps[lines, c4 : 2 * c4] = row
            taps[lines, 2 * c4 :] = after.astype(BF16)

    count = len(rows)
    pl.when(odd)(lambda: fill(range(count - 1, -1, -1)))
    pl.when(jnp.logical_not(odd))(lambda: fill(range(count)))


def dot32(left, right):
    return jnp.dot(left, right, preferred_element_type=F32)


def own_weight_kernel(place_ref, input_ref, far_ref, near_ref, out_ref, taps):
    wide = input_ref.shape[-1]
    c4 = far_ref.shape[-1]

    @pl.when(pl.program_id(0) == 0)
    def _():
        out_ref[...] = jnp.zeros_like(out_ref)

    fill_coarse_taps(place_ref[0] >= 2, (far_ref[0], near_ref[0]), taps)
    first, second = (input_ref[:, 0, 0, i].reshape(c4, wide) for i in range(2))
    out_ref[0] += dot32(second, taps[:wide, :])
    out_ref[1] += dot32(jnp.concatenate([first, second], axis=1), taps[...])
    out_ref[2] += dot32(first, taps[wide:, :])


def own_weight_level(place, received, far, near):
    peers, _, samples, _, own, wide = received.shape
    c4 = peers * own
    row = pl.BlockSpec((1, wide, c4), lambda s: (s, 0, 0))
    return pl.pallas_call(
        own_weight_kernel,
        grid=(samples,),
        in_specs=[
            pl.BlockSpec(memory_space=pltpu.SMEM),
            pl.BlockSpec((peers, 1, 1, 2, own, wide), lambda s: (0, 1, s, 0, 0, 0)),
            row, row,
        ],
        out_specs=pl.BlockSpec((3, c4, 3 * c4), lambda s: (0, 0, 0)),
        out_shape=jax.ShapeDtypeStruct((3, c4, 3 * c4), F32),
        scratch_shapes=[pltpu.VMEM((2 * wide, 3 * c4), BF16)],
        compiler_params=params(VMEM),
        cost_estimate=cost(LONG, 4e6),
        name="own_weight_level",
    )(place, received, far, near)


def coarse_weight_kernel(place_ref, input_ref, from_far_ref, from_near_ref, own_ref, out_ref, taps, total, *, scale):
    sample = pl.program_id(0)
    wide = input_ref.shape[-1]
    part = input_ref.shape[0] * input_ref.shape[-2]
    c4 = from_far_ref.shape[-1]

    fill_coarse_taps(place_ref[0] >= 2, (from_far_ref[0], from_near_ref[0]), taps)
    terms = [dot32(input_ref[:, 0, 0, i].reshape(part, wide), taps[i * wide : (i + 1) * wide, :]) for i in range(2)]

    @pl.when(sample == 0)
    def _():
        for i, term in enumerate(terms):
            total[i] = term

    @pl.when(sample > 0)
    def _():
        for i, term in enumerate(terms):
            total[i] += term

    @pl.when(sample == pl.num_programs(0) - 1)
    def _():
        count = part // 16
        for dy in range(3):
            for d in range(3):
                for side in range(c4 // 128):
                    at = d * c4 + side * 128
                    value = own_ref[dy, :, at : at + 128]
                    if dy != 1:
                        value = value + total[dy // 2, :, at : at + 128]
                    tap = ((2 - dy) * 3 + 2 - d) * (c4 // 128) + side
                    out_ref[tap * count : (tap + 1) * count] = tiles(value * scale)


def coarse_weight_level(place, received, from_far, from_near, own_terms, coarse_cells):
    peers, _, samples, _, own, wide = received.shape
    c4 = peers * own
    shape = (9 * (c4 // 128) * (c4 // 32), 16, 128)
    row = pl.BlockSpec((1, wide, c4), lambda s, place: (s, 0, 0))
    return pl.pallas_call(
        functools.partial(coarse_weight_kernel, scale=1.0 / math.sqrt(coarse_cells)),
        grid_spec=pltpu.PrefetchScalarGridSpec(
            num_scalar_prefetch=1,
            grid=(samples,),
            in_specs=[
                pl.BlockSpec((peers // 2, 1, 1, 2, own, wide), lambda s, place: (place[0] % 2, 1, s, 0, 0, 0)),
                row, row,
                pl.BlockSpec((3, c4 // 2, 3 * c4), lambda s, place: (0, place[0] % 2, 0)),
            ],
            out_specs=pl.BlockSpec(shape, lambda s, place: (0, 0, 0)),
            scratch_shapes=[pltpu.VMEM((2 * wide, 3 * c4), BF16), pltpu.VMEM((2, c4 // 2, 3 * c4), F32)],
        ),
        out_shape=jax.ShapeDtypeStruct(shape, BF16),
        compiler_params=params(VMEM),
        cost_estimate=cost(0.4e9, 2e6),
        name="coarse_weight_level",
    )(place, received, from_far, from_near, own_terms)


def coarse_specs(wide, c4, count):
    return [pl.BlockSpec((1, wide, c4), lambda s: (s, 0, 0))] * count


def coarse_input_kernel(chan_ref, weight_ref, first_ref, second_ref, third_ref, fourth_ref, *rest):
    *piece_refs, taps, stage = rest
    wide, c4 = first_ref.shape[1:]
    own = c4 // len(piece_refs)
    rows = (first_ref[0], second_ref[0], third_ref[0], fourth_ref[0])
    fill_coarse_taps(chan_ref[0] % 2 == 1, rows, taps)
    total = None
    for dy in range(3):
        for d in range(3):
            window = taps[dy * wide : (dy + 2) * wide, d * c4 : (d + 1) * c4]
            term = dott(weight_ref[2 - dy, 2 - d], window)
            total = term if total is None else total + term
    stage[...] = total.astype(BF16)
    for k, ref in enumerate(piece_refs):
        at = pl.multiple_of(jnp.bitwise_xor(chan_ref[0], k) * own, own)
        for i in range(2):
            ref[0, i] = stage[pl.ds(at, own), i * wide : (i + 1) * wide]


def coarse_input_level(chan, weight, rows, peers):
    samples, wide, c4 = rows[0].shape
    own = c4 // peers
    return pl.pallas_call(
        coarse_input_kernel,
        grid=(samples,),
        in_specs=[
            pl.BlockSpec(memory_space=pltpu.SMEM),
            pl.BlockSpec(weight.shape, lambda s: (0, 0, 0, 0)),
        ] + coarse_specs(wide, c4, 4),
        out_specs=[pl.BlockSpec((1, 2, own, wide), lambda s: (s, 0, 0, 0))] * peers,
        out_shape=[jax.ShapeDtypeStruct((samples, 2, own, wide), BF16)] * peers,
        scratch_shapes=[pltpu.VMEM((4 * wide, 3 * c4), BF16), pltpu.VMEM((c4, 2 * wide), BF16)],
        compiler_params=params(VMEM),
        cost_estimate=cost(1.3e9, 3e6),
        name="coarse_input_level",
    )(chan, weight, *rows)


def place_kernel(partners, chan_ref, *refs):
    out_ref = refs[-1]
    if len(refs) > len(partners) + 1:
        out_ref[...] = refs[len(partners)][...]
    for k, ref in zip(partners, refs):
        at = jnp.bitwise_xor(chan_ref[0], k) * 2
        out_ref[:, pl.ds(at, 2)] = ref[...]


def placed(chan, pieces, partners, peers, earlier=(), flops=1e6):
    samples, rows, own, wide = pieces[0].shape
    vmem = pl.BlockSpec(memory_space=pltpu.VMEM)
    return pl.pallas_call(
        functools.partial(place_kernel, partners),
        in_specs=[pl.BlockSpec(memory_space=pltpu.SMEM)] + [vmem] * (len(pieces) + len(earlier)),
        out_shape=jax.ShapeDtypeStruct((samples, rows * peers, own, wide), BF16),
        compiler_params=params(VMEM),
        cost_estimate=cost(flops, 1e6),
        name="place",
    )(chan, *pieces, *earlier)


def join_kernel(first, *refs):
    *part_refs, out_ref, stage, sems = refs
    one, more = part_refs[:2]
    count = one.shape[0]
    copies = []
    for at in range(0, stage.shape[0], 36):
        size = min(36, stage.shape[0] - at)
        held = max(min(size, count - at), 0)
        if held:
            lines = slice(at, at + held)
            stage[lines] = (one[lines].astype(F32) + more[lines].astype(F32)).astype(BF16)
        if held < size:
            stage[at + held : at + size] = jnp.zeros((size - held,) + stage.shape[1:], BF16)
        copies.append(
            pltpu.make_async_copy(
                stage.at[pl.ds(at, size)], out_ref.at[pl.ds(first + at, size)], sems.at[len(copies)]
            )
        )
        copies[-1].start()
    for copy in copies:
        copy.wait()


def joined(one, more, first, size, total, earlier=()):
    hbm = pl.BlockSpec(memory_space=pltpu.HBM)
    vmem = pl.BlockSpec(memory_space=pltpu.VMEM)
    return pl.pallas_call(
        functools.partial(join_kernel, first),
        in_specs=[vmem, vmem] + [hbm] * len(earlier),
        out_specs=hbm,
        out_shape=jax.ShapeDtypeStruct((total, 16, 128), BF16),
        input_output_aliases={2: 0} if earlier else {},
        scratch_shapes=[pltpu.VMEM((size, 16, 128), BF16), pltpu.SemaphoreType.DMA((-(-size // 36),))],
        compiler_params=params(VMEM),
        cost_estimate=cost(1e6, 2e6),
        name="join",
    )(one, more, *earlier)


def sum_kernel(parts_ref, out_ref):
    total = parts_ref[0].astype(F32)
    for k in range(1, parts_ref.shape[0]):
        total = total + parts_ref[k].astype(F32)
    total = total.astype(BF16)
    for k in range(out_ref.shape[0]):
        out_ref[k] = total


def unpack_kernel(place_ref, parts_ref, *rest):
    fine_ref, coarse_ref, fine_stage, coarse_stage, sems = rest[-5:]
    c4 = coarse_ref.shape[-1]
    sides = c4 // 128
    lines, skips = c4 // 2, (fine_ref.shape[-2] - c4) // 2
    line_tiles, skip_tiles = lines // 16, skips // 16
    core = place_ref[0] % 2
    rows = pl.ds(pl.multiple_of(core * lines, lines), lines)
    skip_rows = pl.ds(pl.multiple_of(c4 + core * skips, skips), skips)

    def take(at, count):
        return parts_ref[at : at + count].astype(F32).reshape(count * 16, 128)

    copies = []

    def send(source, target):
        copies.append(pltpu.make_async_copy(source, target, sems.at[len(copies)]))
        copies[-1].start()

    for tap in range(9):
        for side in range(sides):
            at = (tap * sides + side) * line_tiles
            coarse_stage[tap, :, side * 128 : (side + 1) * 128] = take(at, line_tiles)
        send(coarse_stage.at[tap], coarse_ref.at[tap, rows])
        at = 9 * sides * line_tiles + tap * (line_tiles + skip_tiles)
        fine_stage[tap, :lines] = take(at, line_tiles)
        fine_stage[tap, lines:] = take(at + line_tiles, skip_tiles)
        send(fine_stage.at[tap, pl.ds(0, lines)], fine_ref.at[tap, rows])
        send(fine_stage.at[tap, pl.ds(lines, skips)], fine_ref.at[tap, skip_rows])
    for copy in copies:
        copy.wait()


SWAP = ((0, 1), (1, 0))


def grad_sums(parts, chips):
    each = parts.shape[0] // chips
    parts = lax.all_to_all(parts.reshape(chips, each, 16, 128), CHIPS, 0, 0, tiled=True)
    summed = pl.pallas_call(
        sum_kernel,
        out_shape=jax.ShapeDtypeStruct((chips, each, 16, 128), BF16),
        compiler_params=params(VMEM),
        cost_estimate=cost(1e6, 1.3e6),
        name="sum_parts",
    )(parts)
    return lax.all_to_all(summed, CHIPS, 0, 0, tiled=True).reshape(chips * each, 16, 128)


def unpacked(place, half, fine_shape, coarse_shape, earlier=()):
    shapes = [jax.ShapeDtypeStruct((9,) + shape[2:], F32) for shape in (fine_shape, coarse_shape)]
    hbm = pl.BlockSpec(memory_space=pltpu.HBM)
    return pl.pallas_call(
        unpack_kernel,
        in_specs=[pl.BlockSpec(memory_space=pltpu.SMEM), pl.BlockSpec(memory_space=pltpu.VMEM)]
        + [hbm] * len(earlier),
        out_specs=[hbm, hbm],
        out_shape=shapes,
        input_output_aliases={2 + i: i for i in range(len(earlier))},
        scratch_shapes=[
            pltpu.VMEM((9, fine_shape[2] // 2, fine_shape[3]), F32),
            pltpu.VMEM((9, coarse_shape[2] // 2, coarse_shape[3]), F32),
            pltpu.SemaphoreType.DMA((27,)),
        ],
        compiler_params=params(VMEM),
        cost_estimate=cost(1, 1),
        name="unpack",
    )(place, half, *earlier)


def start_kernel(place_ref, cot_ref, pre_ref, near_ref, far_ref, rows, sems):
    samples = cot_ref.shape[0]
    odd = place_ref[0] >= 2
    last = cot_ref.shape[1] - 1
    ends = (jnp.where(odd, 0, last), jnp.where(odd, last, 0))
    copies = [
        [
            pltpu.make_async_copy(ref.at[s, line], rows.at[a, e, s], sems.at[a, e, s])
            for a, ref in enumerate((cot_ref, pre_ref))
        ]
        for e, line in enumerate(ends) for s in range(samples)
    ]
    for pair in copies:
        for copy in pair:
            copy.start()
    for k, pair in enumerate(copies):
        for copy in pair:
            copy.wait()
        e, s = divmod(k, samples)
        grad = rows[0, e, s].astype(F32) * silu_grad(rows[1, e, s].astype(F32))
        (near_ref, far_ref)[e][s] = grad.astype(BF16)


def start_level(place, cot, fine_pre):
    samples, _, wide, c3 = cot.shape
    hbm = pl.BlockSpec(memory_space=pltpu.HBM)
    vmem = pl.BlockSpec(memory_space=pltpu.VMEM)
    edge = jax.ShapeDtypeStruct((samples, wide, c3), BF16)
    return pl.pallas_call(
        start_kernel,
        in_specs=[pl.BlockSpec(memory_space=pltpu.SMEM), hbm, hbm],
        out_specs=[vmem, vmem],
        out_shape=[edge, edge],
        scratch_shapes=[
            pltpu.VMEM((2, 2, samples, wide, c3), BF16),
            pltpu.SemaphoreType.DMA((2, 2, samples)),
        ],
        compiler_params=params(VMEM),
        cost_estimate=cost(1e7, 2e6),
        name="start",
    )(place, in_hbm(cot), in_hbm(fine_pre))


def swapped(near, far):
    count = 1
    for axis in ALL:
        count *= lax.axis_size(axis)
    inside = [(i, i ^ 1) for i in range(count)]
    outside = [(i, i + 1) for i in range(1, count - 1, 2)]
    outside += [(target, source) for source, target in outside]
    return lax.ppermute(near, ALL, inside), lax.ppermute(far, ALL, outside)


def shards(coarse_input, coarse_pre, skip_feats, fine_pre, fine_cotangent, fine_weight, coarse_weight):
    peers = 1
    for axis in CHAN:
        peers *= lax.axis_size(axis)
    devices = peers
    for axis in ROWS:
        devices *= lax.axis_size(axis)
    samples, lines, wide, own = coarse_input.shape
    core = lax.axis_index("core").astype(jnp.int32)
    chan = lax.axis_index(CHAN).astype(jnp.int32).reshape(1)
    place = (core + 2 * (lax.axis_index("xl").astype(jnp.int32))).reshape(1)
    other_place = (1 - core + 2 * (lax.axis_index("xl").astype(jnp.int32))).reshape(1)

    edge_near, edge_far = start_level(place, fine_cotangent, fine_pre)
    pieces = jnp.stack([coarse_pre, coarse_input]).reshape(2, samples, peers, lines // peers, wide, own)
    pieces = pieces.transpose(2, 0, 1, 3, 5, 4)
    edge_near, edge_far = swapped(edge_near, edge_far)
    received = lax.all_to_all(pieces, CHAN, 0, 0, tiled=True)

    cs = skip_feats.shape[-1]
    fine_cells = fine_pre.shape[0] * fine_pre.shape[1] * fine_pre.shape[2] * devices
    fine_grad, box, edge, pooled, up_weight = box_level(fine_cotangent, fine_pre, fine_weight, cs)
    pooled, box_low, box_high = edge_level(place, edge_near, edge_far, edge, pooled, up_weight)
    grad_skip, skip_keep, skip_send = fine_level(
        place, fine_grad, edge_near, edge_far, skip_feats, fine_weight, fine_cells
    )
    received, skip_keep, skip_send = lax.optimization_barrier((received, skip_keep, skip_send))
    near, far = coarse_grad(place, pooled, received)
    from_near, from_far = swapped(near, far)
    fine_keep, fine_send = up_level(place, received, box, box_low, box_high, skip_keep, skip_send, fine_cells)
    fine_more = lax.ppermute(fine_send, "core", SWAP)
    own_terms = own_weight_level(place, received, far, near)
    chips = devices // lax.axis_size("core")
    fine_keep, fine_more = (a.reshape((-1, 16, 128)) for a in (fine_keep, fine_more))
    coarse_count = 9 * (fine_weight.shape[2] - cs) ** 2 // (2 * 16 * 128)
    total = -(-(coarse_count + fine_keep.shape[0]) // chips) * chips
    sums = joined(fine_keep, fine_more, coarse_count, total - coarse_count, total)
    from_near, from_far, sums, own_terms = lax.optimization_barrier((from_near, from_far, sums, own_terms))
    rows = (from_far, far, near, from_near)
    coarse_cells = samples * (lines // peers) * wide * devices
    coarse_send = coarse_weight_level(other_place, received, from_far, from_near, own_terms, coarse_cells)
    coarse_more = lax.ppermute(coarse_send, "core", SWAP)
    coarse_keep = coarse_weight_level(place, received, from_far, from_near, own_terms, coarse_cells)
    back = coarse_input_level(chan, coarse_weight, rows, peers)

    def home(k, piece):
        return lax.ppermute(piece, CHAN, [(i, i ^ k) for i in range(peers)])

    sums = joined(coarse_keep, coarse_more, 0, coarse_count, total, (sums,))
    mine = grad_sums(sums, chips)
    early = [k for k in range(peers) if k not in LATE]
    grad_input = placed(chan, [home(k, back[k]) if k else back[k] for k in early], early, peers, flops=LONG)
    grad_input, *late = lax.optimization_barrier((grad_input, *(back[k] for k in LATE)))
    late = [home(k, piece) for k, piece in zip(LATE, late)]
    mine, grad_input = lax.optimization_barrier((mine, grad_input))
    grad_input = placed(chan, late, LATE, peers, (grad_input,), flops=LONG)
    other = lax.ppermute(mine, "core", SWAP)
    sums = unpacked(place, mine, fine_weight.shape, coarse_weight.shape)
    grad_fine, grad_coarse = unpacked(other_place, other, fine_weight.shape, coarse_weight.shape, sums)
    return (
        grad_skip,
        grad_input.transpose(0, 1, 3, 2),
        grad_fine.reshape(fine_weight.shape),
        grad_coarse.reshape(coarse_weight.shape),
    )


def solution(mesh):
    split = Mesh(mesh.devices.reshape([size for _, size in SPLIT]), tuple(name for name, _ in SPLIT))
    coarse = P(None, ROWS, None, CHAN)
    fine = P(None, ALL, None, None)
    return jax.shard_map(
        shards,
        mesh=split,
        in_specs=(coarse, coarse, fine, fine, fine, P(), P()),
        out_specs=(fine, coarse, P(), P()),
        check_vma=False,
    )
```
